32 devices in a mesh: dp: 4 (over y, x), fsdp: 8 (over z, core).
Axes of the slice: x: 2, y: 2, z: 4, core: 2. Of those that a mesh axis runs over, the one named last changes fastest.
Arguments:
- layer_input: bfloat16 [32, 1024, 768], P(('dp', 'fsdp')), may hold values from -6 to 6
- lengths: int32 [32], P(('dp', 'fsdp')), may hold values from 64 to 1024, as said below
- ln1_gain: bfloat16 [768], P(('dp', 'fsdp')), may hold values from 0.099609375 to 1.8984375
- ln1_bias: bfloat16 [768], P(('dp', 'fsdp')), may hold values from -3 to 3
- w_qkv: bfloat16 [768, 2304], P(('dp', 'fsdp')), may hold values from -0.3125 to 0.3125
- b_qkv: bfloat16 [2304], P(('dp', 'fsdp')), may hold values from -3 to 3
- w_out: bfloat16 [768, 768], P(('dp', 'fsdp')), may hold values from -1.25 to 1.25
- b_out: bfloat16 [768], P(('dp', 'fsdp')), may hold values from -2 to 2
- ln2_gain: bfloat16 [768], P(('dp', 'fsdp')), may hold values from 0.099609375 to 1.8984375
- ln2_bias: bfloat16 [768], P(('dp', 'fsdp')), may hold values from -3 to 3
- w_up: bfloat16 [768, 3072], P(('dp', 'fsdp')), may hold values from -0.21875 to 0.21875
- b_up: bfloat16 [3072], P(('dp', 'fsdp')), may hold values from -3 to 3
- w_down: bfloat16 [3072, 768], P(('dp', 'fsdp')), may hold values from -0.109375 to 0.109375
- b_down: bfloat16 [768], P(('dp', 'fsdp')), may hold values from -2 to 2
- cotangent: bfloat16 [32, 1024, 768], P(('dp', 'fsdp')), may hold values from -6 to 6
Outputs:
- result: bfloat16 [32, 1024, 768], P(('dp', 'fsdp'))
- grad_input: float32 [32, 1024, 768], P(('dp', 'fsdp'))
- grad_ln1_gain: float32 [768], P(('dp', 'fsdp'))
- grad_ln1_bias: float32 [768], P(('dp', 'fsdp'))
- grad_w_qkv: float32 [768, 2304], P(('dp', 'fsdp'))
- grad_b_qkv: float32 [2304], P(('dp', 'fsdp'))
- grad_w_out: float32 [768, 768], P(('dp', 'fsdp'))
- grad_b_out: float32 [768], P(('dp', 'fsdp'))
- grad_ln2_gain: float32 [768], P(('dp', 'fsdp'))
- grad_ln2_bias: float32 [768], P(('dp', 'fsdp'))
- grad_w_up: float32 [768, 3072], P(('dp', 'fsdp'))
- grad_b_up: float32 [3072], P(('dp', 'fsdp'))
- grad_w_down: float32 [3072, 768], P(('dp', 'fsdp'))
- grad_b_down: float32 [768], P(('dp', 'fsdp'))
The draws below stay inside these ranges and needn't reach their ends.
Inputs may be any that keep to these rules, and one draw needn't show every extreme that they name: `lengths`: some slot has length exactly 1024.
All inputs are finite; a program needn't handle non-finite values.
Results may differ from the reference program's by a relative error of at most 0.012.
The reference program's roundings to bfloat16 on the way count: a program that leaves them out, or rounds other values in their place, can miss the bound.
Values may be sent and summed in bfloat16 or wider, within the bound.
No kernel may reach another device: no remote copies, remote signals or barrier semaphores. Data moves between devices by JAX's collectives and lax.ppermute only.
A program may use at most 192 MiB of HBM per device.

```python
import math
import jax
import jax.numpy as jnp
from jax import lax

D = 768
H = 12
HD = 64
FF = 3072
SLOT = 1024
MINLEN = 64
SLOTS = 32


def draw_lengths(key, part):
    key = jax.random.fold_in(key, 7)
    first_key, second_key = jax.random.split(key)
    steps_drawn = jax.random.randint(first_key, (SLOTS,), 0, 33)
    spans = MINLEN + (SLOT - MINLEN) * steps_drawn // 32
    longest = jax.random.randint(second_key, (), 0, SLOTS)
    return jnp.where(jnp.arange(SLOTS) == longest, SLOT, spans).astype(jnp.int32)


def raised(array, rng, source, target, blocks, factor):
    owner, partner = [(jnp.arange(array.shape[dim]) // (array.shape[dim] // blocks)).reshape([-1 if axis == dim else 1 for axis in range(array.ndim)]) for dim in (source, target)]
    chosen = jax.random.permutation(rng, blocks)[partner]
    strong = (owner == chosen) | (owner == (partner + blocks // 2) % blocks)
    return jnp.where(strong, factor * array, array)


def levels(key, shape, shards, smallest, top_value):
    level = 1.0
    for dim, parts in shards:
        heights = jax.random.uniform(jax.random.fold_in(jax.random.fold_in(key, 6), dim), (parts,), jnp.float32, smallest / len(shards), top_value / len(shards))
        level = level * jnp.repeat(jnp.exp(heights), shape[dim] // parts).reshape((-1,) + (1,) * (len(shape) - 1 - dim))
    return level


def noise(stream_key, shape, width, limit, cuts=(), held_as=jnp.bfloat16):
    loudness = levels(stream_key, shape, cuts, -0.22, 0.18) if cuts else 1.0
    array = jax.random.normal(stream_key, shape, jnp.float32) * width * loudness
    return jnp.minimum(jnp.maximum(array, -limit), limit).astype(held_as)


def bell_draw_with(own_key, dims, scale, bound, cuts, heavy, kind=jnp.bfloat16):
    values = scale * jax.random.normal(own_key, dims, jnp.float32)
    if cuts:
        values = values * levels(own_key, dims, cuts, -0.22, 0.18)
    return jnp.clip(raised(values, jax.random.fold_in(own_key, 3), *heavy), -bound, bound).astype(kind)


def setup_inputs(seed: int = 0) -> dict:
    streams_of = jax.random.split(jax.random.key(seed), 16)
    return {
        "layer_input": bell_draw_with(streams_of[0], (SLOTS, SLOT, D), 1.0, 6.0, ((0, 32),), (0, 2, 32, 2.75)),
        "lengths": draw_lengths(jax.random.fold_in(streams_of[15], 71), 0),
        "ln1_gain": jnp.clip(1.0 + 0.18 * jax.random.normal(streams_of[2], (D,), jnp.float32), 0.099609375, 1.8984375).astype(jnp.bfloat16),
        "ln1_bias": noise(streams_of[3], (D,), 0.5, 3.0, ((0, 32),)),
        "w_qkv": noise(streams_of[4], (D, 3 * D), (D // 2) ** -0.5, 0.3125, ((0, 32),)),
        "b_qkv": noise(streams_of[5], (3 * D,), 0.5, 3.0, ((0, 32),)),
        "w_out": noise(streams_of[6], (D, D), (D // 32) ** -0.5, 1.25, ((0, 32),)),
        "b_out": noise(streams_of[7], (D,), 0.3, 2.0, ((0, 32),)),
        "ln2_gain": jnp.clip(1.0 + 0.18 * jax.random.normal(streams_of[8], (D,), jnp.float32), 0.099609375, 1.8984375).astype(jnp.bfloat16),
        "ln2_bias": noise(streams_of[9], (D,), 0.5, 3.0, ((0, 32),)),
        "w_up": noise(streams_of[10], (D, FF), D ** -0.5, 0.21875, ((0, 32),)),
        "b_up": noise(streams_of[11], (FF,), 0.5, 3.0, ((0, 32),)),
        "w_down": noise(streams_of[12], (FF, D), FF ** -0.5, 0.109375, ((0, 32),)),
        "b_down": noise(streams_of[13], (D,), 0.3, 2.0, ((0, 32),)),
        "cotangent": noise(streams_of[14], (SLOTS, SLOT, D), 1.0, 6.0, ((0, 32),)),
    }


norm_eps = 1e-05
highest = lax.Precision.HIGHEST

@jax.custom_vjp
def low(v):
    return lax.optimization_barrier(v.astype(jnp.bfloat16)).astype(jnp.float32)

@jax.custom_vjp
def low_back(v):
    return v

def low_keep(v):
    return (low(v), None)

def low_pass(kept, grad):
    return (grad,)

def back_keep(v):
    return (v, None)

def back_low(kept, grad):
    return (low(grad),)
low.defvjp(low_keep, low_pass)
low_back.defvjp(back_keep, back_low)

def layer_norm(values, gain, bias):
    mean = lax.optimization_barrier(jnp.mean(values, axis=-1, keepdims=True))
    centred = values - mean
    spread = lax.optimization_barrier(jnp.mean(centred * centred, axis=-1, keepdims=True))
    return centred * lax.rsqrt(spread + norm_eps) * gain + bias

def head_attention(queries, keys_in, values, allowed):
    scores = low_back(jnp.einsum('gqd,gkd->gqk', queries, keys_in, precision=highest) * HD ** (-0.5))
    magnitude = jnp.sqrt(scores * scores + 1.0)
    row_top = lax.optimization_barrier(jnp.max(jnp.where(allowed, magnitude, 0.0), axis=-1, keepdims=True))
    exp_terms = jnp.where(allowed, jnp.exp(magnitude - row_top), 0.0)
    row_total = lax.optimization_barrier(jnp.sum(exp_terms, axis=-1, keepdims=True))
    weighted = low(scores / magnitude * (exp_terms / row_total))
    return jnp.einsum('gqk,gkd->gqd', weighted, values, precision=highest)

def block(inputs, lens_in, params):
    ln1_gain, ln1_bias, w_qkv, b_qkv, w_out, b_out, ln2_gain, ln2_bias, w_up, b_up, w_down, b_down = params
    seq_count = inputs.shape[0]
    position = jnp.arange(SLOT, dtype=jnp.int32)
    live_rows = position[None, :] < lens_in[:, None]
    allowed = (position[None, :, None] >= position[None, None, :]) & live_rows[:, None, :]
    normed = low(layer_norm(inputs, ln1_gain, ln1_bias))
    projected = low(low_back(jnp.einsum('gsd,de->gse', normed, w_qkv, precision=highest) + b_qkv))
    pieces = projected.reshape(seq_count, SLOT, 3, H, HD).transpose(2, 3, 0, 1, 4)

    def one_head(head_in):
        return head_attention(head_in[0], head_in[1], head_in[2], allowed)
    head_out = lax.map(jax.checkpoint(one_head), (pieces[0], pieces[1], pieces[2]))
    mixed = low(low_back(head_out.transpose(1, 2, 0, 3).reshape(seq_count, SLOT, D)))
    attended = low_back(jnp.einsum('gsd,de->gse', mixed, w_out, precision=highest) + b_out)
    residual = inputs + attended
    second = low(layer_norm(residual, ln2_gain, ln2_bias))
    hidden = low_back(jnp.einsum('gsd,df->gsf', second, w_up, precision=highest) + b_up)
    activated = low(jax.nn.gelu(hidden, approximate=True))
    branch = low_back(jnp.einsum('gsf,fd->gsd', activated, w_down, precision=highest) + b_down)
    return jnp.where(live_rows[:, :, None], residual + branch, 0.0)

def reference(layer_input, lengths, ln1_gain, ln1_bias, w_qkv, b_qkv, w_out, b_out, ln2_gain, ln2_bias, w_up, b_up, w_down, b_down, cotangent):
    params = tuple((item.astype(jnp.float32) for item in (ln1_gain, ln1_bias, w_qkv, b_qkv, w_out, b_out, ln2_gain, ln2_bias, w_up, b_up, w_down, b_down)))
    group_size = math.gcd(SLOTS, max(1, 4096 // SLOT))
    run_block = jax.checkpoint(block)

    def layer_fn(inputs, *weights):
        grouped = inputs.reshape(SLOTS // group_size, group_size, SLOT, D)
        lens_grouped = lengths.reshape(SLOTS // group_size, group_size)

        def scan_step(state_in, block_in):
            return (state_in, run_block(block_in[0], block_in[1], weights))
        unused, outputs = lax.scan(scan_step, jnp.float32(0.0), (grouped, lens_grouped))
        return outputs.reshape(SLOTS, SLOT, D)
    layer_out, pullback = jax.vjp(layer_fn, layer_input.astype(jnp.float32), *params)
    gradients = pullback(cotangent.astype(jnp.float32))
    return (layer_out.astype(jnp.bfloat16), gradients[0], gradients[1], gradients[2], gradients[3], gradients[4], gradients[5], gradients[6], gradients[7], gradients[8], gradients[9], gradients[10], gradients[11], gradients[12])
```

```python
import functools
import math

import jax
import jax.numpy as jnp
from jax import lax
from jax.experimental import pallas as pl
from jax.experimental.pallas import tpu as pltpu
from jax.sharding import PartitionSpec as P

H = 12
HD = 64
AXES = ("dp", "fsdp")
NORM_EPS = 1e-05
LOG2E = math.log2(math.e)
NT = (((1,), (1,)), ((), ()))
NN = (((1,), (0,)), ((), ()))
TN = (((0,), (0,)), ((), ()))
bf16 = jnp.bfloat16
f32 = jnp.float32
MIB = 2**20


def dot(a, b, dims):
    return lax.dot_general(a, b, dims, preferred_element_type=f32)


def whole(shape):
    return pl.BlockSpec(shape, lambda *i: (0,) * len(shape), pipeline_mode=pl.Buffered(1))


def smem():
    return pl.BlockSpec(memory_space=pltpu.SMEM)


def params(mib):
    return pltpu.CompilerParams(vmem_limit_bytes=mib * MIB)


def sds(shape, dtype):
    return jax.ShapeDtypeStruct(shape, dtype)


def cost(flops, nbytes):
    return pl.CostEstimate(flops=int(flops), bytes_accessed=int(nbytes), transcendentals=0)


def norm_stats(values):
    mean = jnp.mean(values, axis=1, keepdims=True)
    centred = values - mean
    inverse = lax.rsqrt(jnp.mean(centred * centred, axis=1, keepdims=True) + NORM_EPS)
    return centred * inverse, inverse


def unpack_kernel(pack_ref, *rest, n, rows, layout):
    outs, scratch = rest[:-1], rest[-1]
    scratch[...] = pack_ref[...].astype(f32)
    for d in range(n):
        for out, (row, lane, size) in zip(outs, layout):
            out[:, d * size : (d + 1) * size] = scratch[
                d * rows + row : d * rows + row + 1, lane : lane + size
            ]


def unpack(pack, n, layout):
    total = pack.shape[0]
    return pl.pallas_call(
        functools.partial(unpack_kernel, n=n, rows=total // n, layout=layout),
        out_shape=[sds((1, n * size), f32) for _, _, size in layout],
        scratch_shapes=[pltpu.VMEM(pack.shape, f32)],
        compiler_params=params(16),
    )(pack)


def repack_kernel(*refs, n, layout):
    ins, out = refs[:-1], refs[-1]
    out[...] = jnp.zeros_like(out)
    for d in range(n):
        for ref, (row, lane, size) in zip(ins, layout):
            out[d, row : row + 1, lane : lane + size] = ref[:, d * size : (d + 1) * size]


def repack(vectors, n, layout):
    return pl.pallas_call(
        functools.partial(repack_kernel, n=n, layout=layout),
        out_shape=sds((n, 8, 128), f32),
        compiler_params=params(16),
    )(*vectors)


def qkv_kernel(x_ref, g_ref, b_ref, w_ref, bq_ref, a_ref, o_ref):
    normal, _ = norm_stats(x_ref[...].astype(f32))
    a = (normal * g_ref[...] + b_ref[...]).astype(bf16)
    a_ref[...] = a
    o_ref[...] = (dot(a, w_ref[...], NN) + bq_ref[...]).astype(bf16)


def qkv_call(x, gain, bias, w, bq, rb=256):
    s, d = x.shape
    e = bq.shape[1]
    return pl.pallas_call(
        qkv_kernel,
        grid=(s // rb,),
        in_specs=[
            pl.BlockSpec((rb, d), lambda i: (i, 0)),
            whole((1, d)),
            whole((1, d)),
            whole((d, e)),
            whole((1, e)),
        ],
        out_specs=[pl.BlockSpec((rb, d), lambda i: (i, 0)), pl.BlockSpec((rb, e), lambda i: (i, 0))],
        out_shape=[sds((s, d), bf16), sds((s, e), bf16)],
        compiler_params=params(40),
        cost_estimate=cost(2 * s * d * e, 2 * d * e + 2 * s * (2 * d + e)),
    )(x, gain, bias, w, bq)


def fwd_kernel(len_ref, q_ref, k_ref, v_ref, o_ref, rz_ref, *kept, qb, nq):
    p_refs, a_refs = kept[:nq], kept[nq:]
    n = len_ref[0]
    c = HD ** (-0.5) * LOG2E
    lane = lax.broadcasted_iota(jnp.int32, (1, 128), 1)
    for i in range(nq):
        rows = slice(i * qb, (i + 1) * qb)

        @pl.when(n > i * qb)
        def _():
            nk = (i + 1) * qb
            q = q_ref[rows, :]
            k = k_ref[:nk, :]
            v = v_ref[:nk, :]
            row = lax.broadcasted_iota(jnp.int32, (qb, qb), 0)
            col = lax.broadcasted_iota(jnp.int32, (qb, qb), 1)
            mask = (col <= row) & (col < n - i * qb)
            mixed = []
            inverse_total = []
            for h in range(2):
                mine = (lane < HD) if h == 0 else (lane >= HD)
                scores = dot(jnp.where(mine, q, jnp.zeros_like(q)), k, NT) * c
                square = scores * scores + LOG2E * LOG2E
                top = jnp.max(jnp.where(mask, square[:, i * qb :], 0.0), axis=1, keepdims=True)
                if i:
                    top = jnp.maximum(top, jnp.max(square[:, : i * qb], axis=1, keepdims=True))
                inv = lax.rsqrt(square)
                e = jnp.exp2(square * inv - jnp.sqrt(top))
                last = jnp.where(mask, e[:, i * qb :], 0.0)
                e = jnp.concatenate([e[:, : i * qb], last], axis=1) if i else last
                total = jnp.sum(e, axis=1, keepdims=True)
                p = (scores * inv * e).astype(bf16)
                inv = inv * LOG2E
                p_refs[i][h] = p
                a_refs[i][h] = ((1.0 - inv * inv * (1.0 - inv)) * e).astype(bf16)
                rz = 1.0 / total
                mixed.append(dot(p, v, NN) * rz)
                inverse_total.append(rz)
            o_ref[rows, :] = jnp.where(lane < HD, mixed[0], mixed[1]).astype(bf16)
            rz_ref[rows, :] = jnp.where(lane < HD, inverse_total[0], inverse_total[1])

        @pl.when(n <= i * qb)
        def _():
            o_ref[rows, :] = jnp.zeros((qb, 128), bf16)
            rz_ref[rows, :] = jnp.zeros((qb, 128), f32)


def attention_forward(lens, qkv, qb=256, first=0, groups=H // 2):
    s = qkv.shape[0]
    nq = s // qb
    hp = H // 2

    def columns(off):
        return pl.BlockSpec((s, 128), lambda g: (0, first + g + off))

    kept_shape = [sds((2 * groups, qb, (i + 1) * qb), bf16) for i in range(nq)]
    kept_spec = [pl.BlockSpec((2, qb, (i + 1) * qb), lambda g: (g, 0, 0)) for i in range(nq)]
    return pl.pallas_call(
        functools.partial(fwd_kernel, qb=qb, nq=nq),
        grid=(groups,),
        in_specs=[smem(), columns(0), columns(hp), columns(2 * hp)],
        out_specs=[pl.BlockSpec((s, 128), lambda g: (0, g))] * 2 + kept_spec * 2,
        out_shape=[sds((s, 128 * groups), bf16), sds((s, 128 * groups), f32)] + kept_shape * 2,
        compiler_params=params(48),
        cost_estimate=cost(groups * 6e9, groups * 6e6),
    )(lens, qkv, qkv, qkv)


def bwd_kernel(len_ref, q_ref, k_ref, v_ref, o_ref, rz_ref, d_ref, *rest, qb, nq):
    p_refs, a_refs = rest[:nq], rest[nq : 2 * nq]
    out, dk_ref, dv_ref = rest[2 * nq :]
    n = len_ref[0]
    scale = HD ** (-0.5)
    lane = lax.broadcasted_iota(jnp.int32, (1, 128), 1)
    dk_ref[...] = jnp.zeros_like(dk_ref)
    dv_ref[...] = jnp.zeros_like(dv_ref)
    for i in range(nq):
        rows = slice(i * qb, (i + 1) * qb)

        @pl.when(n > i * qb)
        def _():
            nk = (i + 1) * qb
            q = q_ref[rows, :]
            k = k_ref[:nk, :]
            v = v_ref[:nk, :]
            grad = d_ref[rows, :] * rz_ref[rows, :]
            low = grad.astype(bf16)
            along = grad * o_ref[rows, :].astype(f32)
            low_t = low.T
            q_t = q.T
            dq = []
            for h in range(2):
                mine = (lane < HD) if h == 0 else (lane >= HD)
                part = slice(h * HD, (h + 1) * HD)
                total = jnp.sum(jnp.where(mine, along, 0.0), axis=1, keepdims=True)
                dp = dot(jnp.where(mine, low, jnp.zeros_like(low)), v, NT)
                p = p_refs[i][h]
                ds = (a_refs[i][h].astype(f32) * dp - p.astype(f32) * total).astype(bf16)
                dq.append(dot(ds, k, NN))
                dv_ref[part, :nk] += dot(low_t[part, :], p, NN)
                dk_ref[part, :nk] += dot(q_t[part, :], ds, NN)
            out[0, rows, :] = (jnp.where(lane < HD, dq[0], dq[1]) * scale).astype(bf16)

        @pl.when(n <= i * qb)
        def _():
            out[0, rows, :] = jnp.zeros((qb, 128), bf16)

    out[1] = (dk_ref[...] * scale).T.astype(bf16)
    out[2] = dv_ref[...].T.astype(bf16)


def attention_backward(lens, qkv, o, rz, dol, kept, qb=256, first=0, groups=H // 2):
    s = qkv.shape[0]
    nq = s // qb
    hp = H // 2

    def columns(off):
        return pl.BlockSpec((s, 128), lambda g: (0, first + g + off))

    kept_spec = [pl.BlockSpec((2, qb, (i + 1) * qb), lambda g: (first + g, 0, 0)) for i in range(nq)]
    return pl.pallas_call(
        functools.partial(bwd_kernel, qb=qb, nq=nq),
        grid=(groups,),
        in_specs=[smem(), columns(0), columns(hp), columns(2 * hp)] + [columns(0)] * 3 + kept_spec * 2,
        out_specs=pl.BlockSpec((3, s, 128), lambda g: (0, 0, g)),
        out_shape=sds((3, s, 128 * groups), bf16),
        scratch_shapes=[pltpu.VMEM((128, s), f32)] * 2,
        compiler_params=params(48),
        cost_estimate=cost(groups * 4e9, groups * 6e6),
    )(lens, qkv, qkv, qkv, o, rz, dol, *kept)


def ffn_kernel(
    len_ref, x_ref, o_ref, ct_ref, wo_ref, *rest, rb, n, nu
):
    wu_refs, wd_refs = rest[:nu], rest[nu : 2 * nu]
    bo_ref, g2_ref, b2_ref, bu_ref, bd_ref = rest[2 * nu : 2 * nu + 5]
    (y_ref, g_ref, du_ref, c_ref, dyl_ref, drl_ref, dr_ref, dol_ref) = rest[2 * nu + 5 : 2 * nu + 13]
    sbd, sbu, sg2, sb2, sbo, wd = rest[2 * nu + 13 :]
    i = pl.program_id(0)
    d = x_ref.shape[1]
    each = d // n

    @pl.when(i == 0)
    def _():
        for s in (sbd, sbu, sg2, sb2, sbo):
            s[...] = jnp.zeros_like(s)
        for dev in range(n):
            for j in range(nu):
                at = (dev * nu + j) * each
                wd[at : at + each, :] = wd_refs[j][dev * each : (dev + 1) * each, :]

    live = (lax.broadcasted_iota(jnp.int32, (rb, 1), 0) + i * rb) < len_ref[0]
    r = x_ref[...].astype(f32) + dot(o_ref[...], wo_ref[...], NN) + bo_ref[...]
    n2, k2 = norm_stats(r)
    g2 = g2_ref[...]
    c = (n2 * g2 + b2_ref[...]).astype(bf16)
    c_ref[...] = c
    dyl = jnp.where(live, ct_ref[...], jnp.zeros((), bf16))
    dyl_ref[...] = dyl
    y = r + bd_ref[...]
    dc = jnp.zeros_like(r)
    k0 = math.sqrt(2 / math.pi)
    for j in range(nu):
        cols = slice(j * d, (j + 1) * d)
        wu = wu_refs[j][...]
        wdj = wd[cols, :]
        u = dot(c, wu, NN) + bu_ref[:, cols]
        t = dot(dyl, wdj, NT)
        u2 = u * u
        hp = 0.5 + 0.5 * jnp.tanh(u * (k0 + (k0 * 0.044715) * u2))
        g = (u * hp).astype(bf16)
        slope = hp + u * (2.0 * hp * (1.0 - hp)) * (k0 + (3 * k0 * 0.044715) * u2)
        du = (t * slope).astype(bf16)
        g_ref[:, cols] = g
        du_ref[:, cols] = du
        y = y + dot(g, wdj, NN)
        dc = dc + dot(du, wu, NT)
        sbu[:, cols] += jnp.sum(du.astype(f32), axis=0, keepdims=True)
    y_ref[...] = jnp.where(live, y, 0.0).astype(bf16)
    q2 = dc * g2
    inner = q2 - jnp.mean(q2, axis=1, keepdims=True) - n2 * jnp.mean(q2 * n2, axis=1, keepdims=True)
    dr = dyl.astype(f32) + k2 * inner
    dr_ref[...] = dr
    drl = dr.astype(bf16)
    drl_ref[...] = drl
    dol_ref[...] = dot(drl, wo_ref[...], NT)
    sbd[...] += jnp.sum(dyl.astype(f32), axis=0, keepdims=True)
    sg2[...] += jnp.sum(dc * n2, axis=0, keepdims=True)
    sb2[...] += jnp.sum(dc, axis=0, keepdims=True)
    sbo[...] += jnp.sum(drl.astype(f32), axis=0, keepdims=True)


def ffn_call(lens, x, o, ct, weights, bo, g2, b2, bu, bd, n, first, rb=256):
    s, d = x.shape
    ff = bu.shape[1]
    nu = ff // d

    def row(w):
        return pl.BlockSpec((rb, w), lambda i: (i, 0))

    def acc(w):
        return pl.BlockSpec((1, w), lambda i: (0, 0))

    def part(j):
        return pl.BlockSpec((d, d), lambda i: (0, first + j), pipeline_mode=pl.Buffered(1))

    return pl.pallas_call(
        functools.partial(ffn_kernel, rb=rb, n=n, nu=nu),
        grid=(s // rb,),
        in_specs=[smem(), row(d), row(d), row(d)]
        + [part(j) for j in range(1 + 2 * nu)]
        + [whole((1, d)), whole((1, d)), whole((1, d)), whole((1, ff)), whole((1, d))],
        out_specs=[row(d), row(ff), row(ff), row(d), row(d), row(d), row(d), row(d)]
        + [acc(d), acc(ff), acc(d), acc(d), acc(d)],
        out_shape=[
            sds((s, d), bf16),
            sds((s, ff), bf16),
            sds((s, ff), bf16),
            sds((s, d), bf16),
            sds((s, d), bf16),
            sds((s, d), bf16),
            sds((s, d), f32),
            sds((s, d), f32),
            sds((1, d), f32),
            sds((1, ff), f32),
            sds((1, d), f32),
            sds((1, d), f32),
            sds((1, d), f32),
        ],
        scratch_shapes=[pltpu.VMEM((ff, d), bf16)],
        compiler_params=params(56),
        cost_estimate=cost(8 * s * d * ff + 4 * s * d * d, 4 * d * ff + 4 * s * ff + 20 * s * d),
    )(lens, x, o, ct, *([weights] * (1 + 2 * nu)), bo, g2, b2, bu, bd)


def wgrad_kernel(a_ref, b_ref, o_ref):
    b = b_ref[0] if len(b_ref.shape) == 3 else b_ref[...]
    o_ref[...] = dot(a_ref[...], b, TN).astype(o_ref.dtype)


def wgrad(a, b, ta, tb):
    s, m = a.shape
    if b.ndim == 3:
        n = b.shape[0] * b.shape[2]
        b_spec = pl.BlockSpec((1, s, b.shape[2]), lambda i, j: (j, 0, 0))
        tb = b.shape[2]
    else:
        n = b.shape[1]
        b_spec = pl.BlockSpec((s, tb), lambda i, j: (0, j))
    return pl.pallas_call(
        wgrad_kernel,
        grid=(m // ta, n // tb),
        in_specs=[pl.BlockSpec((s, ta), lambda i, j: (0, i)), b_spec],
        out_specs=pl.BlockSpec((ta, tb), lambda i, j: (i, j)),
        out_shape=sds((m, n), bf16),
        compiler_params=params(40),
        cost_estimate=cost(2 * s * m * n, 2 * (s * m + s * n + m * n)),
    )(a, b)


def first_kernel(x_ref, dr_ref, dq_ref, w_ref, g_ref, gi_ref, sg, sb, sq):
    i = pl.program_id(0)

    @pl.when(i == 0)
    def _():
        for s in (sg, sb, sq):
            s[...] = jnp.zeros_like(s)

    normal, inverse = norm_stats(x_ref[...].astype(f32))
    d = x_ref.shape[1]
    da = jnp.zeros(normal.shape, f32)
    for j in range(3):
        part = dq_ref[j]
        da = da + dot(part, w_ref[:, j * d : (j + 1) * d], NT)
        sq[:, j * d : (j + 1) * d] += jnp.sum(part.astype(f32), axis=0, keepdims=True)
    q1 = da * g_ref[...]
    inner = (
        q1 - jnp.mean(q1, axis=1, keepdims=True) - normal * jnp.mean(q1 * normal, axis=1, keepdims=True)
    )
    gi_ref[...] = dr_ref[...] + inverse * inner
    sg[...] += jnp.sum(da * normal, axis=0, keepdims=True)
    sb[...] += jnp.sum(da, axis=0, keepdims=True)


def first_backward(x, dr, dqkv, w, gain, rb=256):
    s, d = x.shape
    e = 3 * d

    def row(w):
        return pl.BlockSpec((rb, w), lambda i: (i, 0))

    def acc(w):
        return pl.BlockSpec((1, w), lambda i: (0, 0))

    return pl.pallas_call(
        first_kernel,
        grid=(s // rb,),
        in_specs=[row(d), row(d), pl.BlockSpec((3, rb, d), lambda i: (0, i, 0)), whole((d, e)), whole((1, d))],
        out_specs=[row(d), acc(d), acc(d), acc(e)],
        out_shape=[sds((s, d), f32), sds((1, d), f32), sds((1, d), f32), sds((1, e), f32)],
        compiler_params=params(40),
        cost_estimate=cost(2 * s * d * e, 2 * d * e + 16 * s * d),
    )(x, dr, dqkv, w, gain)


def scatter_sum(buf, n, order):
    lin = lax.axis_index(AXES)
    bits = n.bit_length() - 1
    rest = buf.shape[1:]
    buf = buf.reshape((2,) * bits + rest)
    left = list(range(bits - 1, -1, -1))
    for step, b in enumerate(order):
        axis = left.index(b)
        left.pop(axis)
        bit = (lin >> b) & 1
        send = lax.dynamic_index_in_dim(buf, 1 - bit, axis, keepdims=False)
        keep = lax.dynamic_index_in_dim(buf, bit, axis, keepdims=False)
        got = lax.ppermute(send, AXES, [(i, i ^ (1 << b)) for i in range(n)])
        buf = keep.astype(f32) + got.astype(f32)
        if step < bits - 1:
            buf = buf.astype(send.dtype)
    return buf


def body(
    n,
    dp,
    layer_input,
    lengths,
    ln1_gain,
    ln1_bias,
    w_qkv,
    b_qkv,
    w_out,
    b_out,
    ln2_gain,
    ln2_bias,
    w_up,
    b_up,
    w_down,
    b_down,
    cotangent,
):
    s, d = layer_input.shape[1:]
    x = layer_input.reshape(s, d)
    ct = cotangent.reshape(s, d)
    e, ff = w_qkv.shape[1], w_up.shape[1]
    each = d // n
    nu = ff // d
    vectors = (ln1_gain, ln1_bias, b_out, ln2_gain, ln2_bias, b_down, b_qkv, b_up)
    if each >= 4:
        layout = [(2, each * k, each) for k in range(5)] + [(3, 0, each), (0, 0, 3 * each), (1, 0, nu * each)]
    else:
        layout = [(0, each * k, each) for k in range(6)] + [(1, 0, 3 * each), (1, 64, nu * each)]
    rows = [
        [(lane, size, vec) for (row, lane, size), vec in zip(layout, vectors) if row == r] for r in range(each)
    ]
    packed = []
    for row in rows:
        pieces, at = [], 0
        for lane, size, vec in sorted(row, key=lambda t: t[0]):
            if lane > at:
                pieces.append(jnp.zeros((lane - at,), bf16))
            pieces.append(vec)
            at = lane + size
        pieces.append(jnp.zeros((128 - at,), bf16))
        packed.append(jnp.concatenate(pieces))
    pack = jnp.stack(packed)
    down = [w_down[j * each : (j + 1) * each] for j in range(nu)]
    block = jnp.concatenate([w_qkv, w_out, w_up, *down, pack], axis=1)
    gathered = lax.all_gather(block, AXES, axis=0, tiled=True)
    wide = e + d + 2 * ff
    g1, b1, bo, g2, b2, bd, bq, bu = unpack(gathered[:, wide:], n, layout)

    a, qkv = qkv_call(x, g1, b1, gathered, bq)
    o, rz, *kept = attention_forward(lengths, qkv)
    (y, g, du, c, dyl, drl, dr, dol, sbd, sbu, sg2, sb2, sbo) = ffn_call(
        lengths, x, o, ct, gathered, bo, g2, b2, bu, bd, n, e // d
    )
    order = list(range(n.bit_length() - 1))
    fs = (n // dp).bit_length() - 1
    order = [0] + order[fs:] + order[1:fs]
    dw_down = wgrad(g, dyl, 768, d)
    grad_down = scatter_sum(dw_down.reshape(n, ff // n, d), n, order)
    dw_up = wgrad(c, du, d, 768)
    grad_up = scatter_sum(dw_up.reshape(n, each, ff), n, order)
    dw_out = wgrad(o, drl, d, d)
    grad_out = scatter_sum(dw_out.reshape(n, each, d), n, order)
    dqkv = attention_backward(lengths, qkv, o, rz, dol, kept)
    dw_qkv = wgrad(a, dqkv, d, d)
    grad_qkv = scatter_sum(dw_qkv.reshape(n, each, e), n, order)
    grad_input, sg1, sb1, sbq = first_backward(x, dr, dqkv, gathered, g1)
    small = repack((sg1, sb1, sbo, sg2, sb2, sbd, sbq, sbu), n, layout)
    small = scatter_sum(small, n, order)
    gs1, gb1, gbo, gs2, gb2, gbd, gbq, gbu = [small[r, lane : lane + size] for r, lane, size in layout]
    return (
        y.reshape(layer_input.shape),
        grad_input.reshape(layer_input.shape),
        gs1,
        gb1,
        grad_qkv,
        gbq,
        grad_out,
        gbo,
        gs2,
        gb2,
        grad_up,
        gbu,
        grad_down,
        gbd,
    )


def solution(mesh):
    split = P(AXES)
    wide = P(AXES, None)
    cube = P(AXES, None, None)
    in_specs = (
        cube, split, split, split, wide, split, wide, split, split, split, wide, split, wide, split, cube,
    )
    out_specs = (
        cube, cube, split, split, wide, split, wide, split, split, split, wide, split, wide, split,
    )
    n = mesh.shape["dp"] * mesh.shape["fsdp"]
    return jax.shard_map(
        functools.partial(body, n, mesh.shape["dp"]),
        mesh=mesh,
        in_specs=in_specs,
        out_specs=out_specs,
        check_vma=False,
    )
```

```python
import functools
import itertools
import math

import jax
import jax.numpy as jnp
from jax import lax
from jax.experimental import pallas as pl
from jax.experimental.pallas import tpu as pltpu
from jax.sharding import PartitionSpec as P

H = 12
HD = 64
AXES = ("dp", "fsdp")
NORM_EPS = 1e-05
LOG2E = math.log2(math.e)
NT = (((1,), (1,)), ((), ()))
NN = (((1,), (0,)), ((), ()))
TN = (((0,), (0,)), ((), ()))
bf16 = jnp.bfloat16
f32 = jnp.float32
MIB = 2**20


def dot(a, b, dims):
    return lax.dot_general(a, b, dims, preferred_element_type=f32)


def whole(shape):
    return pl.BlockSpec(shape, lambda *i: (0,) * len(shape), pipeline_mode=pl.Buffered(1))


def smem():
    return pl.BlockSpec(memory_space=pltpu.SMEM)


def after(deps):
    return [pl.BlockSpec(memory_space=pl.ANY)] * len(deps)


def params(mib):
    return pltpu.CompilerParams(vmem_limit_bytes=mib * MIB)


def sds(shape, dtype):
    return jax.ShapeDtypeStruct(shape, dtype)


def cost(us):
    return pl.CostEstimate(flops=int(us * 1e9), bytes_accessed=0, transcendentals=0)


def norm_stats(values):
    mean = jnp.mean(values, axis=1, keepdims=True)
    centred = values - mean
    inverse = lax.rsqrt(jnp.mean(centred * centred, axis=1, keepdims=True) + NORM_EPS)
    return centred * inverse, inverse


def vector_layout(each, d, e, ff):
    return [(1, each * k, each) for k in range(6)] + [(0, 0, each * (e // d)), (0, 128, each * (ff // d))]


def prepare_kernel(idx_ref, *refs, layout, halves, nu):
    ins, (mine, theirs, mine_rest, theirs_rest) = refs[:12], refs[12:16]
    both, rest, low, down, sems = refs[16:21]
    small = refs[21:]
    wq, wo, wu, wd = ins[:4]
    each, e = wq.shape
    d = wo.shape[1]
    ff = wu.shape[1]
    targets = [both.at[:, :e], rest.at[:, :d], rest.at[:, d : d + ff], down]
    targets += list(small)
    copies = [pltpu.make_async_copy(ref, to, sems.at[k]) for k, (ref, to) in enumerate(zip(ins, targets))]
    for copy in copies:
        copy.start()
    low[...] = jnp.zeros_like(low)
    for copy in copies:
        copy.wait()
    for j in range(nu):
        rest[:, d + ff + j * d : d + ff + (j + 1) * d] = down[j * each : (j + 1) * each, :]
    for k, (row, lane, size) in enumerate(layout):
        low[row : row + 1, lane : lane + size] = small[k][...].astype(f32)
    both[:, e:] = low[...].astype(bf16)
    core = idx_ref[3]
    for ref, own, other, half in ((both, mine, theirs, halves[0]), (rest, mine_rest, theirs_rest, halves[1])):
        own[...] = ref[:, pl.ds(pl.multiple_of(core * half, 128), half)]
        other[...] = ref[:, pl.ds(pl.multiple_of((1 - core) * half, 128), half)]


def prepare(idx, wq, wo, wu, wd, vectors, layout):
    each, e = wq.shape
    d, ff = wo.shape[1], wu.shape[1]
    wide = d + 2 * ff
    halves = ((e + 256) // 2, wide // 2)
    return pl.pallas_call(
        functools.partial(prepare_kernel, layout=layout, halves=halves, nu=ff // d),
        in_specs=[smem()] + [pl.BlockSpec(memory_space=pltpu.HBM)] * 12,
        out_shape=[sds((each, h), bf16) for h in halves for _ in range(2)],
        scratch_shapes=[
            pltpu.VMEM((each, e + 256), bf16),
            pltpu.VMEM((each, wide), bf16),
            pltpu.VMEM((each, 256), f32),
            pltpu.VMEM(wd.shape, bf16),
            pltpu.SemaphoreType.DMA((12,)),
        ]
        + [pltpu.VMEM((1, v.shape[0]), bf16) for v in vectors],
        compiler_params=params(60),
    )(idx, wq, wo, wu, wd, *[v.reshape(1, -1) for v in vectors])


def gathered_chip(idx_ref, k, at):
    x, y, z = (idx_ref[i] for i in range(3))
    first, deep = at // 4, z ^ ((at // 2) % 2 + 2 * (at % 2))
    second = k % 2
    if (k // 2) % 2 == 0:
        return ((y ^ second) * 2 + (x ^ first)) * 4 + deep
    return ((y ^ first) * 2 + (x ^ second)) * 4 + deep


def qkv_kernel(idx_ref, x_ref, *rest, n, each, layout, pieces):
    parts, (a_ref, o_ref, w_ref), vecs, low = rest[:pieces], rest[pieces : pieces + 3], rest[pieces + 3 : -1], rest[-1]
    quarter = w_ref.shape[3]
    e = o_ref.shape[1]

    @pl.when(pl.program_id(0) == 0)
    def _():
        if pieces == 1:
            for k in range(4):
                w_ref[k] = parts[0][:, k * quarter : (k + 1) * quarter].reshape(w_ref.shape[1:])
        else:
            core = idx_ref[3]
            for k, part in enumerate(parts):
                quarter_at = 2 * (core if k < 4 else 1 - core) + (k // 2) % 2
                for at in range(8):
                    w_ref[quarter_at, gathered_chip(idx_ref, k, at)] = part[at]
        low[...] = w_ref[3, :, :, quarter - 256 :].astype(f32)
        for dev in range(n):
            for out, (row, lane, size) in zip(vecs, layout):
                at = dev * each + row
                out[:, dev * size : (dev + 1) * size] = low[at // 48, at % 48 : at % 48 + 1, lane : lane + size]

    normal, _ = norm_stats(x_ref[...].astype(f32))
    a = (normal * vecs[0][...] + vecs[1][...]).astype(bf16)
    a_ref[...] = a
    for k in range(4):
        cols = slice(k * quarter, min((k + 1) * quarter, e))
        wide = cols.stop - cols.start
        w = w_ref[k].reshape(a.shape[1], quarter)
        o_ref[:, cols] = (dot(a, w[:, :wide], NN) + vecs[6][:, cols]).astype(bf16)


def qkv_call(idx, x, parts, n, layout, e, rb=256):
    s, d = x.shape
    each = d // n
    quarter = (e + 256) // 4
    sizes = [n * size for _, _, size in layout]
    return pl.pallas_call(
        functools.partial(qkv_kernel, n=n, each=each, layout=layout, pieces=len(parts)),
        grid=(s // rb,),
        in_specs=[smem(), pl.BlockSpec((rb, d), lambda i: (i, 0))] + [whole(p.shape) for p in parts],
        out_specs=[
            pl.BlockSpec((rb, d), lambda i: (i, 0)),
            pl.BlockSpec((rb, e), lambda i: (i, 0)),
            whole((4, d // 48, 48, quarter)),
        ]
        + [whole((1, size)) for size in sizes],
        out_shape=[sds((s, d), bf16), sds((s, e), bf16), sds((4, d // 48, 48, quarter), bf16)]
        + [sds((1, size), f32) for size in sizes],
        scratch_shapes=[pltpu.VMEM((d // 48, 48, 256), f32)],
        compiler_params=params(60),
        cost_estimate=cost(9),
    )(idx, x, *parts)


def fwd_kernel(len_ref, q_ref, k_ref, v_ref, *refs, qb, nq):
    o_ref, rz_ref, *kept = refs[-2 - 2 * nq :]
    p_refs, a_refs = kept[:nq], kept[nq:]
    n = len_ref[0]
    c = HD ** (-0.5) * LOG2E
    lane = lax.broadcasted_iota(jnp.int32, (1, 128), 1)
    for i in range(nq):
        rows = slice(i * qb, (i + 1) * qb)

        @pl.when(n > i * qb)
        def _():
            nk = (i + 1) * qb
            q = q_ref[rows, :]
            k = k_ref[:nk, :]
            v = v_ref[:nk, :]
            row = lax.broadcasted_iota(jnp.int32, (qb, qb), 0)
            col = lax.broadcasted_iota(jnp.int32, (qb, qb), 1)
            mask = (col <= row) & (col < n - i * qb)
            mixed = []
            inverse_total = []
            for h in range(2):
                mine = (lane < HD) if h == 0 else (lane >= HD)
                scores = dot(jnp.where(mine, q, jnp.zeros_like(q)), k, NT) * c
                square = scores * scores + LOG2E * LOG2E
                top = jnp.max(jnp.where(mask, square[:, i * qb :], 0.0), axis=1, keepdims=True)
                if i:
                    top = jnp.maximum(top, jnp.max(square[:, : i * qb], axis=1, keepdims=True))
                inv = lax.rsqrt(square)
                e = jnp.exp2(square * inv - jnp.sqrt(top))
                last = jnp.where(mask, e[:, i * qb :], 0.0)
                e = jnp.concatenate([e[:, : i * qb], last], axis=1) if i else last
                total = jnp.sum(e, axis=1, keepdims=True)
                p = (scores * inv * e).astype(bf16)
                inv = inv * LOG2E
                p_refs[i][h] = p
                a_refs[i][h] = ((1.0 - inv * inv * (1.0 - inv)) * e).astype(bf16)
                rz = 1.0 / total
                mixed.append(dot(p, v, NN) * rz)
                inverse_total.append(rz)
            o_ref[rows, :] = jnp.where(lane < HD, mixed[0], mixed[1]).astype(bf16)
            rz_ref[rows, :] = jnp.where(lane < HD, inverse_total[0], inverse_total[1])

        @pl.when(n <= i * qb)
        def _():
            o_ref[rows, :] = jnp.zeros((qb, 128), bf16)
            rz_ref[rows, :] = jnp.zeros((qb, 128), f32)


def attention_forward(lens, qkv, first, groups, before=(), deps=(), qb=256):
    s = qkv.shape[0]
    nq = s // qb
    hp = H // 2

    def columns(off):
        return pl.BlockSpec((s, 128), lambda g: (0, first + g + off))

    kept_shape = [sds((H, qb, (i + 1) * qb), bf16) for i in range(nq)]
    kept_spec = [pl.BlockSpec((2, qb, (i + 1) * qb), lambda g: (first + g, 0, 0)) for i in range(nq)]
    return pl.pallas_call(
        functools.partial(fwd_kernel, qb=qb, nq=nq),
        grid=(groups,),
        in_specs=[smem(), columns(0), columns(hp), columns(2 * hp)] + after(before) + after(deps),
        out_specs=[columns(0)] * 2 + kept_spec * 2,
        out_shape=[sds((s, H * HD), bf16), sds((s, H * HD), f32)] + kept_shape * 2,
        input_output_aliases={4 + k: k for k in range(len(before))},
        compiler_params=params(60),
        cost_estimate=cost(7.5 * groups),
    )(lens, qkv, qkv, qkv, *before, *deps)


def bwd_kernel(len_ref, q_ref, k_ref, v_ref, o_ref, rz_ref, d_ref, *rest, qb, nq):
    p_refs, a_refs = rest[:nq], rest[nq : 2 * nq]
    out, dk_ref, dv_ref = rest[-3:]
    n = len_ref[0]
    scale = HD ** (-0.5)
    lane = lax.broadcasted_iota(jnp.int32, (1, 128), 1)
    dk_ref[...] = jnp.zeros_like(dk_ref)
    dv_ref[...] = jnp.zeros_like(dv_ref)
    for i in range(nq):
        rows = slice(i * qb, (i + 1) * qb)

        @pl.when(n > i * qb)
        def _():
            nk = (i + 1) * qb
            q = q_ref[rows, :]
            k = k_ref[:nk, :]
            v = v_ref[:nk, :]
            grad = d_ref[rows, :] * rz_ref[rows, :]
            low = grad.astype(bf16)
            along = grad * o_ref[rows, :].astype(f32)
            low_t = low.T
            q_t = q.T
            dq = []
            for h in range(2):
                mine = (lane < HD) if h == 0 else (lane >= HD)
                part = slice(h * HD, (h + 1) * HD)
                total = jnp.sum(jnp.where(mine, along, 0.0), axis=1, keepdims=True)
                dp = dot(jnp.where(mine, low, jnp.zeros_like(low)), v, NT)
                p = p_refs[i][h]
                ds = (a_refs[i][h].astype(f32) * dp - p.astype(f32) * total).astype(bf16)
                dq.append(dot(ds, k, NN))
                dv_ref[part, :nk] += dot(low_t[part, :], p, NN)
                dk_ref[part, :nk] += dot(q_t[part, :], ds, NN)
            out[0, rows, :] = (jnp.where(lane < HD, dq[0], dq[1]) * scale).astype(bf16)

        @pl.when(n <= i * qb)
        def _():
            out[0, rows, :] = jnp.zeros((qb, 128), bf16)

    out[1] = (dk_ref[...] * scale).T.astype(bf16)
    out[2] = dv_ref[...].T.astype(bf16)


def attention_backward(lens, qkv, o, rz, dol, kept, deps=(), qb=256, first=0, groups=H // 2):
    s = qkv.shape[0]
    nq = s // qb
    hp = H // 2

    def columns(off):
        return pl.BlockSpec((s, 128), lambda g: (0, first + g + off))

    kept_spec = [pl.BlockSpec((2, qb, (i + 1) * qb), lambda g: (first + g, 0, 0)) for i in range(nq)]
    return pl.pallas_call(
        functools.partial(bwd_kernel, qb=qb, nq=nq),
        grid=(groups,),
        in_specs=[smem(), columns(0), columns(hp), columns(2 * hp)] + [columns(0)] * 3 + kept_spec * 2 + after(deps),
        out_specs=pl.BlockSpec((3, s, 128), lambda g: (0, 0, g)),
        out_shape=sds((3, s, 128 * groups), bf16),
        scratch_shapes=[pltpu.VMEM((128, s), f32)] * 2,
        compiler_params=params(60),
        cost_estimate=cost(26),
    )(lens, qkv, qkv, qkv, o, rz, dol, *kept, *deps)


def ffn_kernel(len_ref, idx_ref, x_ref, o_ref, ct_ref, *rest, rb, n, nu, pieces, cut):
    parts, rest = rest[:pieces], rest[pieces:]
    bo_ref, g2_ref, b2_ref, bu_ref, bd_ref = rest[:5]
    (y_ref, g_ref, du_ref, c_ref, dyl_ref, drl_ref, dr_ref, dol_ref) = rest[5:13]
    sbd, sbu, sg2, sb2, sbo, w_ref, wd, sems = rest[13:]
    i = pl.program_id(0)
    d = x_ref.shape[1]
    each = d // n
    chips, rows, wide = w_ref.shape

    def weight(at):
        return w_ref[:, :, at : at + d].reshape(d, d)

    @pl.when(i == 0)
    def _():
        if pieces == 1:
            copies = [pltpu.make_async_copy(parts[0], w_ref, sems.at[0])]
        else:
            copies = []
            half = wide // 2
            core = idx_ref[3]
            for k, part in enumerate(parts):
                who, later = core if k < 4 else 1 - core, (k // 2) % 2
                lane = pl.multiple_of(who * half + later * cut, 128)
                for at in range(8):
                    to = w_ref.at[gathered_chip(idx_ref, k, at), :, pl.ds(lane, half - cut if later else cut)]
                    copies.append(pltpu.make_async_copy(part.at[at], to, sems.at[k * 8 + at]))
        for copy in copies:
            copy.start()
        for s in (sbd, sbu, sg2, sb2, sbo):
            s[...] = jnp.zeros_like(s)
        for copy in copies:
            copy.wait()
        for dev in range(n):
            for j in range(nu):
                at = (dev * nu + j) * each
                row = dev * each
                lane = (1 + nu + j) * d
                wd[at : at + each, :] = w_ref[row // rows, row % rows : row % rows + each, lane : lane + d]

    live = (lax.broadcasted_iota(jnp.int32, (rb, 1), 0) + i * rb) < len_ref[0]
    r = x_ref[...].astype(f32) + dot(o_ref[...], weight(0), NN) + bo_ref[...]
    n2, k2 = norm_stats(r)
    g2 = g2_ref[...]
    c = (n2 * g2 + b2_ref[...]).astype(bf16)
    c_ref[...] = c
    dyl = jnp.where(live, ct_ref[...], jnp.zeros((), bf16))
    dyl_ref[...] = dyl
    y = r + bd_ref[...]
    dc = jnp.zeros_like(r)
    k0 = math.sqrt(2 / math.pi)
    for j in range(nu):
        cols = slice(j * d, (j + 1) * d)
        wu = weight((1 + j) * d)
        wdj = wd[cols, :]
        u = dot(c, wu, NN) + bu_ref[:, cols]
        t = dot(dyl, wdj, NT)
        u2 = u * u
        hp = 0.5 + 0.5 * jnp.tanh(u * (k0 + (k0 * 0.044715) * u2))
        g = (u * hp).astype(bf16)
        slope = hp + u * (2.0 * hp * (1.0 - hp)) * (k0 + (3 * k0 * 0.044715) * u2)
        du = (t * slope).astype(bf16)
        g_ref[:, cols] = g
        du_ref[:, cols] = du
        y = y + dot(g, wdj, NN)
        dc = dc + dot(du, wu, NT)
        sbu[:, cols] += jnp.sum(du.astype(f32), axis=0, keepdims=True)
    y_ref[...] = jnp.where(live, y, 0.0).astype(bf16)
    q2 = dc * g2
    inner = q2 - jnp.mean(q2, axis=1, keepdims=True) - n2 * jnp.mean(q2 * n2, axis=1, keepdims=True)
    dr = dyl.astype(f32) + k2 * inner
    dr_ref[...] = dr
    drl = dr.astype(bf16)
    drl_ref[...] = drl
    dol_ref[...] = dot(drl, weight(0), NT)
    sbd[...] += jnp.sum(dyl.astype(f32), axis=0, keepdims=True)
    sg2[...] += jnp.sum(dc * n2, axis=0, keepdims=True)
    sb2[...] += jnp.sum(dc, axis=0, keepdims=True)
    sbo[...] += jnp.sum(drl.astype(f32), axis=0, keepdims=True)


def ffn_call(lens, idx, x, o, ct, parts, bo, g2, b2, bu, bd, n, cut, deps=(), rb=256):
    s, d = x.shape
    ff = bu.shape[1]
    nu = ff // d
    wide = d + 2 * ff

    def row(w):
        return pl.BlockSpec((rb, w), lambda i: (i, 0))

    def acc(w):
        return pl.BlockSpec((1, w), lambda i: (0, 0))

    return pl.pallas_call(
        functools.partial(ffn_kernel, rb=rb, n=n, nu=nu, pieces=len(parts), cut=cut),
        grid=(s // rb,),
        in_specs=[smem(), smem(), row(d), row(d), row(d)]
        + [pl.BlockSpec(memory_space=pltpu.HBM)] * len(parts)
        + [whole((1, d)), whole((1, d)), whole((1, d)), whole((1, ff)), whole((1, d))],
        out_specs=[row(d), row(ff), row(ff), row(d), row(d), row(d), row(d), row(d)]
        + [acc(d), acc(ff), acc(d), acc(d), acc(d)],
        out_shape=[
            sds((s, d), bf16),
            sds((s, ff), bf16),
            sds((s, ff), bf16),
            sds((s, d), bf16),
            sds((s, d), bf16),
            sds((s, d), bf16),
            sds((s, d), f32),
            sds((s, d), f32),
            sds((1, d), f32),
            sds((1, ff), f32),
            sds((1, d), f32),
            sds((1, d), f32),
            sds((1, d), f32),
        ],
        scratch_shapes=[
            pltpu.VMEM((d // 48, 48, wide), bf16),
            pltpu.VMEM((ff, d), bf16),
            pltpu.SemaphoreType.DMA((64,)),
        ],
        compiler_params=params(60),
        cost_estimate=cost(37),
    )(lens, idx, x, o, ct, *parts, bo, g2, b2, bu, bd)


def wgrad_kernel(a_ref, b_ref, o_ref):
    b = b_ref[0] if len(b_ref.shape) == 3 else b_ref[...]
    o_ref[...] = dot(a_ref[...], b, TN).astype(o_ref.dtype)


def wgrad(a, b, ta, tb):
    s, m = a.shape
    if b.ndim == 3:
        n = b.shape[0] * b.shape[2]
        b_spec = pl.BlockSpec((1, s, b.shape[2]), lambda i, j: (j, 0, 0))
        tb = b.shape[2]
    else:
        n = b.shape[1]
        b_spec = pl.BlockSpec((s, tb), lambda i, j: (0, j))
    return pl.pallas_call(
        wgrad_kernel,
        grid=(m // ta, n // tb),
        in_specs=[pl.BlockSpec((s, ta), lambda i, j: (0, i)), b_spec],
        out_specs=pl.BlockSpec((ta, tb), lambda i, j: (i, j)),
        out_shape=sds((m, n), bf16),
        compiler_params=params(40),
        cost_estimate=cost(9),
    )(a, b)


def by_core(idx_ref, grad, keep, send, each):
    pairs = grad.reshape(grad.shape[0] // (2 * each), 2, each, grad.shape[1])
    first = idx_ref[3] == 0
    keep[...] = jnp.where(first, pairs[:, 0], pairs[:, 1]).astype(bf16)
    send[...] = jnp.where(first, pairs[:, 1], pairs[:, 0]).astype(bf16)


def down_kernel(idx_ref, g_ref, b_ref, keep, send, *, each, nu):
    grad = dot(g_ref[...], b_ref[...], TN)
    d = grad.shape[1]
    chips = grad.shape[0] // (2 * each * nu)
    parts = grad.reshape(chips, 2, nu, each, d)
    first = idx_ref[3] == 0
    for j in range(nu):
        cols = slice(j * d, (j + 1) * d)
        keep[:, :, cols] = jnp.where(first, parts[:, 0, j], parts[:, 1, j]).astype(bf16)
        send[:, :, cols] = jnp.where(first, parts[:, 1, j], parts[:, 0, j]).astype(bf16)


def down_grad(idx, g, dyl, n, deps=()):
    s, ff = g.shape
    d = dyl.shape[1]
    each, nu = d // n, ff // d
    chips = n // 2 // nu
    spec = pl.BlockSpec((chips, each, ff), lambda i: (i, 0, 0))
    return pl.pallas_call(
        functools.partial(down_kernel, each=each, nu=nu),
        grid=(nu,),
        in_specs=[smem(), pl.BlockSpec((s, d), lambda i: (0, i)), whole((s, d))],
        out_specs=[spec, spec],
        out_shape=[sds((n // 2, each, ff), bf16)] * 2,
        compiler_params=params(60),
        cost_estimate=cost(9),
    )(idx, g, dyl)


def up_kernel(idx_ref, c_ref, du_ref, keep, send, *, each):
    by_core(idx_ref, dot(c_ref[...], du_ref[...], TN), keep, send, each)


def up_grad(idx, c, du, n):
    s, d = c.shape
    ff = du.shape[1]
    each = d // n
    spec = pl.BlockSpec((n // 2, each, d), lambda j: (0, 0, j))
    return pl.pallas_call(
        functools.partial(up_kernel, each=each),
        grid=(ff // d,),
        in_specs=[smem(), whole((s, d)), pl.BlockSpec((s, d), lambda j: (0, j))],
        out_specs=[spec, spec],
        out_shape=[sds((n // 2, each, ff), bf16)] * 2,
        compiler_params=params(60),
        cost_estimate=cost(9),
    )(idx, c, du)


def attention_grads_kernel(idx_ref, a_ref, dqkv_ref, o_ref, drl_ref, *rest, each):
    keep_a, send_a, keep_b, send_b = rest[-4:]
    j = pl.program_id(0)

    @pl.when(j < 2)
    def _():
        by_core(idx_ref, dot(a_ref[...], dqkv_ref[0], TN), keep_a, send_a, each)

    @pl.when(j == 2)
    def _():
        by_core(idx_ref, dot(a_ref[...], dqkv_ref[0], TN), keep_b, send_b, each)

    @pl.when(j == 3)
    def _():
        by_core(idx_ref, dot(o_ref[...], drl_ref[...], TN), keep_b, send_b, each)


def attention_grads(idx, a, dqkv, o, drl, n, deps=()):
    s, d = a.shape
    each = d // n
    spec_a = pl.BlockSpec((n // 2, each, d), lambda j: (0, 0, jnp.minimum(j, 1)))
    spec_b = pl.BlockSpec((n // 2, each, d), lambda j: (0, 0, jnp.maximum(j - 2, 0)))
    return pl.pallas_call(
        functools.partial(attention_grads_kernel, each=each),
        grid=(4,),
        in_specs=[
            smem(),
            whole((s, d)),
            pl.BlockSpec((1, s, d), lambda j: (jnp.minimum(j, 2), 0, 0)),
            whole((s, d)),
            whole((s, d)),
        ]
        + after(deps),
        out_specs=[spec_a, spec_a, spec_b, spec_b],
        out_shape=[sds((n // 2, each, 2 * d), bf16)] * 4,
        compiler_params=params(60),
        cost_estimate=cost(40),
    )(idx, a, dqkv, o, drl, *deps)


def first_kernel(x_ref, dr_ref, dq_ref, w_ref, g_ref, sbo, sg2, sb2, sbd, sbu, *rest):
    gi_ref, out = rest[-2:]
    i = pl.program_id(0)
    d = x_ref.shape[1]
    quarter = w_ref.shape[3]

    @pl.when(i == 0)
    def _():
        out[:, : 5 * d] = jnp.zeros((1, 5 * d), f32)
        for k, ref in enumerate((sbo, sg2, sb2, sbd)):
            out[:, (5 + k) * d : (6 + k) * d] = ref[...]
        out[:, 9 * d :] = sbu[...]

    normal, inverse = norm_stats(x_ref[...].astype(f32))
    da = jnp.zeros(normal.shape, f32)
    for k in range(4):
        w = w_ref[k].reshape(d, quarter)
        at = k * quarter
        while at < min((k + 1) * quarter, 3 * d):
            j = at // d
            end = min((k + 1) * quarter, (j + 1) * d)
            part = dq_ref[j, :, at - j * d : end - j * d]
            da = da + dot(part, w[:, at - k * quarter : end - k * quarter], NT)
            out[:, 2 * d + at : 2 * d + end] += jnp.sum(part.astype(f32), axis=0, keepdims=True)
            at = end
    q1 = da * g_ref[...]
    inner = (
        q1 - jnp.mean(q1, axis=1, keepdims=True) - normal * jnp.mean(q1 * normal, axis=1, keepdims=True)
    )
    gi_ref[...] = dr_ref[...] + inverse * inner
    out[:, :d] += jnp.sum(da * normal, axis=0, keepdims=True)
    out[:, d : 2 * d] += jnp.sum(da, axis=0, keepdims=True)


def first_backward(x, dr, dqkv, w, gain, sums, deps=(), rb=256):
    s, d = x.shape

    def row(w):
        return pl.BlockSpec((rb, w), lambda i: (i, 0))

    wide = 9 * d + sums[-1].shape[1]
    return pl.pallas_call(
        first_kernel,
        grid=(s // rb,),
        in_specs=[row(d), row(d), pl.BlockSpec((3, rb, d), lambda i: (0, i, 0)), whole(w.shape), whole((1, d))]
        + [whole(t.shape) for t in sums]
        + after(deps),
        out_specs=[row(d), pl.BlockSpec((1, wide), lambda i: (0, 0))],
        out_shape=[sds((s, d), f32), sds((1, wide), f32)],
        compiler_params=params(60),
        cost_estimate=cost(10),
    )(x, dr, dqkv, w, gain, *sums, *deps)


def scatter_sum(buf, n, order):
    lin = lax.axis_index(AXES)
    bits = n.bit_length() - 1
    rest = buf.shape[1:]
    buf = buf.reshape((2,) * bits + rest)
    left = list(range(bits - 1, -1, -1))
    for step, b in enumerate(order):
        axis = left.index(b)
        left.pop(axis)
        bit = (lin >> b) & 1
        send = lax.dynamic_index_in_dim(buf, 1 - bit, axis, keepdims=False)
        keep = lax.dynamic_index_in_dim(buf, bit, axis, keepdims=False)
        got = lax.ppermute(send, AXES, [(i, i ^ (1 << b)) for i in range(n)])
        buf = keep.astype(f32) + got.astype(f32)
        if step < bits - 1:
            buf = buf.astype(send.dtype)
    return buf


def permute(x, mask, n=32):
    return lax.ppermute(x, AXES, [(i, i ^ mask) for i in range(n)])


CORE, XBIT, YBIT = 1, 8, 16


def join(block, got):
    return jnp.concatenate([block[None], got[None]])


def gather_cores(mine, theirs, core):
    got = permute(theirs, CORE)
    return jnp.where(core == 0, jnp.concatenate([mine, got]), jnp.concatenate([got, mine]))


def gather_first(block, cut):
    a, b = block[..., :cut], block[..., cut:]
    return a, permute(a, XBIT), b, permute(b, YBIT)


def gather_second(a, b):
    parts = (a, permute(a, YBIT), b, permute(b, XBIT))
    return [t.reshape((8,) + t.shape[-2:]) for t in parts]


def tie(value, *others):
    return lax.optimization_barrier((value, *others))[0]


def fold_kernel(idx_ref, *refs, plan, joined):
    ins, outs = refs[: 2 * len(plan)], refs[-2 if joined else -2 * len(plan) :]
    lane = 0
    for k, (dim, which) in enumerate(plan):
        kept, got = ins[2 * k], ins[2 * k + 1]
        lead, wide = kept.shape[:-2], kept.shape[-1]
        for side in range(2):
            out = outs[side if joined else 2 * k + side]
            at = idx_ref[which] if side == 0 else 1 - idx_ref[which]
            for t in itertools.product(*[range(m) for m in lead[:dim] + lead[dim + 1 :]]):
                source = t[:dim] + (at,) + t[dim:]
                value = (kept[source].astype(f32) + got[source].astype(f32)).astype(bf16)
                if joined:
                    out[t + (slice(None), slice(lane, lane + wide))] = value
                else:
                    out[t] = value
        lane += wide


def fold(idx, pairs, plan, us, deps=(), joined=False):
    stepped = pairs[0][0].ndim > 3 and not joined
    args, in_specs, out_specs, out_shape, total = [], [], [], [], 0
    for (kept, got), (dim, _) in zip(pairs, plan):
        lead, (each, wide) = kept.shape[:-2], kept.shape[-2:]
        left = lead[:dim] + lead[dim + 1 :]
        total += wide
        args += [kept, got]

        def spec(shape):
            if not stepped:
                return pl.BlockSpec()
            m = len(shape)
            return pl.BlockSpec(shape[:-3] + (1,) + shape[-2:], lambda i: (0,) * (m - 3) + (i, 0, 0))

        in_specs += [spec(kept.shape)] * 2
        out_specs += [spec(left + (each, wide))] * 2
        out_shape += [sds(left + (each, wide), bf16)] * 2
    if joined:
        out_specs, out_shape = [pl.BlockSpec()] * 2, [sds(left + (each, total), bf16)] * 2
    grid = {"grid": (pairs[0][0].shape[-3],)} if stepped else {}
    return pl.pallas_call(
        functools.partial(fold_kernel, plan=plan, joined=joined),
        in_specs=[smem()] + in_specs + after(deps),
        out_specs=out_specs,
        out_shape=out_shape,
        compiler_params=params(24),
        cost_estimate=cost(us),
        **grid,
    )(idx, *args, *deps)


def last_kernel(kept, got, *refs, cuts):
    outs = refs[-len(cuts) :]
    total = kept[...].astype(f32) + got[...].astype(f32)
    each = total.shape[0]
    at = 0
    for out, (rows, wide) in zip(outs, cuts):
        for j in range(rows):
            out[j * each : (j + 1) * each, :] = total[:, at : at + wide]
            at += wide


def fold_last(kept, got, cuts, deps=()):
    each = kept.shape[0]
    return pl.pallas_call(
        functools.partial(last_kernel, cuts=cuts),
        in_specs=[pl.BlockSpec()] * 2 + after(deps),
        out_specs=[pl.BlockSpec()] * len(cuts),
        out_shape=[sds((rows * each, wide), f32) for rows, wide in cuts],
        compiler_params=params(24),
        cost_estimate=cost(1),
    )(kept, got, *deps)


def body(
    n,
    dp,
    layer_input,
    lengths,
    ln1_gain,
    ln1_bias,
    w_qkv,
    b_qkv,
    w_out,
    b_out,
    ln2_gain,
    ln2_bias,
    w_up,
    b_up,
    w_down,
    b_down,
    cotangent,
):
    s, d = layer_input.shape[1:]
    x = layer_input.reshape(s, d)
    ct = cotangent.reshape(s, d)
    e, ff = w_qkv.shape[1], w_up.shape[1]
    each = d // n
    nu = ff // d
    fast = n == 32 and dp == 4
    lin = lax.axis_index(AXES)
    idx = jnp.stack([(lin >> 3) & 1, (lin >> 4) & 1, (lin >> 1) & 3, lin & 1, (lin >> 1) & 1, (lin >> 2) & 1]).astype(jnp.int32)
    vectors = (ln1_gain, ln1_bias, b_out, ln2_gain, ln2_bias, b_down, b_qkv, b_up)
    layout = vector_layout(each, d, e, ff)
    mine, theirs, mine_rest, theirs_rest = prepare(idx, w_qkv, w_out, w_up, w_down, vectors, layout)
    cut_q, cut_r = (e + 256) // 4, 128 * (-(-(d + 2 * ff) // 512))
    if fast:
        core = lin & 1
        q = gather_cores(mine, theirs, core)
        r = gather_cores(mine_rest, theirs_rest, core)
        ra, rb = r[:, :cut_r], r[:, cut_r:]
        q = join(q, permute(q, 4))
        q, ra, rb = lax.optimization_barrier((q, ra, rb))
        q = join(q, permute(q, 2))
        q, ra = lax.optimization_barrier((q, ra))
        a0, a1, b0, b1 = gather_first(q, cut_q)
        ra = join(ra, permute(ra, 4))
        a1, b1, ra, rb = lax.optimization_barrier((a1, b1, ra, rb))
        qa, qb = join(a0, a1), join(b0, b1)
        parts = gather_second(qa, qb)
        rb = join(rb, permute(rb, 4))
        ra = join(ra, permute(ra, 2))
        parts = lax.optimization_barrier((*parts, ra, rb))
        ra, rb, parts = parts[4], parts[5], list(parts[:4])
        parts += [permute(t, CORE) for t in parts]
        got_rb = permute(rb, 2)
        got_ra = permute(ra, XBIT)
    else:
        def gathered(own, other):
            both = jnp.where((lin & 1) == 0, jnp.concatenate([own, other], 1), jnp.concatenate([other, own], 1))
            return lax.all_gather(both, AXES, axis=0, tiled=True)

        parts = [gathered(mine, theirs)]
        rest = [gathered(mine_rest, theirs_rest).reshape(d // 48, 48, d + 2 * ff)]
    a, qkv, wq, g1, b1, bo, g2, b2, bd, bq, bu = qkv_call(idx, x, parts, n, layout, e)
    if fast:
        rb = join(rb, tie(got_rb, qkv))
        got_rb = permute(rb, YBIT)
        done = attention_forward(lengths, qkv, 0, 2, deps=(rb,))
        ra, rb = join(ra, tie(got_ra, done[0])), join(rb, tie(got_rb, done[0]))
        ra, ga, rb, gb = gather_second(ra, rb)
        done = attention_forward(lengths, qkv, 2, 3, before=done, deps=(ra,))
        ga, gb = tie(ga, done[0]), tie(gb, done[0])
        rest = [ra, ga, rb, gb]
        rest += [permute(t, CORE) for t in rest]
        o, rz, *kept = attention_forward(lengths, qkv, 5, 1, before=done, deps=(ga, gb))
    else:
        o, rz, *kept = attention_forward(lengths, qkv, 0, H // 2)
    (y, g, du, c, dyl, drl, dr, dol, sbd, sbu, sg2, sb2, sbo) = ffn_call(
        lengths, idx, x, o, ct, rest, bo, g2, b2, bu, bd, n, cut_r
    )
    sums = (sbo, sg2, sb2, sbd, sbu)
    if fast:
        core_x, core_y, deep_0, deep_1 = 0, 1, 4, 5

        def chips(t):
            return t.reshape((2, 2, 4) + t.shape[1:])

        def deep(t):
            return t.reshape((2, 2) + t.shape[1:])

        keep_d, send_d = down_grad(idx, g, dyl, n)
        got_d = permute(send_d, CORE)
        keep_u, send_u = up_grad(idx, c, du, n)
        got_u = permute(send_u, CORE)
        kd, sd = fold(idx, [(chips(keep_d), chips(got_d))], [(1, core_x)], 2.5, deps=(keep_u,))
        rd = permute(sd, XBIT)
        ku, su = fold(idx, [(chips(keep_u), chips(got_u))], [(0, core_y)], 2.5, deps=(kd,))
        ru = permute(su, YBIT)
        dqkv = attention_backward(lengths, qkv, o, rz, dol, kept, deps=(ku,))
        kd, sd, ku, su = fold(idx, [(kd, rd), (ku, ru)], [(0, core_y), (0, core_x)], 2.5, deps=(dqkv,))
        rd, ru = permute(sd, YBIT), permute(su, XBIT)
        ka, sa, kb, sb = attention_grads(idx, a, dqkv, o, drl, n, deps=(kd,))
        ga, gb = permute(sa, CORE), permute(sb, CORE)
        pairs = [(deep(kd), deep(rd)), (deep(ku), deep(ru))]
        kw, sw = fold(idx, pairs, [(1, deep_0)] * 2, 30, deps=(ka,), joined=True)
        rw = permute(sw, 2)
        pairs = [(chips(ka), chips(ga)), (chips(kb), chips(gb))]
        ka, sa, kb, sb = fold(idx, pairs, [(1, core_x), (0, core_y)], 2.5, deps=(kw,))
        ra, rb = permute(sa, XBIT), permute(sb, YBIT)
        grad_input, total = first_backward(x, dr, dqkv, wq, g1, sums, deps=(ka,))
        kw, sw = fold(idx, [(kw, rw)], [(0, deep_1)], 1, deps=(total,))
        rw = permute(sw, 4)
        ka, sa, kb, sb = fold(idx, [(ka, ra), (kb, rb)], [(0, core_y), (0, core_x)], 1, deps=(kw,))
        ra, rb = permute(sa, YBIT), permute(sb, XBIT)
        for mask in (CORE, XBIT, YBIT, 2, 4):
            total = total + permute(total, mask)
        pairs = [(deep(ka), deep(ra)), (deep(kb), deep(rb))]
        kq, sq = fold(idx, pairs, [(1, deep_0)] * 2, 1, joined=True)
        rq = permute(sq, 2)
        grad_down, grad_up = fold_last(kw, rw, [(nu, d), (1, ff)], deps=(kq,))
        kq, sq = fold(idx, [(kq, rq)], [(0, deep_1)], 1, deps=(grad_up,))
        grad_qkv, grad_out = fold_last(kq, permute(sq, 4), [(1, e), (1, d)])
    else:
        order = list(range(n.bit_length() - 1))
        grad_down = scatter_sum(wgrad(g, dyl, d, d).reshape(n, ff // n, d), n, order)
        grad_up = scatter_sum(wgrad(c, du, d, d).reshape(n, each, ff), n, order)
        grad_out = scatter_sum(wgrad(o, drl, d, d).reshape(n, each, d), n, order)
        dqkv = attention_backward(lengths, qkv, o, rz, dol, kept)
        grad_qkv = scatter_sum(wgrad(a, dqkv, d, d).reshape(n, each, e), n, order)
        grad_input, total = first_backward(x, dr, dqkv, wq, g1, sums)
        total = lax.psum(total, AXES)
    shares, at = [], 0
    for size in (each, each, 3 * each, each, each, each, each, nu * each):
        shares.append(lax.dynamic_slice_in_dim(total[0], at + lin * size, size))
        at += n * size
    gs1, gb1, gbq, gbo, gs2, gb2, gbd, gbu = shares
    return (
        y.reshape(layer_input.shape),
        grad_input.reshape(layer_input.shape),
        gs1,
        gb1,
        grad_qkv,
        gbq,
        grad_out,
        gbo,
        gs2,
        gb2,
        grad_up,
        gbu,
        grad_down,
        gbd,
    )


def solution(mesh):
    split = P(AXES)
    wide = P(AXES, None)
    cube = P(AXES, None, None)
    in_specs = (
        cube, split, split, split, wide, split, wide, split, split, split, wide, split, wide, split, cube,
    )
    out_specs = (
        cube, cube, split, split, wide, split, wide, split, split, split, wide, split, wide, split,
    )
    n = mesh.shape["dp"] * mesh.shape["fsdp"]
    return jax.shard_map(
        functools.partial(body, n, mesh.shape["dp"]),
        mesh=mesh,
        in_specs=in_specs,
        out_specs=out_specs,
        check_vma=False,
    )
```

```python
import functools
import itertools
import math

import jax
import jax.numpy as jnp
from jax import lax
from jax.experimental import pallas as pl
from jax.experimental.pallas import tpu as pltpu
from jax.sharding import PartitionSpec as P

H = 12
HD = 64
AXES = ("dp", "fsdp")
NORM_EPS = 1e-05
LOG2E = math.log2(math.e)
NT = (((1,), (1,)), ((), ()))
NN = (((1,), (0,)), ((), ()))
TN = (((0,), (0,)), ((), ()))
bf16 = jnp.bfloat16
f32 = jnp.float32
MIB = 2**20


def dot(a, b, dims):
    return lax.dot_general(a, b, dims, preferred_element_type=f32)


def whole(shape):
    return pl.BlockSpec(shape, lambda *i: (0,) * len(shape), pipeline_mode=pl.Buffered(1))


def smem():
    return pl.BlockSpec(memory_space=pltpu.SMEM)


def tie(value, *others):
    return lax.optimization_barrier((value, *others))[0]


def params(mib):
    return pltpu.CompilerParams(vmem_limit_bytes=mib * MIB)


def sds(shape, dtype):
    return jax.ShapeDtypeStruct(shape, dtype)


def cost(us):
    return pl.CostEstimate(flops=int(us * 1e9), bytes_accessed=0, transcendentals=0)


def norm_stats(values):
    mean = jnp.mean(values, axis=1, keepdims=True)
    centred = values - mean
    inverse = lax.rsqrt(jnp.mean(centred * centred, axis=1, keepdims=True) + NORM_EPS)
    return centred * inverse, inverse


def vector_layout(each, d, e, ff):
    return [(1, each * k, each) for k in range(6)] + [(0, 0, each * (e // d)), (0, 128, each * (ff // d))]


def prepare_kernel(idx_ref, *refs, layout, halves, nu):
    ins, (mine, theirs, mine_rest, theirs_rest) = refs[:12], refs[12:16]
    both, rest, low, down, sems = refs[16:21]
    small = refs[21:]
    wq, wo, wu, wd = ins[:4]
    each, e = wq.shape
    d = wo.shape[1]
    ff = wu.shape[1]
    targets = [both.at[:, :e], rest.at[:, :d], rest.at[:, d : d + ff], down]
    targets += list(small)
    copies = [pltpu.make_async_copy(ref, to, sems.at[k]) for k, (ref, to) in enumerate(zip(ins, targets))]
    for copy in copies:
        copy.start()
    low[...] = jnp.zeros_like(low)
    for copy in copies:
        copy.wait()
    for j in range(nu):
        rest[:, d + ff + j * d : d + ff + (j + 1) * d] = down[j * each : (j + 1) * each, :]
    for k, (row, lane, size) in enumerate(layout):
        low[row : row + 1, lane : lane + size] = small[k][...].astype(f32)
    both[:, e:] = low[...].astype(bf16)
    core = idx_ref[3]
    for ref, own, other, half in ((both, mine, theirs, halves[0]), (rest, mine_rest, theirs_rest, halves[1])):
        own[...] = ref[:, pl.ds(pl.multiple_of(core * half, 128), half)]
        other[...] = ref[:, pl.ds(pl.multiple_of((1 - core) * half, 128), half)]


def prepare(idx, wq, wo, wu, wd, vectors, layout):
    each, e = wq.shape
    d, ff = wo.shape[1], wu.shape[1]
    wide = d + 2 * ff
    halves = ((e + 256) // 2, wide // 2)
    return pl.pallas_call(
        functools.partial(prepare_kernel, layout=layout, halves=halves, nu=ff // d),
        in_specs=[smem()] + [pl.BlockSpec(memory_space=pltpu.HBM)] * 12,
        out_shape=[sds((each, h), bf16) for h in halves for _ in range(2)],
        scratch_shapes=[
            pltpu.VMEM((each, e + 256), bf16),
            pltpu.VMEM((each, wide), bf16),
            pltpu.VMEM((each, 256), f32),
            pltpu.VMEM(wd.shape, bf16),
            pltpu.SemaphoreType.DMA((12,)),
        ]
        + [pltpu.VMEM((1, v.shape[0]), bf16) for v in vectors],
        compiler_params=params(60),
    )(idx, wq, wo, wu, wd, *[v.reshape(1, -1) for v in vectors])


def gathered_chip(idx_ref, k, at):
    x, y, z = (idx_ref[i] for i in range(3))
    first, deep = at // 4, z ^ ((at // 2) % 2 + 2 * (at % 2))
    second = k % 2
    if (k // 2) % 2 == 0:
        return ((y ^ second) * 2 + (x ^ first)) * 4 + deep
    return ((y ^ first) * 2 + (x ^ second)) * 4 + deep


def qkv_kernel(idx_ref, x_ref, *rest, n, each, layout, pieces):
    parts, (a_ref, o_ref, w_ref), vecs, low = rest[:pieces], rest[pieces : pieces + 3], rest[pieces + 3 : -1], rest[-1]
    quarter = w_ref.shape[3]
    e = o_ref.shape[1]

    @pl.when(pl.program_id(0) == 0)
    def _():
        if pieces == 1:
            for k in range(4):
                w_ref[k] = parts[0][:, k * quarter : (k + 1) * quarter].reshape(w_ref.shape[1:])
        else:
            core = idx_ref[3]
            for k, part in enumerate(parts):
                quarter_at = 2 * (core if k < 4 else 1 - core) + (k // 2) % 2
                for at in range(8):
                    w_ref[quarter_at, gathered_chip(idx_ref, k, at)] = part[at]
        low[...] = w_ref[3, :, :, quarter - 256 :].astype(f32)
        for dev in range(n):
            for out, (row, lane, size) in zip(vecs, layout):
                at = dev * each + row
                out[:, dev * size : (dev + 1) * size] = low[at // 48, at % 48 : at % 48 + 1, lane : lane + size]

    normal, _ = norm_stats(x_ref[...].astype(f32))
    a = (normal * vecs[0][...] + vecs[1][...]).astype(bf16)
    a_ref[...] = a
    for k in range(4):
        cols = slice(k * quarter, min((k + 1) * quarter, e))
        wide = cols.stop - cols.start
        w = w_ref[k].reshape(a.shape[1], quarter)
        o_ref[:, cols] = (dot(a, w[:, :wide], NN) + vecs[6][:, cols]).astype(bf16)


def qkv_call(idx, x, parts, n, layout, e, rb=256):
    s, d = x.shape
    each = d // n
    quarter = (e + 256) // 4
    sizes = [n * size for _, _, size in layout]
    return pl.pallas_call(
        functools.partial(qkv_kernel, n=n, each=each, layout=layout, pieces=len(parts)),
        grid=(s // rb,),
        in_specs=[smem(), pl.BlockSpec((rb, d), lambda i: (i, 0))] + [whole(p.shape) for p in parts],
        out_specs=[
            pl.BlockSpec((rb, d), lambda i: (i, 0)),
            pl.BlockSpec((rb, e), lambda i: (i, 0)),
            whole((4, d // 48, 48, quarter)),
        ]
        + [whole((1, size)) for size in sizes],
        out_shape=[sds((s, d), bf16), sds((s, e), bf16), sds((4, d // 48, 48, quarter), bf16)]
        + [sds((1, size), f32) for size in sizes],
        scratch_shapes=[pltpu.VMEM((d // 48, 48, 256), f32)],
        compiler_params=params(60),
        cost_estimate=cost(9),
    )(idx, x, *parts)


def fwd_kernel(len_ref, q_ref, k_ref, v_ref, *refs, qb, nq, rc):
    s_ref, z_ref, m_ref = refs[-3:]
    o_ref, rz_ref, *kept = refs[-5 - 2 * nq : -3]
    p_refs, a_refs = kept[:nq], kept[nq:]
    n = len_ref[0]
    lane = lax.broadcasted_iota(jnp.int32, (1, 128), 1)

    def emit(blocks):
        units = [(i, h) for i in blocks for h in range(2)]

        def scores(t):
            i, h = units[t]
            q = q_ref[i * qb : (i + 1) * qb, :] * jnp.asarray(HD**-0.5, bf16)
            mine = (lane < HD) if h == 0 else (lane >= HD)
            nk = (i + 1) * qb
            s_ref[t % 2, :, :nk] = dot(jnp.where(mine, q, jnp.zeros_like(q)), k_ref[:nk, :], NT)

        def weights(t):
            i, h = units[t]
            for r0 in range(0, qb, rc):
                rr = slice(r0, r0 + rc)
                row = lax.broadcasted_iota(jnp.int32, (rc, qb), 0) + r0
                col = lax.broadcasted_iota(jnp.int32, (rc, qb), 1)
                mask = (col <= row) & (col < n - i * qb)
                top = jnp.where(mask, jnp.abs(s_ref[t % 2, rr, i * qb : (i + 1) * qb]), 0.0)
                for j in range(i):
                    top = jnp.maximum(top, jnp.abs(s_ref[t % 2, rr, j * qb : (j + 1) * qb]))
                top = jnp.max(top, axis=1, keepdims=True)
                top = jnp.sqrt(top * top + 1.0)
                total = jnp.zeros((rc, qb), f32)
                for j in range(i + 1):
                    cols = slice(j * qb, (j + 1) * qb)
                    s = s_ref[t % 2, rr, cols]
                    square = s * s + 1.0
                    inv = lax.rsqrt(square)
                    e = jnp.exp(square * inv - top)
                    if j == i:
                        e = jnp.where(mask, e, 0.0)
                    total = total + e
                    p_refs[i][h, rr, cols] = (s * inv * e).astype(bf16)
                    a_refs[i][h, rr, cols] = ((1.0 - inv * inv * (1.0 - inv)) * e).astype(bf16)
                rz = 1.0 / jnp.sum(total, axis=1, keepdims=True)
                z_ref[t % 2, rr, :] = jnp.broadcast_to(rz, (rc, 128))

        def mix(t):
            i, h = units[t]
            rows = slice(i * qb, (i + 1) * qb)
            rz = z_ref[t % 2]
            mixed = dot(p_refs[i][h], v_ref[: (i + 1) * qb, :], NN) * rz
            if h == 0:
                m_ref[...] = mixed
                rz_ref[rows, :] = rz
            else:
                o_ref[rows, :] = jnp.where(lane < HD, m_ref[...], mixed).astype(bf16)
                rz_ref[rows, :] = jnp.where(lane < HD, rz_ref[rows, :], rz)

        scores(0)
        for t in range(len(units)):
            if t + 1 < len(units):
                scores(t + 1)
            weights(t)
            mix(t)

    by_blocks(n, qb, nq, emit, lambda rows: dead_block(rows, (o_ref, rz_ref)))


def dead_block(rows, refs):
    for ref in refs:
        ref[rows, :] = jnp.zeros((rows.stop - rows.start, ref.shape[1]), ref.dtype)


def by_blocks(n, qb, nq, emit, dead):
    @pl.when(n > (nq - 1) * qb)
    def _():
        emit(list(range(nq)))

    @pl.when(n <= (nq - 1) * qb)
    def _():
        for i in range(nq):

            @pl.when(n > i * qb)
            def _():
                emit([i])

            @pl.when(n <= i * qb)
            def _():
                dead(slice(i * qb, (i + 1) * qb))


def attention_forward(lens, qkv, first, groups, before=(), deps=(), qb=256):
    s = qkv.shape[0]
    nq = s // qb
    hp = H // 2

    def columns(off):
        return pl.BlockSpec((s, 128), lambda g: (0, first + g + off))

    kept_shape = [sds((H, qb, (i + 1) * qb), bf16) for i in range(nq)]
    kept_spec = [pl.BlockSpec((2, qb, (i + 1) * qb), lambda g: (first + g, 0, 0)) for i in range(nq)]
    return pl.pallas_call(
        functools.partial(fwd_kernel, qb=qb, nq=nq, rc=32),
        grid=(groups,),
        in_specs=[smem(), columns(0), columns(hp), columns(2 * hp)] + [pl.BlockSpec(memory_space=pl.ANY)] * len(before),
        out_specs=[columns(0)] * 2 + kept_spec * 2,
        out_shape=[sds((s, H * HD), bf16), sds((s, H * HD), f32)] + kept_shape * 2,
        input_output_aliases={4 + k: k for k in range(len(before))},
        scratch_shapes=[
            pltpu.VMEM((2, qb, s), f32),
            pltpu.VMEM((2, qb, 128), f32),
            pltpu.VMEM((qb, 128), f32),
        ],
        compiler_params=params(60),
        cost_estimate=cost(7.5 * groups),
    )(tie(lens, *deps), qkv, qkv, qkv, *before)


def bwd_kernel(len_ref, q_ref, k_ref, v_ref, o_ref, rz_ref, d_ref, *rest, qb, nq, rc):
    p_refs, a_refs = rest[:nq], rest[nq : 2 * nq]
    out, dk_ref, dv_ref, dp_ref, ds_ref, low_ref, total_ref, low_t, q_t, dq_ref = rest[-10:]
    n = len_ref[0]
    scale = HD ** (-0.5)
    lane = lax.broadcasted_iota(jnp.int32, (1, 128), 1)
    dk_ref[...] = jnp.zeros_like(dk_ref)
    dv_ref[...] = jnp.zeros_like(dv_ref)

    def emit(blocks):
        units = [(i, h) for i in blocks for h in range(2)]

        def weight_grads(t):
            i, h = units[t]
            nk = (i + 1) * qb
            mine = (lane < HD) if h == 0 else (lane >= HD)
            if h == 0:
                rows = slice(i * qb, (i + 1) * qb)
                grad = d_ref[rows, :] * rz_ref[rows, :]
                low = grad.astype(bf16)
                along = grad * o_ref[rows, :].astype(f32)
                low_ref[i % 2] = low
                low_t[i % 2] = low.T
                q_t[i % 2] = q_ref[rows, :].T
                for k in range(2):
                    half = jnp.where((lane < HD) if k == 0 else (lane >= HD), along, 0.0)
                    total_ref[i % 2, k] = jnp.broadcast_to(jnp.sum(half, axis=1, keepdims=True), (qb, 128))
            low = low_ref[i % 2]
            dp_ref[t % 2, :, :nk] = dot(jnp.where(mine, low, jnp.zeros_like(low)), v_ref[:nk, :], NT)

        def score_grads(t):
            i, h = units[t]
            for r0 in range(0, qb, rc):
                rr = slice(r0, r0 + rc)
                total = jnp.concatenate([total_ref[i % 2, h, rr, :]] * (qb // 128), axis=1)
                for j in range(i + 1):
                    cols = slice(j * qb, (j + 1) * qb)
                    first = a_refs[i][h, rr, cols].astype(f32) * dp_ref[t % 2, rr, cols]
                    ds_ref[t % 2, rr, cols] = (first - p_refs[i][h, rr, cols].astype(f32) * total).astype(bf16)

        def grads(t):
            i, h = units[t]
            nk = (i + 1) * qb
            part = slice(h * HD, (h + 1) * HD)
            ds = ds_ref[t % 2, :, :nk]
            dq = dot(ds, k_ref[:nk, :], NN)
            if h == 0:
                dq_ref[...] = dq
            else:
                out[0, i * qb : nk, :] = (jnp.where(lane < HD, dq_ref[...], dq) * scale).astype(bf16)
            dv_ref[part, :nk] += dot(low_t[i % 2, part, :], p_refs[i][h], NN)
            dk_ref[part, :nk] += dot(q_t[i % 2, part, :], ds, NN)

        weight_grads(0)
        for t in range(len(units)):
            if t + 1 < len(units):
                weight_grads(t + 1)
            score_grads(t)
            grads(t)

    by_blocks(n, qb, nq, emit, lambda rows: dead_block(rows, (out.at[0],)))
    out[1] = (dk_ref[...] * scale).T.astype(bf16)
    out[2] = dv_ref[...].T.astype(bf16)


def attention_backward(lens, qkv, o, rz, dol, kept, deps=(), qb=256, first=0, groups=H // 2):
    s = qkv.shape[0]
    nq = s // qb
    hp = H // 2

    def columns(off):
        return pl.BlockSpec((s, 128), lambda g: (0, first + g + off))

    kept_spec = [pl.BlockSpec((2, qb, (i + 1) * qb), lambda g: (first + g, 0, 0)) for i in range(nq)]
    return pl.pallas_call(
        functools.partial(bwd_kernel, qb=qb, nq=nq, rc=64),
        grid=(groups,),
        in_specs=[smem(), columns(0), columns(hp), columns(2 * hp)] + [columns(0)] * 3 + kept_spec * 2,
        out_specs=pl.BlockSpec((3, s, 128), lambda g: (0, 0, g)),
        out_shape=sds((3, s, 128 * groups), bf16),
        scratch_shapes=[pltpu.VMEM((128, s), f32)] * 2
        + [
            pltpu.VMEM((2, qb, s), f32),
            pltpu.VMEM((2, qb, s), bf16),
            pltpu.VMEM((2, qb, 128), bf16),
            pltpu.VMEM((2, 2, qb, 128), f32),
            pltpu.VMEM((2, 128, qb), bf16),
            pltpu.VMEM((2, 128, qb), bf16),
            pltpu.VMEM((qb, 128), f32),
        ],
        compiler_params=params(60),
        cost_estimate=cost(26),
    )(tie(lens, *deps), qkv, qkv, qkv, o, rz, dol, *kept)


def ffn_kernel(len_ref, idx_ref, x_ref, o_ref, ct_ref, *rest, rb, n, nu, pieces, cut):
    parts, rest = rest[:pieces], rest[pieces:]
    bo_ref, g2_ref, b2_ref, bu_ref, bd_ref = rest[:5]
    (y_ref, g_ref, du_ref, c_ref, dyl_ref, drl_ref, dr_ref, dol_ref) = rest[5:13]
    sbd, sbu, sg2, sb2, sbo, w_ref, wd, sems = rest[13:]
    i = pl.program_id(0)
    d = x_ref.shape[1]
    each = d // n
    chips, rows, wide = w_ref.shape

    def weight(at):
        return w_ref[:, :, at : at + d].reshape(d, d)

    @pl.when(i == 0)
    def _():
        if pieces == 1:
            copies = [pltpu.make_async_copy(parts[0], w_ref, sems.at[0])]
        else:
            copies = []
            half = wide // 2
            core = idx_ref[3]
            for k, part in enumerate(parts):
                who, later = core if k < 4 else 1 - core, (k // 2) % 2
                lane = pl.multiple_of(who * half + later * cut, 128)
                for at in range(8):
                    to = w_ref.at[gathered_chip(idx_ref, k, at), :, pl.ds(lane, half - cut if later else cut)]
                    copies.append(pltpu.make_async_copy(part.at[at], to, sems.at[k * 8 + at]))
        for copy in copies:
            copy.start()
        for s in (sbd, sbu, sg2, sb2, sbo):
            s[...] = jnp.zeros_like(s)
        for copy in copies:
            copy.wait()
        for dev in range(n):
            for j in range(nu):
                at = (dev * nu + j) * each
                row = dev * each
                lane = (1 + nu + j) * d
                wd[at : at + each, :] = w_ref[row // rows, row % rows : row % rows + each, lane : lane + d]

    live = (lax.broadcasted_iota(jnp.int32, (rb, 1), 0) + i * rb) < len_ref[0]
    r = x_ref[...].astype(f32) + dot(o_ref[...], weight(0), NN) + bo_ref[...]
    n2, k2 = norm_stats(r)
    g2 = g2_ref[...]
    c = (n2 * g2 + b2_ref[...]).astype(bf16)
    c_ref[...] = c
    dyl = jnp.where(live, ct_ref[...], jnp.zeros((), bf16))
    dyl_ref[...] = dyl
    y = r + bd_ref[...]
    dc = jnp.zeros_like(r)
    k0 = math.sqrt(2 / math.pi)
    for j in range(nu):
        cols = slice(j * d, (j + 1) * d)
        wu = weight((1 + j) * d)
        wdj = wd[cols, :]
        u = dot(c, wu, NN) + bu_ref[:, cols]
        t = dot(dyl, wdj, NT)
        u2 = u * u
        hp = 0.5 + 0.5 * jnp.tanh(u * (k0 + (k0 * 0.044715) * u2))
        g = (u * hp).astype(bf16)
        slope = hp + u * (2.0 * hp * (1.0 - hp)) * (k0 + (3 * k0 * 0.044715) * u2)
        du = (t * slope).astype(bf16)
        g_ref[:, cols] = g
        du_ref[:, cols] = du
        y = y + dot(g, wdj, NN)
        dc = dc + dot(du, wu, NT)
        sbu[:, cols] += jnp.sum(du.astype(f32), axis=0, keepdims=True)
    y_ref[...] = jnp.where(live, y, 0.0).astype(bf16)
    q2 = dc * g2
    inner = q2 - jnp.mean(q2, axis=1, keepdims=True) - n2 * jnp.mean(q2 * n2, axis=1, keepdims=True)
    dr = dyl.astype(f32) + k2 * inner
    dr_ref[...] = dr
    drl = dr.astype(bf16)
    drl_ref[...] = drl
    dol_ref[...] = dot(drl, weight(0), NT)
    sbd[...] += jnp.sum(dyl.astype(f32), axis=0, keepdims=True)
    sg2[...] += jnp.sum(dc * n2, axis=0, keepdims=True)
    sb2[...] += jnp.sum(dc, axis=0, keepdims=True)
    sbo[...] += jnp.sum(drl.astype(f32), axis=0, keepdims=True)


def ffn_call(lens, idx, x, o, ct, parts, bo, g2, b2, bu, bd, n, cut, rb=256):
    s, d = x.shape
    ff = bu.shape[1]
    nu = ff // d
    wide = d + 2 * ff

    def row(w):
        return pl.BlockSpec((rb, w), lambda i: (i, 0))

    def acc(w):
        return pl.BlockSpec((1, w), lambda i: (0, 0))

    return pl.pallas_call(
        functools.partial(ffn_kernel, rb=rb, n=n, nu=nu, pieces=len(parts), cut=cut),
        grid=(s // rb,),
        in_specs=[smem(), smem(), row(d), row(d), row(d)]
        + [pl.BlockSpec(memory_space=pltpu.HBM)] * len(parts)
        + [whole((1, d)), whole((1, d)), whole((1, d)), whole((1, ff)), whole((1, d))],
        out_specs=[row(d), row(ff), row(ff), row(d), row(d), row(d), row(d), row(d)]
        + [acc(d), acc(ff), acc(d), acc(d), acc(d)],
        out_shape=[
            sds((s, d), bf16),
            sds((s, ff), bf16),
            sds((s, ff), bf16),
            sds((s, d), bf16),
            sds((s, d), bf16),
            sds((s, d), bf16),
            sds((s, d), f32),
            sds((s, d), f32),
            sds((1, d), f32),
            sds((1, ff), f32),
            sds((1, d), f32),
            sds((1, d), f32),
            sds((1, d), f32),
        ],
        scratch_shapes=[
            pltpu.VMEM((d // 48, 48, wide), bf16),
            pltpu.VMEM((ff, d), bf16),
            pltpu.SemaphoreType.DMA((64,)),
        ],
        compiler_params=params(60),
        cost_estimate=cost(37),
    )(lens, idx, x, o, ct, *parts, bo, g2, b2, bu, bd)


def wgrad_kernel(a_ref, b_ref, o_ref):
    b = b_ref[0] if len(b_ref.shape) == 3 else b_ref[...]
    o_ref[...] = dot(a_ref[...], b, TN).astype(o_ref.dtype)


def wgrad(a, b, ta, tb):
    s, m = a.shape
    if b.ndim == 3:
        n = b.shape[0] * b.shape[2]
        b_spec = pl.BlockSpec((1, s, b.shape[2]), lambda i, j: (j, 0, 0))
        tb = b.shape[2]
    else:
        n = b.shape[1]
        b_spec = pl.BlockSpec((s, tb), lambda i, j: (0, j))
    return pl.pallas_call(
        wgrad_kernel,
        grid=(m // ta, n // tb),
        in_specs=[pl.BlockSpec((s, ta), lambda i, j: (0, i)), b_spec],
        out_specs=pl.BlockSpec((ta, tb), lambda i, j: (i, j)),
        out_shape=sds((m, n), bf16),
        compiler_params=params(40),
        cost_estimate=cost(9),
    )(a, b)


def by_core(idx_ref, grad, keep, send, each):
    pairs = grad.reshape(grad.shape[0] // (2 * each), 2, each, grad.shape[1])
    first = idx_ref[3] == 0
    keep[...] = jnp.where(first, pairs[:, 0], pairs[:, 1]).astype(bf16)
    send[...] = jnp.where(first, pairs[:, 1], pairs[:, 0]).astype(bf16)


def down_kernel(idx_ref, g_ref, b_ref, keep, send, *, each, nu):
    grad = dot(g_ref[...], b_ref[...], TN)
    d = grad.shape[1]
    chips = grad.shape[0] // (2 * each * nu)
    parts = grad.reshape(chips, 2, nu, each, d)
    first = idx_ref[3] == 0
    for j in range(nu):
        cols = slice(j * d, (j + 1) * d)
        keep[:, :, cols] = jnp.where(first, parts[:, 0, j], parts[:, 1, j]).astype(bf16)
        send[:, :, cols] = jnp.where(first, parts[:, 1, j], parts[:, 0, j]).astype(bf16)


def down_grad(idx, g, dyl, n):
    s, ff = g.shape
    d = dyl.shape[1]
    each, nu = d // n, ff // d
    chips = n // 2 // nu
    spec = pl.BlockSpec((chips, each, ff), lambda i: (i, 0, 0))
    return pl.pallas_call(
        functools.partial(down_kernel, each=each, nu=nu),
        grid=(nu,),
        in_specs=[smem(), pl.BlockSpec((s, d), lambda i: (0, i)), whole((s, d))],
        out_specs=[spec, spec],
        out_shape=[sds((n // 2, each, ff), bf16)] * 2,
        compiler_params=params(60),
        cost_estimate=cost(9),
    )(idx, g, dyl)


def up_kernel(idx_ref, c_ref, du_ref, keep, send, *, each):
    by_core(idx_ref, dot(c_ref[...], du_ref[...], TN), keep, send, each)


def up_grad(idx, c, du, n):
    s, d = c.shape
    ff = du.shape[1]
    each = d // n
    spec = pl.BlockSpec((n // 2, each, d), lambda j: (0, 0, j))
    return pl.pallas_call(
        functools.partial(up_kernel, each=each),
        grid=(ff // d,),
        in_specs=[smem(), whole((s, d)), pl.BlockSpec((s, d), lambda j: (0, j))],
        out_specs=[spec, spec],
        out_shape=[sds((n // 2, each, ff), bf16)] * 2,
        compiler_params=params(60),
        cost_estimate=cost(9),
    )(idx, c, du)


def attention_grads_kernel(idx_ref, a_ref, dqkv_ref, o_ref, drl_ref, *rest, each):
    keep_a, send_a, keep_b, send_b = rest[-4:]
    j = pl.program_id(0)

    @pl.when(j < 2)
    def _():
        by_core(idx_ref, dot(a_ref[...], dqkv_ref[0], TN), keep_a, send_a, each)

    @pl.when(j == 2)
    def _():
        by_core(idx_ref, dot(a_ref[...], dqkv_ref[0], TN), keep_b, send_b, each)

    @pl.when(j == 3)
    def _():
        by_core(idx_ref, dot(o_ref[...], drl_ref[...], TN), keep_b, send_b, each)


def attention_grads(idx, a, dqkv, o, drl, n, deps=()):
    s, d = a.shape
    each = d // n
    spec_a = pl.BlockSpec((n // 2, each, d), lambda j: (0, 0, jnp.minimum(j, 1)))
    spec_b = pl.BlockSpec((n // 2, each, d), lambda j: (0, 0, jnp.maximum(j - 2, 0)))
    return pl.pallas_call(
        functools.partial(attention_grads_kernel, each=each),
        grid=(4,),
        in_specs=[
            smem(),
            whole((s, d)),
            pl.BlockSpec((1, s, d), lambda j: (jnp.minimum(j, 2), 0, 0)),
            whole((s, d)),
            whole((s, d)),
        ]
       ,
        out_specs=[spec_a, spec_a, spec_b, spec_b],
        out_shape=[sds((n // 2, each, 2 * d), bf16)] * 4,
        compiler_params=params(60),
        cost_estimate=cost(40),
    )(tie(idx, *deps), a, dqkv, o, drl)


def first_kernel(x_ref, dr_ref, dq_ref, w_ref, g_ref, sbo, sg2, sb2, sbd, sbu, *rest):
    gi_ref, out = rest[-2:]
    i = pl.program_id(0)
    d = x_ref.shape[1]
    quarter = w_ref.shape[3]

    @pl.when(i == 0)
    def _():
        out[:, : 5 * d] = jnp.zeros((1, 5 * d), f32)
        for k, ref in enumerate((sbo, sg2, sb2, sbd)):
            out[:, (5 + k) * d : (6 + k) * d] = ref[...]
        out[:, 9 * d :] = sbu[...]

    normal, inverse = norm_stats(x_ref[...].astype(f32))
    da = jnp.zeros(normal.shape, f32)
    for k in range(4):
        w = w_ref[k].reshape(d, quarter)
        at = k * quarter
        while at < min((k + 1) * quarter, 3 * d):
            j = at // d
            end = min((k + 1) * quarter, (j + 1) * d)
            part = dq_ref[j, :, at - j * d : end - j * d]
            da = da + dot(part, w[:, at - k * quarter : end - k * quarter], NT)
            out[:, 2 * d + at : 2 * d + end] += jnp.sum(part.astype(f32), axis=0, keepdims=True)
            at = end
    q1 = da * g_ref[...]
    inner = (
        q1 - jnp.mean(q1, axis=1, keepdims=True) - normal * jnp.mean(q1 * normal, axis=1, keepdims=True)
    )
    gi_ref[...] = dr_ref[...] + inverse * inner
    out[:, :d] += jnp.sum(da * normal, axis=0, keepdims=True)
    out[:, d : 2 * d] += jnp.sum(da, axis=0, keepdims=True)


def first_backward(x, dr, dqkv, w, gain, sums, deps=(), rb=256):
    s, d = x.shape

    def row(w):
        return pl.BlockSpec((rb, w), lambda i: (i, 0))

    wide = 9 * d + sums[-1].shape[1]
    return pl.pallas_call(
        first_kernel,
        grid=(s // rb,),
        in_specs=[row(d), row(d), pl.BlockSpec((3, rb, d), lambda i: (0, i, 0)), whole(w.shape), whole((1, d))]
        + [whole(t.shape) for t in sums]
       ,
        out_specs=[row(d), pl.BlockSpec((1, wide), lambda i: (0, 0))],
        out_shape=[sds((s, d), f32), sds((1, wide), f32)],
        compiler_params=params(60),
        cost_estimate=cost(10),
    )(x, dr, dqkv, w, tie(gain, *deps), *sums)


def scatter_sum(buf, n, order):
    lin = lax.axis_index(AXES)
    bits = n.bit_length() - 1
    rest = buf.shape[1:]
    buf = buf.reshape((2,) * bits + rest)
    left = list(range(bits - 1, -1, -1))
    for step, b in enumerate(order):
        axis = left.index(b)
        left.pop(axis)
        bit = (lin >> b) & 1
        send = lax.dynamic_index_in_dim(buf, 1 - bit, axis, keepdims=False)
        keep = lax.dynamic_index_in_dim(buf, bit, axis, keepdims=False)
        got = lax.ppermute(send, AXES, [(i, i ^ (1 << b)) for i in range(n)])
        buf = keep.astype(f32) + got.astype(f32)
        if step < bits - 1:
            buf = buf.astype(send.dtype)
    return buf


def permute(x, mask, n=32):
    return lax.ppermute(x, AXES, [(i, i ^ mask) for i in range(n)])


CORE, XBIT, YBIT = 1, 8, 16


def join(block, got):
    return jnp.concatenate([block[None], got[None]])


def gather_cores(mine, theirs, core):
    got = permute(theirs, CORE)
    return jnp.where(core == 0, jnp.concatenate([mine, got]), jnp.concatenate([got, mine]))


def gather_first(block, cut):
    a, b = block[..., :cut], block[..., cut:]
    return a, permute(a, XBIT), b, permute(b, YBIT)


def gather_second(a, b):
    parts = (a, permute(a, YBIT), b, permute(b, XBIT))
    return [t.reshape((8,) + t.shape[-2:]) for t in parts]


def fold_kernel(idx_ref, *refs, plan, joined):
    ins, outs = refs[: 2 * len(plan)], refs[-2 if joined else -2 * len(plan) :]
    lane = 0
    for k, (dim, which) in enumerate(plan):
        kept, got = ins[2 * k], ins[2 * k + 1]
        lead, wide = kept.shape[:-2], kept.shape[-1]
        for side in range(2):
            out = outs[side if joined else 2 * k + side]
            at = idx_ref[which] if side == 0 else 1 - idx_ref[which]
            for t in itertools.product(*[range(m) for m in lead[:dim] + lead[dim + 1 :]]):
                source = t[:dim] + (at,) + t[dim:]
                value = (kept[source].astype(f32) + got[source].astype(f32)).astype(bf16)
                if joined:
                    out[t + (slice(None), slice(lane, lane + wide))] = value
                else:
                    out[t] = value
        lane += wide


def fold(idx, pairs, plan, us, deps=(), joined=False):
    stepped = pairs[0][0].ndim > 3 and not joined
    args, in_specs, out_specs, out_shape, total = [], [], [], [], 0
    for (kept, got), (dim, _) in zip(pairs, plan):
        lead, (each, wide) = kept.shape[:-2], kept.shape[-2:]
        left = lead[:dim] + lead[dim + 1 :]
        total += wide
        args += [kept, got]

        def spec(shape):
            if not stepped:
                return pl.BlockSpec()
            m = len(shape)
            return pl.BlockSpec(shape[:-3] + (1,) + shape[-2:], lambda i: (0,) * (m - 3) + (i, 0, 0))

        in_specs += [spec(kept.shape)] * 2
        out_specs += [spec(left + (each, wide))] * 2
        out_shape += [sds(left + (each, wide), bf16)] * 2
    if joined:
        out_specs, out_shape = [pl.BlockSpec()] * 2, [sds(left + (each, total), bf16)] * 2
    grid = {"grid": (pairs[0][0].shape[-3],)} if stepped else {}
    return pl.pallas_call(
        functools.partial(fold_kernel, plan=plan, joined=joined),
        in_specs=[smem()] + in_specs,
        out_specs=out_specs,
        out_shape=out_shape,
        compiler_params=params(24),
        cost_estimate=cost(us),
        **grid,
    )(tie(idx, *deps), *args)


def last_kernel(kept, got, *refs, cuts):
    outs = refs[-len(cuts) :]
    total = kept[...].astype(f32) + got[...].astype(f32)
    each = total.shape[0]
    at = 0
    for out, (rows, wide) in zip(outs, cuts):
        for j in range(rows):
            out[j * each : (j + 1) * each, :] = total[:, at : at + wide]
            at += wide


def fold_last(kept, got, cuts, deps=()):
    each = kept.shape[0]
    return pl.pallas_call(
        functools.partial(last_kernel, cuts=cuts),
        in_specs=[pl.BlockSpec()] * 2,
        out_specs=[pl.BlockSpec()] * len(cuts),
        out_shape=[sds((rows * each, wide), f32) for rows, wide in cuts],
        compiler_params=params(24),
        cost_estimate=cost(1),
    )(tie(kept, *deps), got)


def body(
    n,
    dp,
    layer_input,
    lengths,
    ln1_gain,
    ln1_bias,
    w_qkv,
    b_qkv,
    w_out,
    b_out,
    ln2_gain,
    ln2_bias,
    w_up,
    b_up,
    w_down,
    b_down,
    cotangent,
):
    s, d = layer_input.shape[1:]
    x = layer_input.reshape(s, d)
    ct = cotangent.reshape(s, d)
    e, ff = w_qkv.shape[1], w_up.shape[1]
    each = d // n
    nu = ff // d
    fast = n == 32 and dp == 4
    lin = lax.axis_index(AXES)
    idx = jnp.stack([(lin >> 3) & 1, (lin >> 4) & 1, (lin >> 1) & 3, lin & 1, (lin >> 1) & 1, (lin >> 2) & 1]).astype(jnp.int32)
    vectors = (ln1_gain, ln1_bias, b_out, ln2_gain, ln2_bias, b_down, b_qkv, b_up)
    layout = vector_layout(each, d, e, ff)
    mine, theirs, mine_rest, theirs_rest = prepare(idx, w_qkv, w_out, w_up, w_down, vectors, layout)
    cut_q, cut_r = (e + 256) // 4, 128 * (-(-(d + 2 * ff) // 512))
    if fast:
        core = lin & 1
        q = gather_cores(mine, theirs, core)
        r = gather_cores(mine_rest, theirs_rest, core)
        q = join(q, permute(q, 4))
        q = tie(q, r)
        q = join(q, permute(q, 2))
        r = tie(r, q)
        a0, a1, b0, b1 = gather_first(q, cut_q)
        got_r = permute(r, 4)
        qa, qb = join(a0, a1), join(b0, b1)
        parts = gather_second(qa, qb)
        r = join(r, tie(got_r, qa, qb))
        parts[1], parts[3] = tie(parts[1], r), tie(parts[3], r)
        parts += [permute(t, CORE) for t in parts]
        ra, rb = r[..., :cut_r], r[..., cut_r:]
        ra, rb = join(ra, permute(ra, 2)), join(rb, permute(rb, 2))
        got_ra, got_rb = permute(ra, XBIT), permute(rb, YBIT)
        x_in = tie(x, ra, rb)
    else:
        def gathered(own, other):
            both = jnp.where((lin & 1) == 0, jnp.concatenate([own, other], 1), jnp.concatenate([other, own], 1))
            return lax.all_gather(both, AXES, axis=0, tiled=True)

        x_in = x
        parts = [gathered(mine, theirs)]
        rest = [gathered(mine_rest, theirs_rest).reshape(d // 48, 48, d + 2 * ff)]
    a, qkv, wq, g1, b1, bo, g2, b2, bd, bq, bu = qkv_call(idx, x_in, parts, n, layout, e)
    if fast:
        ra, rb = join(ra, tie(got_ra, qkv)), join(rb, tie(got_rb, qkv))
        ra, ga, rb, gb = gather_second(ra, rb)
        o, rz, *kept = attention_forward(lengths, qkv, 0, H // 2, deps=(ra, rb))
        other_ra, other_rb = permute(ra, CORE), permute(rb, CORE)
        ga, gb = tie(ga, o, other_ra, other_rb), tie(gb, o, other_ra, other_rb)
        rest = [ra, ga, rb, gb, other_ra, permute(ga, CORE), other_rb, permute(gb, CORE)]
    else:
        o, rz, *kept = attention_forward(lengths, qkv, 0, H // 2)
    (y, g, du, c, dyl, drl, dr, dol, sbd, sbu, sg2, sb2, sbo) = ffn_call(
        lengths, idx, x, o, ct, rest, bo, g2, b2, bu, bd, n, cut_r
    )
    sums = (sbo, sg2, sb2, sbd, sbu)
    if fast:
        core_x, core_y, deep_0, deep_1 = 0, 1, 4, 5

        def chips(t):
            return t.reshape((2, 2, 4) + t.shape[1:])

        def deep(t):
            return t.reshape((2, 2) + t.shape[1:])

        keep_d, send_d = down_grad(idx, g, dyl, n)
        got_d = permute(send_d, CORE)
        keep_u, send_u = up_grad(idx, c, du, n)
        got_u = permute(send_u, CORE)
        kd, sd = fold(idx, [(chips(keep_d), chips(got_d))], [(1, core_x)], 2.5, deps=(keep_u,))
        rd = permute(sd, XBIT)
        ku, su = fold(idx, [(chips(keep_u), chips(got_u))], [(0, core_y)], 2.5, deps=(kd,))
        ru = permute(su, YBIT)
        dqkv = attention_backward(lengths, qkv, o, rz, dol, kept, deps=(ku,))
        kd, sd, ku, su = fold(idx, [(kd, rd), (ku, ru)], [(0, core_y), (0, core_x)], 2.5, deps=(dqkv,))
        rd, ru = permute(sd, YBIT), permute(su, XBIT)
        ka, sa, kb, sb = attention_grads(idx, a, dqkv, o, drl, n, deps=(kd,))
        ga, gb = permute(sa, CORE), permute(sb, CORE)
        pairs = [(deep(kd), deep(rd)), (deep(ku), deep(ru))]
        kw, sw = fold(idx, pairs, [(1, deep_0)] * 2, 30, deps=(ka,), joined=True)
        rw = permute(sw, 2)
        pairs = [(chips(ka), chips(ga)), (chips(kb), chips(gb))]
        ka, sa, kb, sb = fold(idx, pairs, [(1, core_x), (0, core_y)], 2.5, deps=(kw,))
        ra, rb = permute(sa, XBIT), permute(sb, YBIT)
        grad_input, total = first_backward(x, dr, dqkv, wq, g1, sums, deps=(ka,))
        got = permute(total, CORE)
        kw, sw = fold(idx, [(kw, rw)], [(0, deep_1)], 1, deps=(total,))
        rw = permute(sw, 4)
        ka, sa, kb, sb = fold(idx, [(ka, ra), (kb, rb)], [(0, core_y), (0, core_x)], 1, deps=(kw,))
        ra, rb = permute(sa, YBIT), permute(sb, XBIT)
        total = total + tie(got, ka)
        got = [permute(total, mask) for mask in (XBIT, YBIT, XBIT | YBIT)]
        grad_down, grad_up = fold_last(kw, rw, [(nu, d), (1, ff)], deps=(ra, rb))
        got = lax.optimization_barrier((*got, grad_up))
        total = total + got[0] + got[1] + got[2]
        pairs = [(deep(ka), deep(ra)), (deep(kb), deep(rb))]
        kq, sq = fold(idx, pairs, [(1, deep_0)] * 2, 1, deps=(grad_up, total), joined=True)
        rq = permute(sq, 2)
        got = [permute(total, mask) for mask in (2, 4, 6)]
        kq, sq = fold(idx, [(kq, rq)], [(0, deep_1)], 1)
        rq = permute(sq, 4)
        got = lax.optimization_barrier((*got, kq))
        total = total + got[0] + got[1] + got[2]
        grad_qkv, grad_out = fold_last(kq, rq, [(1, e), (1, d)])
    else:
        order = list(range(n.bit_length() - 1))
        grad_down = scatter_sum(wgrad(g, dyl, d, d).reshape(n, ff // n, d), n, order)
        grad_up = scatter_sum(wgrad(c, du, d, d).reshape(n, each, ff), n, order)
        grad_out = scatter_sum(wgrad(o, drl, d, d).reshape(n, each, d), n, order)
        dqkv = attention_backward(lengths, qkv, o, rz, dol, kept)
        grad_qkv = scatter_sum(wgrad(a, dqkv, d, d).reshape(n, each, e), n, order)
        grad_input, total = first_backward(x, dr, dqkv, wq, g1, sums)
        total = lax.psum(total, AXES)
    shares, at = [], 0
    for size in (each, each, 3 * each, each, each, each, each, nu * each):
        shares.append(lax.dynamic_slice_in_dim(total[0], at + lin * size, size))
        at += n * size
    gs1, gb1, gbq, gbo, gs2, gb2, gbd, gbu = shares
    return (
        y.reshape(layer_input.shape),
        grad_input.reshape(layer_input.shape),
        gs1,
        gb1,
        grad_qkv,
        gbq,
        grad_out,
        gbo,
        gs2,
        gb2,
        grad_up,
        gbu,
        grad_down,
        gbd,
    )


def solution(mesh):
    split = P(AXES)
    wide = P(AXES, None)
    cube = P(AXES, None, None)
    in_specs = (
        cube, split, split, split, wide, split, wide, split, split, split, wide, split, wide, split, cube,
    )
    out_specs = (
        cube, cube, split, split, wide, split, wide, split, split, split, wide, split, wide, split,
    )
    n = mesh.shape["dp"] * mesh.shape["fsdp"]
    return jax.shard_map(
        functools.partial(body, n, mesh.shape["dp"]),
        mesh=mesh,
        in_specs=in_specs,
        out_specs=out_specs,
        check_vma=False,
    )
```

```python
import functools
import itertools
import math

import jax
import jax.numpy as jnp
from jax import lax
from jax.experimental import pallas as pl
from jax.experimental.pallas import tpu as pltpu
from jax.sharding import PartitionSpec as P

H = 12
HD = 64
AXES = ("dp", "fsdp")
NORM_EPS = 1e-05
LOG2E = math.log2(math.e)
NT = (((1,), (1,)), ((), ()))
NN = (((1,), (0,)), ((), ()))
TN = (((0,), (0,)), ((), ()))
bf16 = jnp.bfloat16
f32 = jnp.float32
MIB = 2**20


def dot(a, b, dims):
    return lax.dot_general(a, b, dims, preferred_element_type=f32)


def whole(shape):
    return pl.BlockSpec(shape, lambda *i: (0,) * len(shape), pipeline_mode=pl.Buffered(1))


def smem():
    return pl.BlockSpec(memory_space=pltpu.SMEM)


def tie(value, *others):
    return lax.optimization_barrier((value, *others))[0]


def params(mib):
    return pltpu.CompilerParams(vmem_limit_bytes=mib * MIB)


def sds(shape, dtype):
    return jax.ShapeDtypeStruct(shape, dtype)


def cost(us):
    return pl.CostEstimate(flops=int(us * 1e9), bytes_accessed=0, transcendentals=0)


def norm_stats(values):
    mean = jnp.mean(values, axis=1, keepdims=True)
    centred = values - mean
    inverse = lax.rsqrt(jnp.mean(centred * centred, axis=1, keepdims=True) + NORM_EPS)
    return centred * inverse, inverse


def vector_layout(each, d, e, ff):
    return [(1, each * k, each) for k in range(6)] + [(0, 0, each * (e // d)), (0, 128, each * (ff // d))]


def prepare_kernel(idx_ref, *refs, layout, halves, nu):
    ins, (mine, theirs, mine_rest, theirs_rest) = refs[:12], refs[12:16]
    both, rest, low, down, sems = refs[16:21]
    small = refs[21:]
    wq, wo, wu, wd = ins[:4]
    each, e = wq.shape
    d = wo.shape[1]
    ff = wu.shape[1]
    targets = [both.at[:, :e], rest.at[:, :d], rest.at[:, d : d + ff], down]
    targets += list(small)
    copies = [pltpu.make_async_copy(ref, to, sems.at[k]) for k, (ref, to) in enumerate(zip(ins, targets))]
    for copy in copies:
        copy.start()
    low[...] = jnp.zeros_like(low)
    for copy in copies:
        copy.wait()
    for j in range(nu):
        rest[:, d + ff + j * d : d + ff + (j + 1) * d] = down[j * each : (j + 1) * each, :]
    for k, (row, lane, size) in enumerate(layout):
        low[row : row + 1, lane : lane + size] = small[k][...].astype(f32)
    both[:, e:] = low[...].astype(bf16)
    core = idx_ref[3]
    for ref, own, other, half in ((both, mine, theirs, halves[0]), (rest, mine_rest, theirs_rest, halves[1])):
        own[...] = ref[:, pl.ds(pl.multiple_of(core * half, 128), half)]
        other[...] = ref[:, pl.ds(pl.multiple_of((1 - core) * half, 128), half)]


def prepare(idx, wq, wo, wu, wd, vectors, layout):
    each, e = wq.shape
    d, ff = wo.shape[1], wu.shape[1]
    wide = d + 2 * ff
    halves = ((e + 256) // 2, wide // 2)
    return pl.pallas_call(
        functools.partial(prepare_kernel, layout=layout, halves=halves, nu=ff // d),
        in_specs=[smem()] + [pl.BlockSpec(memory_space=pltpu.HBM)] * 12,
        out_shape=[sds((each, h), bf16) for h in halves for _ in range(2)],
        scratch_shapes=[
            pltpu.VMEM((each, e + 256), bf16),
            pltpu.VMEM((each, wide), bf16),
            pltpu.VMEM((each, 256), f32),
            pltpu.VMEM(wd.shape, bf16),
            pltpu.SemaphoreType.DMA((12,)),
        ]
        + [pltpu.VMEM((1, v.shape[0]), bf16) for v in vectors],
        compiler_params=params(60),
    )(idx, wq, wo, wu, wd, *[v.reshape(1, -1) for v in vectors])


def gathered_chip(idx_ref, k, at):
    x, y, z = (idx_ref[i] for i in range(3))
    first, deep = at // 4, z ^ ((at // 2) % 2 + 2 * (at % 2))
    second = k % 2
    if (k // 2) % 2 == 0:
        return ((y ^ second) * 2 + (x ^ first)) * 4 + deep
    return ((y ^ first) * 2 + (x ^ second)) * 4 + deep


def qkv_kernel(idx_ref, x_ref, *rest, n, each, layout, pieces):
    parts, (a_ref, o_ref, w_ref), vecs, low = rest[:pieces], rest[pieces : pieces + 3], rest[pieces + 3 : -1], rest[-1]
    quarter = w_ref.shape[3]
    e = o_ref.shape[1]

    @pl.when(pl.program_id(0) == 0)
    def _():
        if pieces == 1:
            for k in range(4):
                w_ref[k] = parts[0][:, k * quarter : (k + 1) * quarter].reshape(w_ref.shape[1:])
        else:
            core = idx_ref[3]
            for k, part in enumerate(parts):
                quarter_at = 2 * (core if k < 4 else 1 - core) + (k // 2) % 2
                for at in range(8):
                    w_ref[quarter_at, gathered_chip(idx_ref, k, at)] = part[at]
        low[...] = w_ref[3, :, :, quarter - 256 :].astype(f32)
        for dev in range(n):
            for out, (row, lane, size) in zip(vecs, layout):
                at = dev * each + row
                out[:, dev * size : (dev + 1) * size] = low[at // 48, at % 48 : at % 48 + 1, lane : lane + size]

    normal, _ = norm_stats(x_ref[...].astype(f32))
    a = (normal * vecs[0][...] + vecs[1][...]).astype(bf16)
    a_ref[...] = a
    for k in range(4):
        cols = slice(k * quarter, min((k + 1) * quarter, e))
        wide = cols.stop - cols.start
        w = w_ref[k].reshape(a.shape[1], quarter)
        o_ref[:, cols] = (dot(a, w[:, :wide], NN) + vecs[6][:, cols]).astype(bf16)


def qkv_call(idx, x, parts, n, layout, e, rb=256):
    s, d = x.shape
    each = d // n
    quarter = (e + 256) // 4
    sizes = [n * size for _, _, size in layout]
    return pl.pallas_call(
        functools.partial(qkv_kernel, n=n, each=each, layout=layout, pieces=len(parts)),
        grid=(s // rb,),
        in_specs=[smem(), pl.BlockSpec((rb, d), lambda i: (i, 0))] + [whole(p.shape) for p in parts],
        out_specs=[
            pl.BlockSpec((rb, d), lambda i: (i, 0)),
            pl.BlockSpec((rb, e), lambda i: (i, 0)),
            whole((4, d // 48, 48, quarter)),
        ]
        + [whole((1, size)) for size in sizes],
        out_shape=[sds((s, d), bf16), sds((s, e), bf16), sds((4, d // 48, 48, quarter), bf16)]
        + [sds((1, size), f32) for size in sizes],
        scratch_shapes=[pltpu.VMEM((d // 48, 48, 256), f32)],
        compiler_params=params(60),
        cost_estimate=cost(9),
    )(idx, x, *parts)


def fwd_kernel(len_ref, q_ref, k_ref, v_ref, *refs, qb, nq, rc):
    s_ref, z_ref, m_ref = refs[-3:]
    o_ref, rz_ref, *kept = refs[-5 - 2 * nq : -3]
    p_refs, a_refs = kept[:nq], kept[nq:]
    n = len_ref[0]
    lane = lax.broadcasted_iota(jnp.int32, (1, 128), 1)

    def emit(blocks):
        units = [(i, h) for i in blocks for h in range(2)]

        def scores(t):
            i, h = units[t]
            q = q_ref[i * qb : (i + 1) * qb, :] * jnp.asarray(HD**-0.5, bf16)
            mine = (lane < HD) if h == 0 else (lane >= HD)
            nk = (i + 1) * qb
            s_ref[t % 2, :, :nk] = dot(jnp.where(mine, q, jnp.zeros_like(q)), k_ref[:nk, :], NT)

        def weights(t):
            i, h = units[t]
            for r0 in range(0, qb, rc):
                rr = slice(r0, r0 + rc)
                row = lax.broadcasted_iota(jnp.int32, (rc, qb), 0) + r0
                col = lax.broadcasted_iota(jnp.int32, (rc, qb), 1)
                mask = (col <= row) & (col < n - i * qb)
                top = jnp.where(mask, jnp.abs(s_ref[t % 2, rr, i * qb : (i + 1) * qb]), 0.0)
                for j in range(i):
                    top = jnp.maximum(top, jnp.abs(s_ref[t % 2, rr, j * qb : (j + 1) * qb]))
                top = jnp.max(top, axis=1, keepdims=True)
                top = jnp.sqrt(top * top + 1.0)
                total = jnp.zeros((rc, qb), f32)
                for j in range(i + 1):
                    cols = slice(j * qb, (j + 1) * qb)
                    s = s_ref[t % 2, rr, cols]
                    square = s * s + 1.0
                    inv = lax.rsqrt(square)
                    e = jnp.exp(square * inv - top)
                    if j == i:
                        e = jnp.where(mask, e, 0.0)
                    total = total + e
                    p_refs[i][h, rr, cols] = (s * inv * e).astype(bf16)
                    a_refs[i][h, rr, cols] = ((1.0 - inv * inv * (1.0 - inv)) * e).astype(bf16)
                rz = 1.0 / jnp.sum(total, axis=1, keepdims=True)
                z_ref[t % 2, rr, :] = jnp.broadcast_to(rz, (rc, 128))

        def mix(t):
            i, h = units[t]
            rows = slice(i * qb, (i + 1) * qb)
            rz = z_ref[t % 2]
            mixed = dot(p_refs[i][h], v_ref[: (i + 1) * qb, :], NN) * rz
            if h == 0:
                m_ref[...] = mixed
                rz_ref[rows, :] = rz
            else:
                o_ref[rows, :] = jnp.where(lane < HD, m_ref[...], mixed).astype(bf16)
                rz_ref[rows, :] = jnp.where(lane < HD, rz_ref[rows, :], rz)

        scores(0)
        for t in range(len(units)):
            if t + 1 < len(units):
                scores(t + 1)
            weights(t)
            mix(t)

    by_blocks(n, qb, nq, emit, lambda rows: dead_block(rows, (o_ref, rz_ref)))


def dead_block(rows, refs):
    for ref in refs:
        ref[rows, :] = jnp.zeros((rows.stop - rows.start, ref.shape[1]), ref.dtype)


def by_blocks(n, qb, nq, emit, dead):
    @pl.when(n > (nq - 1) * qb)
    def _():
        emit(list(range(nq)))

    @pl.when(n <= (nq - 1) * qb)
    def _():
        for i in range(nq):

            @pl.when(n > i * qb)
            def _():
                emit([i])

            @pl.when(n <= i * qb)
            def _():
                dead(slice(i * qb, (i + 1) * qb))


def attention_forward(lens, qkv, first, groups, before=(), deps=(), qb=256):
    s = qkv.shape[0]
    nq = s // qb
    hp = H // 2

    def columns(off):
        return pl.BlockSpec((s, 128), lambda g: (0, first + g + off))

    kept_shape = [sds((H, qb, (i + 1) * qb), bf16) for i in range(nq)]
    kept_spec = [pl.BlockSpec((2, qb, (i + 1) * qb), lambda g: (first + g, 0, 0)) for i in range(nq)]
    return pl.pallas_call(
        functools.partial(fwd_kernel, qb=qb, nq=nq, rc=32),
        grid=(groups,),
        in_specs=[smem(), columns(0), columns(hp), columns(2 * hp)] + [pl.BlockSpec(memory_space=pl.ANY)] * len(before),
        out_specs=[columns(0)] * 2 + kept_spec * 2,
        out_shape=[sds((s, H * HD), bf16), sds((s, H * HD), f32)] + kept_shape * 2,
        input_output_aliases={4 + k: k for k in range(len(before))},
        scratch_shapes=[
            pltpu.VMEM((2, qb, s), f32),
            pltpu.VMEM((2, qb, 128), f32),
            pltpu.VMEM((qb, 128), f32),
        ],
        compiler_params=params(60),
        cost_estimate=cost(7.5 * groups),
    )(tie(lens, *deps), qkv, qkv, qkv, *before)


def bwd_kernel(len_ref, q_ref, k_ref, v_ref, o_ref, rz_ref, d_ref, *rest, qb, nq, rc):
    p_refs, a_refs = rest[:nq], rest[nq : 2 * nq]
    out, dk_ref, dv_ref, dp_ref, ds_ref, low_ref, total_ref, low_t, q_t, dq_ref = rest[-10:]
    n = len_ref[0]
    scale = HD ** (-0.5)
    lane = lax.broadcasted_iota(jnp.int32, (1, 128), 1)
    dk_ref[...] = jnp.zeros_like(dk_ref)
    dv_ref[...] = jnp.zeros_like(dv_ref)

    def emit(blocks):
        units = [(i, h) for i in blocks for h in range(2)]

        def weight_grads(t):
            i, h = units[t]
            nk = (i + 1) * qb
            mine = (lane < HD) if h == 0 else (lane >= HD)
            if h == 0:
                rows = slice(i * qb, (i + 1) * qb)
                grad = d_ref[rows, :] * rz_ref[rows, :]
                low = grad.astype(bf16)
                along = grad * o_ref[rows, :].astype(f32)
                low_ref[i % 2] = low
                low_t[i % 2] = low.T
                q_t[i % 2] = q_ref[rows, :].T
                for k in range(2):
                    half = jnp.where((lane < HD) if k == 0 else (lane >= HD), along, 0.0)
                    total_ref[i % 2, k] = jnp.broadcast_to(jnp.sum(half, axis=1, keepdims=True), (qb, 128))
            low = low_ref[i % 2]
            dp_ref[t % 2, :, :nk] = dot(jnp.where(mine, low, jnp.zeros_like(low)), v_ref[:nk, :], NT)

        def score_grads(t):
            i, h = units[t]
            for r0 in range(0, qb, rc):
                rr = slice(r0, r0 + rc)
                total = jnp.concatenate([total_ref[i % 2, h, rr, :]] * (qb // 128), axis=1)
                for j in range(i + 1):
                    cols = slice(j * qb, (j + 1) * qb)
                    first = a_refs[i][h, rr, cols].astype(f32) * dp_ref[t % 2, rr, cols]
                    ds_ref[t % 2, rr, cols] = (first - p_refs[i][h, rr, cols].astype(f32) * total).astype(bf16)

        def grads(t):
            i, h = units[t]
            nk = (i + 1) * qb
            part = slice(h * HD, (h + 1) * HD)
            ds = ds_ref[t % 2, :, :nk]
            dq = dot(ds, k_ref[:nk, :], NN)
            if h == 0:
                dq_ref[...] = dq
            else:
                out[0, i * qb : nk, :] = (jnp.where(lane < HD, dq_ref[...], dq) * scale).astype(bf16)
            dv_ref[part, :nk] += dot(low_t[i % 2, part, :], p_refs[i][h], NN)
            dk_ref[part, :nk] += dot(q_t[i % 2, part, :], ds, NN)

        weight_grads(0)
        for t in range(len(units)):
            if t + 1 < len(units):
                weight_grads(t + 1)
            score_grads(t)
            grads(t)

    by_blocks(n, qb, nq, emit, lambda rows: dead_block(rows, (out.at[0],)))
    out[1] = (dk_ref[...] * scale).T.astype(bf16)
    out[2] = dv_ref[...].T.astype(bf16)


def attention_backward(lens, qkv, o, rz, dol, kept, deps=(), qb=256, first=0, groups=H // 2):
    s = qkv.shape[0]
    nq = s // qb
    hp = H // 2

    def columns(off):
        return pl.BlockSpec((s, 128), lambda g: (0, first + g + off))

    kept_spec = [pl.BlockSpec((2, qb, (i + 1) * qb), lambda g: (first + g, 0, 0)) for i in range(nq)]
    return pl.pallas_call(
        functools.partial(bwd_kernel, qb=qb, nq=nq, rc=64),
        grid=(groups,),
        in_specs=[smem(), columns(0), columns(hp), columns(2 * hp)] + [columns(0)] * 3 + kept_spec * 2,
        out_specs=pl.BlockSpec((3, s, 128), lambda g: (0, 0, g)),
        out_shape=sds((3, s, 128 * groups), bf16),
        scratch_shapes=[pltpu.VMEM((128, s), f32)] * 2
        + [
            pltpu.VMEM((2, qb, s), f32),
            pltpu.VMEM((2, qb, s), bf16),
            pltpu.VMEM((2, qb, 128), bf16),
            pltpu.VMEM((2, 2, qb, 128), f32),
            pltpu.VMEM((2, 128, qb), bf16),
            pltpu.VMEM((2, 128, qb), bf16),
            pltpu.VMEM((qb, 128), f32),
        ],
        compiler_params=params(40),
        cost_estimate=cost(26),
    )(tie(lens, *deps), qkv, qkv, qkv, o, rz, dol, *kept)


def ffn_kernel(len_ref, idx_ref, x_ref, o_ref, ct_ref, *rest, rb, n, nu, pieces, cut):
    parts, rest = rest[:pieces], rest[pieces:]
    bo_ref, g2_ref, b2_ref, bu_ref, bd_ref = rest[:5]
    (y_ref, g_ref, du_ref, c_ref, dyl_ref, drl_ref, dr_ref, dol_ref) = rest[5:13]
    sbd, sbu, sg2, sb2, sbo, w_ref, wd, sems = rest[13:]
    i = pl.program_id(0)
    d = x_ref.shape[1]
    each = d // n
    chips, rows, wide = w_ref.shape

    def weight(at):
        return w_ref[:, :, at : at + d].reshape(d, d)

    core = idx_ref[3]

    def copies(k):
        if pieces == 1:
            return [pltpu.make_async_copy(parts[0], w_ref, sems.at[0])]
        who, later, half = core if k < 4 else 1 - core, (k // 2) % 2, wide // 2
        lane = pl.multiple_of(who * half + later * cut, 128)
        size = half - cut if later else cut
        return [
            pltpu.make_async_copy(
                parts[k].at[at], w_ref.at[gathered_chip(idx_ref, k, at), :, pl.ds(lane, size)], sems.at[k * 8 + at]
            )
            for at in range(8)
        ]

    def wait(which):
        for k in which:
            for copy in copies(k):
                copy.wait()

    order = (0, 1, 4, 5, 2, 3, 6, 7) if pieces > 1 else (0,)

    @pl.when(i == 0)
    def _():
        for k in order:
            for copy in copies(k):
                copy.start()
        for s in (sbd, sbu, sg2, sb2, sbo):
            s[...] = jnp.zeros_like(s)
        wait(order[:4])

    live = (lax.broadcasted_iota(jnp.int32, (rb, 1), 0) + i * rb) < len_ref[0]
    r = x_ref[...].astype(f32) + dot(o_ref[...], weight(0), NN) + bo_ref[...]
    n2, k2 = norm_stats(r)
    g2 = g2_ref[...]
    c = (n2 * g2 + b2_ref[...]).astype(bf16)
    c_ref[...] = c
    dyl = jnp.where(live, ct_ref[...], jnp.zeros((), bf16))
    dyl_ref[...] = dyl
    y = r + bd_ref[...]
    dc = jnp.zeros_like(r)

    @pl.when(i == 0)
    def _():
        wait(order[4:])
        for dev in range(n):
            for j in range(nu):
                at = (dev * nu + j) * each
                row = dev * each
                lane = (1 + nu + j) * d
                wd[at : at + each, :] = w_ref[row // rows, row % rows : row % rows + each, lane : lane + d]

    k0 = math.sqrt(2 / math.pi)
    for j in range(nu):
        cols = slice(j * d, (j + 1) * d)
        wu = weight((1 + j) * d)
        wdj = wd[cols, :]
        u = dot(c, wu, NN) + bu_ref[:, cols]
        t = dot(dyl, wdj, NT)
        u2 = u * u
        hp = 0.5 + 0.5 * jnp.tanh(u * (k0 + (k0 * 0.044715) * u2))
        g = (u * hp).astype(bf16)
        slope = hp + u * (2.0 * hp * (1.0 - hp)) * (k0 + (3 * k0 * 0.044715) * u2)
        du = (t * slope).astype(bf16)
        g_ref[:, cols] = g
        du_ref[:, cols] = du
        y = y + dot(g, wdj, NN)
        dc = dc + dot(du, wu, NT)
        sbu[:, cols] += jnp.sum(du.astype(f32), axis=0, keepdims=True)
    y_ref[...] = jnp.where(live, y, 0.0).astype(bf16)
    q2 = dc * g2
    inner = q2 - jnp.mean(q2, axis=1, keepdims=True) - n2 * jnp.mean(q2 * n2, axis=1, keepdims=True)
    dr = dyl.astype(f32) + k2 * inner
    dr_ref[...] = dr
    drl = dr.astype(bf16)
    drl_ref[...] = drl
    dol_ref[...] = dot(drl, weight(0), NT)
    sbd[...] += jnp.sum(dyl.astype(f32), axis=0, keepdims=True)
    sg2[...] += jnp.sum(dc * n2, axis=0, keepdims=True)
    sb2[...] += jnp.sum(dc, axis=0, keepdims=True)
    sbo[...] += jnp.sum(drl.astype(f32), axis=0, keepdims=True)


def ffn_call(lens, idx, x, o, ct, parts, bo, g2, b2, bu, bd, n, cut, rb=256):
    s, d = x.shape
    ff = bu.shape[1]
    nu = ff // d
    wide = d + 2 * ff

    def row(w):
        return pl.BlockSpec((rb, w), lambda i: (i, 0))

    def acc(w):
        return pl.BlockSpec((1, w), lambda i: (0, 0))

    return pl.pallas_call(
        functools.partial(ffn_kernel, rb=rb, n=n, nu=nu, pieces=len(parts), cut=cut),
        grid=(s // rb,),
        in_specs=[smem(), smem(), row(d), row(d), row(d)]
        + [pl.BlockSpec(memory_space=pltpu.HBM)] * len(parts)
        + [whole((1, d)), whole((1, d)), whole((1, d)), whole((1, ff)), whole((1, d))],
        out_specs=[row(d), row(ff), row(ff), row(d), row(d), row(d), row(d), row(d)]
        + [acc(d), acc(ff), acc(d), acc(d), acc(d)],
        out_shape=[
            sds((s, d), bf16),
            sds((s, ff), bf16),
            sds((s, ff), bf16),
            sds((s, d), bf16),
            sds((s, d), bf16),
            sds((s, d), bf16),
            sds((s, d), f32),
            sds((s, d), f32),
            sds((1, d), f32),
            sds((1, ff), f32),
            sds((1, d), f32),
            sds((1, d), f32),
            sds((1, d), f32),
        ],
        scratch_shapes=[
            pltpu.VMEM((d // 48, 48, wide), bf16),
            pltpu.VMEM((ff, d), bf16),
            pltpu.SemaphoreType.DMA((64,)),
        ],
        compiler_params=params(60),
        cost_estimate=cost(37),
    )(lens, idx, x, o, ct, *parts, bo, g2, b2, bu, bd)


def wgrad_kernel(a_ref, b_ref, o_ref):
    b = b_ref[0] if len(b_ref.shape) == 3 else b_ref[...]
    o_ref[...] = dot(a_ref[...], b, TN).astype(o_ref.dtype)


def wgrad(a, b, ta, tb):
    s, m = a.shape
    if b.ndim == 3:
        n = b.shape[0] * b.shape[2]
        b_spec = pl.BlockSpec((1, s, b.shape[2]), lambda i, j: (j, 0, 0))
        tb = b.shape[2]
    else:
        n = b.shape[1]
        b_spec = pl.BlockSpec((s, tb), lambda i, j: (0, j))
    return pl.pallas_call(
        wgrad_kernel,
        grid=(m // ta, n // tb),
        in_specs=[pl.BlockSpec((s, ta), lambda i, j: (0, i)), b_spec],
        out_specs=pl.BlockSpec((ta, tb), lambda i, j: (i, j)),
        out_shape=sds((m, n), bf16),
        compiler_params=params(40),
        cost_estimate=cost(9),
    )(a, b)


def by_core(idx_ref, grad, keep, send, each):
    pairs = grad.reshape(grad.shape[0] // (2 * each), 2, each, grad.shape[1])
    first = idx_ref[3] == 0
    keep[...] = jnp.where(first, pairs[:, 0], pairs[:, 1]).astype(bf16)
    send[...] = jnp.where(first, pairs[:, 1], pairs[:, 0]).astype(bf16)


def down_kernel(idx_ref, g_ref, b_ref, keep, send, *, each, nu):
    grad = dot(g_ref[...], b_ref[...], TN)
    d = grad.shape[1]
    chips = grad.shape[0] // (2 * each * nu)
    parts = grad.reshape(chips, 2, nu, each, d)
    first = idx_ref[3] == 0
    for j in range(nu):
        cols = slice(j * d, (j + 1) * d)
        keep[:, :, cols] = jnp.where(first, parts[:, 0, j], parts[:, 1, j]).astype(bf16)
        send[:, :, cols] = jnp.where(first, parts[:, 1, j], parts[:, 0, j]).astype(bf16)


def down_grad(idx, g, dyl, n):
    s, ff = g.shape
    d = dyl.shape[1]
    each, nu = d // n, ff // d
    chips = n // 2 // nu
    spec = pl.BlockSpec((chips, each, ff), lambda i: (i, 0, 0))
    return pl.pallas_call(
        functools.partial(down_kernel, each=each, nu=nu),
        grid=(nu,),
        in_specs=[smem(), pl.BlockSpec((s, d), lambda i: (0, i)), whole((s, d))],
        out_specs=[spec, spec],
        out_shape=[sds((n // 2, each, ff), bf16)] * 2,
        compiler_params=params(60),
        cost_estimate=cost(9),
    )(idx, g, dyl)


def up_kernel(idx_ref, c_ref, du_ref, keep, send, *, each):
    by_core(idx_ref, dot(c_ref[...], du_ref[...], TN), keep, send, each)


def up_grad(idx, c, du, n):
    s, d = c.shape
    ff = du.shape[1]
    each = d // n
    spec = pl.BlockSpec((n // 2, each, d), lambda j: (0, 0, j))
    return pl.pallas_call(
        functools.partial(up_kernel, each=each),
        grid=(ff // d,),
        in_specs=[smem(), whole((s, d)), pl.BlockSpec((s, d), lambda j: (0, j))],
        out_specs=[spec, spec],
        out_shape=[sds((n // 2, each, ff), bf16)] * 2,
        compiler_params=params(60),
        cost_estimate=cost(9),
    )(idx, c, du)


def attention_grads_kernel(idx_ref, a_ref, dqkv_ref, o_ref, drl_ref, *rest, each):
    keep_a, send_a, keep_b, send_b = rest[-4:]
    j = pl.program_id(0)

    @pl.when(j < 2)
    def _():
        by_core(idx_ref, dot(a_ref[...], dqkv_ref[0], TN), keep_a, send_a, each)

    @pl.when(j == 2)
    def _():
        by_core(idx_ref, dot(a_ref[...], dqkv_ref[0], TN), keep_b, send_b, each)

    @pl.when(j == 3)
    def _():
        by_core(idx_ref, dot(o_ref[...], drl_ref[...], TN), keep_b, send_b, each)


def attention_grads(idx, a, dqkv, o, drl, n, deps=()):
    s, d = a.shape
    each = d // n
    spec_a = pl.BlockSpec((n // 2, each, d), lambda j: (0, 0, jnp.minimum(j, 1)))
    spec_b = pl.BlockSpec((n // 2, each, d), lambda j: (0, 0, jnp.maximum(j - 2, 0)))
    return pl.pallas_call(
        functools.partial(attention_grads_kernel, each=each),
        grid=(4,),
        in_specs=[
            smem(),
            whole((s, d)),
            pl.BlockSpec((1, s, d), lambda j: (jnp.minimum(j, 2), 0, 0)),
            whole((s, d)),
            whole((s, d)),
        ]
       ,
        out_specs=[spec_a, spec_a, spec_b, spec_b],
        out_shape=[sds((n // 2, each, 2 * d), bf16)] * 4,
        compiler_params=params(40),
        cost_estimate=cost(40),
    )(tie(idx, *deps), a, dqkv, o, drl)


def first_kernel(x_ref, dr_ref, dq_ref, w_ref, g_ref, sbo, sg2, sb2, sbd, sbu, *rest):
    gi_ref, out = rest[-2:]
    i = pl.program_id(0)
    d = x_ref.shape[1]
    quarter = w_ref.shape[3]

    @pl.when(i == 0)
    def _():
        out[:, : 5 * d] = jnp.zeros((1, 5 * d), f32)
        for k, ref in enumerate((sbo, sg2, sb2, sbd)):
            out[:, (5 + k) * d : (6 + k) * d] = ref[...]
        out[:, 9 * d :] = sbu[...]

    normal, inverse = norm_stats(x_ref[...].astype(f32))
    da = jnp.zeros(normal.shape, f32)
    for k in range(4):
        w = w_ref[k].reshape(d, quarter)
        at = k * quarter
        while at < min((k + 1) * quarter, 3 * d):
            j = at // d
            end = min((k + 1) * quarter, (j + 1) * d)
            part = dq_ref[j, :, at - j * d : end - j * d]
            da = da + dot(part, w[:, at - k * quarter : end - k * quarter], NT)
            out[:, 2 * d + at : 2 * d + end] += jnp.sum(part.astype(f32), axis=0, keepdims=True)
            at = end
    q1 = da * g_ref[...]
    inner = (
        q1 - jnp.mean(q1, axis=1, keepdims=True) - normal * jnp.mean(q1 * normal, axis=1, keepdims=True)
    )
    gi_ref[...] = dr_ref[...] + inverse * inner
    out[:, :d] += jnp.sum(da * normal, axis=0, keepdims=True)
    out[:, d : 2 * d] += jnp.sum(da, axis=0, keepdims=True)


def first_backward(x, dr, dqkv, w, gain, sums, deps=(), rb=256):
    s, d = x.shape

    def row(w):
        return pl.BlockSpec((rb, w), lambda i: (i, 0))

    wide = 9 * d + sums[-1].shape[1]
    return pl.pallas_call(
        first_kernel,
        grid=(s // rb,),
        in_specs=[row(d), row(d), pl.BlockSpec((3, rb, d), lambda i: (0, i, 0)), whole(w.shape), whole((1, d))]
        + [whole(t.shape) for t in sums]
       ,
        out_specs=[row(d), pl.BlockSpec((1, wide), lambda i: (0, 0))],
        out_shape=[sds((s, d), f32), sds((1, wide), f32)],
        compiler_params=params(40),
        cost_estimate=cost(10),
    )(x, dr, dqkv, w, tie(gain, *deps), *sums)


def scatter_sum(buf, n, order):
    lin = lax.axis_index(AXES)
    bits = n.bit_length() - 1
    rest = buf.shape[1:]
    buf = buf.reshape((2,) * bits + rest)
    left = list(range(bits - 1, -1, -1))
    for step, b in enumerate(order):
        axis = left.index(b)
        left.pop(axis)
        bit = (lin >> b) & 1
        send = lax.dynamic_index_in_dim(buf, 1 - bit, axis, keepdims=False)
        keep = lax.dynamic_index_in_dim(buf, bit, axis, keepdims=False)
        got = lax.ppermute(send, AXES, [(i, i ^ (1 << b)) for i in range(n)])
        buf = keep.astype(f32) + got.astype(f32)
        if step < bits - 1:
            buf = buf.astype(send.dtype)
    return buf


def permute(x, mask, n=32):
    return lax.ppermute(x, AXES, [(i, i ^ mask) for i in range(n)])


CORE, XBIT, YBIT = 1, 8, 16


def join(block, got):
    return jnp.concatenate([block[None], got[None]])


def gather_cores(mine, theirs, core):
    got = permute(theirs, CORE)
    return jnp.where(core == 0, jnp.concatenate([mine, got]), jnp.concatenate([got, mine]))


def gather_first(block, cut):
    a, b = block[..., :cut], block[..., cut:]
    return a, permute(a, XBIT), b, permute(b, YBIT)


def gather_second(a, b):
    parts = (a, permute(a, YBIT), b, permute(b, XBIT))
    return [t.reshape((8,) + t.shape[-2:]) for t in parts]


def fold_kernel(idx_ref, *refs, plan, joined):
    ins, outs = refs[: 2 * len(plan)], refs[-2 if joined else -2 * len(plan) :]
    lane = 0
    for k, (dim, which) in enumerate(plan):
        kept, got = ins[2 * k], ins[2 * k + 1]
        lead, wide = kept.shape[:-2], kept.shape[-1]
        for side in range(2):
            out = outs[side if joined else 2 * k + side]
            at = idx_ref[which] if side == 0 else 1 - idx_ref[which]
            for t in itertools.product(*[range(m) for m in lead[:dim] + lead[dim + 1 :]]):
                source = t[:dim] + (at,) + t[dim:]
                value = (kept[source].astype(f32) + got[source].astype(f32)).astype(bf16)
                if joined:
                    out[t + (slice(None), slice(lane, lane + wide))] = value
                else:
                    out[t] = value
        lane += wide


def fold(idx, pairs, plan, us, deps=(), joined=False):
    stepped = pairs[0][0].ndim > 3 and not joined
    args, in_specs, out_specs, out_shape, total = [], [], [], [], 0
    for (kept, got), (dim, _) in zip(pairs, plan):
        lead, (each, wide) = kept.shape[:-2], kept.shape[-2:]
        left = lead[:dim] + lead[dim + 1 :]
        total += wide
        args += [kept, got]

        def spec(shape):
            if not stepped:
                return pl.BlockSpec()
            m = len(shape)
            return pl.BlockSpec(shape[:-3] + (1,) + shape[-2:], lambda i: (0,) * (m - 3) + (i, 0, 0))

        in_specs += [spec(kept.shape)] * 2
        out_specs += [spec(left + (each, wide))] * 2
        out_shape += [sds(left + (each, wide), bf16)] * 2
    if joined:
        out_specs, out_shape = [pl.BlockSpec()] * 2, [sds(left + (each, total), bf16)] * 2
    grid = {"grid": (pairs[0][0].shape[-3],)} if stepped else {}
    return pl.pallas_call(
        functools.partial(fold_kernel, plan=plan, joined=joined),
        in_specs=[smem()] + in_specs,
        out_specs=out_specs,
        out_shape=out_shape,
        compiler_params=params(24),
        cost_estimate=cost(us),
        **grid,
    )(tie(idx, *deps), *args)


def last_kernel(kept, got, *refs, cuts):
    outs = refs[-len(cuts) :]
    total = kept[...].astype(f32) + got[...].astype(f32)
    each = total.shape[0]
    at = 0
    for out, (rows, wide) in zip(outs, cuts):
        for j in range(rows):
            out[j * each : (j + 1) * each, :] = total[:, at : at + wide]
            at += wide


def fold_last(kept, got, cuts, deps=()):
    each = kept.shape[0]
    return pl.pallas_call(
        functools.partial(last_kernel, cuts=cuts),
        in_specs=[pl.BlockSpec()] * 2,
        out_specs=[pl.BlockSpec()] * len(cuts),
        out_shape=[sds((rows * each, wide), f32) for rows, wide in cuts],
        compiler_params=params(24),
        cost_estimate=cost(1),
    )(tie(kept, *deps), got)


def body(
    n,
    dp,
    layer_input,
    lengths,
    ln1_gain,
    ln1_bias,
    w_qkv,
    b_qkv,
    w_out,
    b_out,
    ln2_gain,
    ln2_bias,
    w_up,
    b_up,
    w_down,
    b_down,
    cotangent,
):
    s, d = layer_input.shape[1:]
    x = layer_input.reshape(s, d)
    ct = cotangent.reshape(s, d)
    e, ff = w_qkv.shape[1], w_up.shape[1]
    each = d // n
    nu = ff // d
    fast = n == 32 and dp == 4
    lin = lax.axis_index(AXES)
    idx = jnp.stack([(lin >> 3) & 1, (lin >> 4) & 1, (lin >> 1) & 3, lin & 1, (lin >> 1) & 1, (lin >> 2) & 1]).astype(jnp.int32)
    vectors = (ln1_gain, ln1_bias, b_out, ln2_gain, ln2_bias, b_down, b_qkv, b_up)
    layout = vector_layout(each, d, e, ff)
    mine, theirs, mine_rest, theirs_rest = prepare(idx, w_qkv, w_out, w_up, w_down, vectors, layout)
    cut_q, cut_r = (e + 256) // 4, 128 * (-(-(d + 2 * ff) // 512))
    if fast:
        core = lin & 1
        q = gather_cores(mine, theirs, core)
        r = gather_cores(mine_rest, theirs_rest, core)
        q = join(q, permute(q, 4))
        q = tie(q, r)
        q = join(q, permute(q, 2))
        r = tie(r, q)
        a0, a1, b0, b1 = gather_first(q, cut_q)
        got_r = permute(r, 4)
        qa, qb = join(a0, a1), join(b0, b1)
        parts = gather_second(qa, qb)
        r = join(r, tie(got_r, qa, qb))
        parts[1], parts[3] = tie(parts[1], r), tie(parts[3], r)
        parts += [permute(t, CORE) for t in parts]
        ra, rb = r[..., :cut_r], r[..., cut_r:]
        ra, rb = join(ra, permute(ra, 2)), join(rb, permute(rb, 2))
        got_ra, got_rb = permute(ra, XBIT), permute(rb, YBIT)
        x_in = tie(x, ra, rb)
    else:
        def gathered(own, other):
            both = jnp.where((lin & 1) == 0, jnp.concatenate([own, other], 1), jnp.concatenate([other, own], 1))
            return lax.all_gather(both, AXES, axis=0, tiled=True)

        x_in = x
        parts = [gathered(mine, theirs)]
        rest = [gathered(mine_rest, theirs_rest).reshape(d // 48, 48, d + 2 * ff)]
    a, qkv, wq, g1, b1, bo, g2, b2, bd, bq, bu = qkv_call(idx, x_in, parts, n, layout, e)
    if fast:
        ra, rb = join(ra, tie(got_ra, qkv)), join(rb, tie(got_rb, qkv))
        ra, ga, rb, gb = gather_second(ra, rb)
        o, rz, *kept = attention_forward(lengths, qkv, 0, H // 2, deps=(ra, rb))
        other_ra, other_rb = permute(ra, CORE), permute(rb, CORE)
        ga, gb = tie(ga, o, other_ra, other_rb), tie(gb, o, other_ra, other_rb)
        rest = [ra, ga, rb, gb, other_ra, permute(ga, CORE), other_rb, permute(gb, CORE)]
    else:
        o, rz, *kept = attention_forward(lengths, qkv, 0, H // 2)
    (y, g, du, c, dyl, drl, dr, dol, sbd, sbu, sg2, sb2, sbo) = ffn_call(
        lengths, idx, x, o, ct, rest, bo, g2, b2, bu, bd, n, cut_r
    )
    sums = (sbo, sg2, sb2, sbd, sbu)
    if fast:
        core_x, core_y, deep_0, deep_1 = 0, 1, 4, 5

        def chips(t):
            return t.reshape((2, 2, 4) + t.shape[1:])

        def deep(t):
            return t.reshape((2, 2) + t.shape[1:])

        keep_d, send_d = down_grad(idx, g, dyl, n)
        got_d = permute(send_d, CORE)
        keep_u, send_u = up_grad(idx, c, du, n)
        got_u = permute(send_u, CORE)
        kd, sd = fold(idx, [(chips(keep_d), chips(got_d))], [(1, core_x)], 2.5, deps=(keep_u,))
        rd = permute(sd, XBIT)
        ku, su = fold(idx, [(chips(keep_u), chips(got_u))], [(0, core_y)], 2.5, deps=(kd,))
        ru = permute(su, YBIT)
        dqkv = attention_backward(lengths, qkv, o, rz, dol, kept, deps=(ku,))
        kd, sd, ku, su = fold(idx, [(kd, rd), (ku, ru)], [(0, core_y), (0, core_x)], 2.5, deps=(dqkv,))
        rd, ru = permute(sd, YBIT), permute(su, XBIT)
        ka, sa, kb, sb = attention_grads(idx, a, dqkv, o, drl, n, deps=(kd,))
        ga, gb = permute(sa, CORE), permute(sb, CORE)
        pairs = [(deep(kd), deep(rd)), (deep(ku), deep(ru))]
        kw, sw = fold(idx, pairs, [(1, deep_0)] * 2, 30, deps=(ka,), joined=True)
        rw = permute(sw, 2)
        pairs = [(chips(ka), chips(ga)), (chips(kb), chips(gb))]
        ka, sa, kb, sb = fold(idx, pairs, [(1, core_x), (0, core_y)], 2.5, deps=(kw,))
        ra, rb = permute(sa, XBIT), permute(sb, YBIT)
        grad_input, total = first_backward(x, dr, dqkv, wq, g1, sums, deps=(ka,))
        got = permute(total, CORE)
        kw, sw = fold(idx, [(kw, rw)], [(0, deep_1)], 1, deps=(total,))
        rw = permute(sw, 4)
        ka, sa, kb, sb = fold(idx, [(ka, ra), (kb, rb)], [(0, core_y), (0, core_x)], 1, deps=(kw,))
        ra, rb = permute(sa, YBIT), permute(sb, XBIT)
        total = total + tie(got, ka)
        got = [permute(total, mask) for mask in (XBIT, YBIT, XBIT | YBIT)]
        grad_down, grad_up = fold_last(kw, rw, [(nu, d), (1, ff)], deps=(ra, rb))
        got = lax.optimization_barrier((*got, grad_up))
        total = total + got[0] + got[1] + got[2]
        pairs = [(deep(ka), deep(ra)), (deep(kb), deep(rb))]
        kq, sq = fold(idx, pairs, [(1, deep_0)] * 2, 1, deps=(grad_up, total), joined=True)
        rq = permute(sq, 2)
        got = [permute(total, mask) for mask in (2, 4, 6)]
        kq, sq = fold(idx, [(kq, rq)], [(0, deep_1)], 1)
        rq = permute(sq, 4)
        got = lax.optimization_barrier((*got, kq))
        total = total + got[0] + got[1] + got[2]
        grad_qkv, grad_out = fold_last(kq, rq, [(1, e), (1, d)])
    else:
        order = list(range(n.bit_length() - 1))
        grad_down = scatter_sum(wgrad(g, dyl, d, d).reshape(n, ff // n, d), n, order)
        grad_up = scatter_sum(wgrad(c, du, d, d).reshape(n, each, ff), n, order)
        grad_out = scatter_sum(wgrad(o, drl, d, d).reshape(n, each, d), n, order)
        dqkv = attention_backward(lengths, qkv, o, rz, dol, kept)
        grad_qkv = scatter_sum(wgrad(a, dqkv, d, d).reshape(n, each, e), n, order)
        grad_input, total = first_backward(x, dr, dqkv, wq, g1, sums)
        total = lax.psum(total, AXES)
    shares, at = [], 0
    for size in (each, each, 3 * each, each, each, each, each, nu * each):
        shares.append(lax.dynamic_slice_in_dim(total[0], at + lin * size, size))
        at += n * size
    gs1, gb1, gbq, gbo, gs2, gb2, gbd, gbu = shares
    return (
        y.reshape(layer_input.shape),
        grad_input.reshape(layer_input.shape),
        gs1,
        gb1,
        grad_qkv,
        gbq,
        grad_out,
        gbo,
        gs2,
        gb2,
        grad_up,
        gbu,
        grad_down,
        gbd,
    )


def solution(mesh):
    split = P(AXES)
    wide = P(AXES, None)
    cube = P(AXES, None, None)
    in_specs = (
        cube, split, split, split, wide, split, wide, split, split, split, wide, split, wide, split, cube,
    )
    out_specs = (
        cube, cube, split, split, wide, split, wide, split, split, split, wide, split, wide, split,
    )
    n = mesh.shape["dp"] * mesh.shape["fsdp"]
    return jax.shard_map(
        functools.partial(body, n, mesh.shape["dp"]),
        mesh=mesh,
        in_specs=in_specs,
        out_specs=out_specs,
        check_vma=False,
    )
```

```python
import functools
import itertools
import math

import jax
import jax.numpy as jnp
from jax import lax
from jax.experimental import pallas as pl
from jax.experimental.pallas import tpu as pltpu
from jax.sharding import PartitionSpec as P

H = 12
HD = 64
AXES = ("dp", "fsdp")
NORM_EPS = 1e-05
LOG2E = math.log2(math.e)
NT = (((1,), (1,)), ((), ()))
NN = (((1,), (0,)), ((), ()))
TN = (((0,), (0,)), ((), ()))
bf16 = jnp.bfloat16
f32 = jnp.float32
MIB = 2**20


def dot(a, b, dims):
    return lax.dot_general(a, b, dims, preferred_element_type=f32)


def whole(shape):
    return pl.BlockSpec(shape, lambda *i: (0,) * len(shape), pipeline_mode=pl.Buffered(1))


def smem():
    return pl.BlockSpec(memory_space=pltpu.SMEM)


def tie(value, *others):
    return lax.optimization_barrier((value, *others))[0]


def params(mib):
    return pltpu.CompilerParams(vmem_limit_bytes=mib * MIB)


def sds(shape, dtype):
    return jax.ShapeDtypeStruct(shape, dtype)


def cost(us):
    return pl.CostEstimate(flops=int(us * 1e9), bytes_accessed=0, transcendentals=0)


def norm_stats(values):
    mean = jnp.mean(values, axis=1, keepdims=True)
    centred = values - mean
    inverse = lax.rsqrt(jnp.mean(centred * centred, axis=1, keepdims=True) + NORM_EPS)
    return centred * inverse, inverse


def vector_layout(each, d, e, ff):
    return [(1, each * k, each) for k in range(6)] + [(0, 0, each * (e // d)), (0, 128, each * (ff // d))]


def by_half(ref, core, own, other):
    half = own.shape[1]
    own[...] = ref[:, pl.ds(pl.multiple_of(core * half, 128), half)]
    other[...] = ref[:, pl.ds(pl.multiple_of((1 - core) * half, 128), half)]


def fetch(pairs, sems):
    copies = [pltpu.make_async_copy(ref, to, sems.at[k]) for k, (ref, to) in enumerate(pairs)]
    for copy in copies:
        copy.start()
    return copies


def prepare_kernel(*refs, layout):
    ins, (own, other), (both, low, sems), small = refs[:9], refs[9:11], refs[11:14], refs[14:]
    e = ins[0].shape[1]
    copies = fetch(list(zip(ins, (both.at[:, :e], *small))), sems)
    low[...] = jnp.zeros_like(low)
    for copy in copies:
        copy.wait()
    for k, (row, lane, size) in enumerate(layout):
        low[row : row + 1, lane : lane + size] = small[k][...].astype(f32)
    both[:, e:] = low[...].astype(bf16)
    by_half(both, lax.axis_index("fsdp") & 1, own, other)


def prepare(wq, vectors, layout):
    each, e = wq.shape
    return pl.pallas_call(
        functools.partial(prepare_kernel, layout=layout),
        in_specs=[pl.BlockSpec(memory_space=pltpu.HBM)] * 9,
        out_shape=[sds((each, (e + 256) // 2), bf16)] * 2,
        scratch_shapes=[
            pltpu.VMEM((each, e + 256), bf16),
            pltpu.VMEM((each, 256), f32),
            pltpu.SemaphoreType.DMA((9,)),
        ]
        + [pltpu.VMEM((1, v.shape[0]), bf16) for v in vectors],
        compiler_params=params(60),
        cost_estimate=cost(2),
    )(wq, *[v.reshape(1, -1) for v in vectors])


def prepare_rest_kernel(wo, wu, wd, own, other, rest, down, sems, *, nu):
    each, d = wo.shape
    ff = wu.shape[1]
    copies = fetch([(wo, rest.at[:, :d]), (wu, rest.at[:, d : d + ff]), (wd, down)], sems)
    for copy in copies:
        copy.wait()
    for j in range(nu):
        rest[:, d + ff + j * d : d + ff + (j + 1) * d] = down[j * each : (j + 1) * each, :]
    by_half(rest, lax.axis_index("fsdp") & 1, own, other)


def prepare_rest(wo, wu, wd):
    each, d = wo.shape
    ff = wu.shape[1]
    wide = d + 2 * ff
    return pl.pallas_call(
        functools.partial(prepare_rest_kernel, nu=ff // d),
        in_specs=[pl.BlockSpec(memory_space=pltpu.HBM)] * 3,
        out_shape=[sds((each, wide // 2), bf16)] * 2,
        scratch_shapes=[
            pltpu.VMEM((each, wide), bf16),
            pltpu.VMEM(wd.shape, bf16),
            pltpu.SemaphoreType.DMA((3,)),
        ],
        compiler_params=params(60),
        cost_estimate=cost(2),
    )(wo, wu, wd)


def gathered_chip(idx_ref, k, at):
    x, y, z = (idx_ref[i] for i in range(3))
    first, deep = at // 4, z ^ ((at // 2) % 2 + 2 * (at % 2))
    second = k % 2
    if (k // 2) % 2 == 0:
        return ((y ^ second) * 2 + (x ^ first)) * 4 + deep
    return ((y ^ first) * 2 + (x ^ second)) * 4 + deep


def qkv_kernel(idx_ref, x_ref, *rest, n, each, layout, pieces):
    parts, (a_ref, o_ref, w_ref), vecs, low = rest[:pieces], rest[pieces : pieces + 3], rest[pieces + 3 : -1], rest[-1]
    quarter = w_ref.shape[3]
    e = o_ref.shape[1]

    @pl.when(pl.program_id(0) == 0)
    def _():
        if pieces == 1:
            for k in range(4):
                w_ref[k] = parts[0][:, k * quarter : (k + 1) * quarter].reshape(w_ref.shape[1:])
        else:
            core = idx_ref[3]
            for k, part in enumerate(parts):
                quarter_at = 2 * (core if k < 4 else 1 - core) + (k // 2) % 2
                for at in range(8):
                    w_ref[quarter_at, gathered_chip(idx_ref, k, at)] = part[at]
        low[...] = w_ref[3, :, :, quarter - 256 :].astype(f32)
        for dev in range(n):
            for out, (row, lane, size) in zip(vecs, layout):
                at = dev * each + row
                out[:, dev * size : (dev + 1) * size] = low[at // 48, at % 48 : at % 48 + 1, lane : lane + size]

    normal, _ = norm_stats(x_ref[...].astype(f32))
    a = (normal * vecs[0][...] + vecs[1][...]).astype(bf16)
    a_ref[...] = a
    for k in range(4):
        cols = slice(k * quarter, min((k + 1) * quarter, e))
        wide = cols.stop - cols.start
        w = w_ref[k].reshape(a.shape[1], quarter)
        o_ref[:, cols] = (dot(a, w[:, :wide], NN) + vecs[6][:, cols]).astype(bf16)


def qkv_call(idx, x, parts, n, layout, e, rb=256):
    s, d = x.shape
    each = d // n
    quarter = (e + 256) // 4
    sizes = [n * size for _, _, size in layout]
    return pl.pallas_call(
        functools.partial(qkv_kernel, n=n, each=each, layout=layout, pieces=len(parts)),
        grid=(s // rb,),
        in_specs=[smem(), pl.BlockSpec((rb, d), lambda i: (i, 0))] + [whole(p.shape) for p in parts],
        out_specs=[
            pl.BlockSpec((rb, d), lambda i: (i, 0)),
            pl.BlockSpec((rb, e), lambda i: (i, 0)),
            whole((4, d // 48, 48, quarter)),
        ]
        + [whole((1, size)) for size in sizes],
        out_shape=[sds((s, d), bf16), sds((s, e), bf16), sds((4, d // 48, 48, quarter), bf16)]
        + [sds((1, size), f32) for size in sizes],
        scratch_shapes=[pltpu.VMEM((d // 48, 48, 256), f32)],
        compiler_params=params(60),
        cost_estimate=cost(9),
    )(idx, x, *parts)


def fwd_kernel(len_ref, q_ref, k_ref, v_ref, *refs, qb, nq, rc):
    s_ref, z_ref, m_ref = refs[-3:]
    o_ref, rz_ref, *kept = refs[-5 - 2 * nq : -3]
    p_refs, a_refs = kept[:nq], kept[nq:]
    n = len_ref[0]
    lane = lax.broadcasted_iota(jnp.int32, (1, 128), 1)

    def emit(blocks):
        units = [(i, h) for i in blocks for h in range(2)]

        def scores(t):
            i, h = units[t]
            q = q_ref[i * qb : (i + 1) * qb, :] * jnp.asarray(HD**-0.5, bf16)
            mine = (lane < HD) if h == 0 else (lane >= HD)
            nk = (i + 1) * qb
            s_ref[t % 2, :, :nk] = dot(jnp.where(mine, q, jnp.zeros_like(q)), k_ref[:nk, :], NT)

        def weights(t):
            i, h = units[t]
            for r0 in range(0, qb, rc):
                rr = slice(r0, r0 + rc)
                row = lax.broadcasted_iota(jnp.int32, (rc, qb), 0) + r0
                col = lax.broadcasted_iota(jnp.int32, (rc, qb), 1)
                mask = (col <= row) & (col < n - i * qb)
                top = jnp.where(mask, jnp.abs(s_ref[t % 2, rr, i * qb : (i + 1) * qb]), 0.0)
                for j in range(i):
                    top = jnp.maximum(top, jnp.abs(s_ref[t % 2, rr, j * qb : (j + 1) * qb]))
                top = jnp.max(top, axis=1, keepdims=True)
                top = jnp.sqrt(top * top + 1.0)
                total = jnp.zeros((rc, qb), f32)
                for j in range(i + 1):
                    cols = slice(j * qb, (j + 1) * qb)
                    s = s_ref[t % 2, rr, cols]
                    square = s * s + 1.0
                    inv = lax.rsqrt(square)
                    e = jnp.exp(square * inv - top)
                    if j == i:
                        e = jnp.where(mask, e, 0.0)
                    total = total + e
                    p_refs[i][h, rr, cols] = (s * inv * e).astype(bf16)
                    a_refs[i][h, rr, cols] = ((1.0 - inv * inv * (1.0 - inv)) * e).astype(bf16)
                rz = 1.0 / jnp.sum(total, axis=1, keepdims=True)
                z_ref[t % 2, rr, :] = jnp.broadcast_to(rz, (rc, 128))

        def mix(t):
            i, h = units[t]
            rows = slice(i * qb, (i + 1) * qb)
            rz = z_ref[t % 2]
            mixed = dot(p_refs[i][h], v_ref[: (i + 1) * qb, :], NN) * rz
            if h == 0:
                m_ref[...] = mixed
                rz_ref[rows, :] = rz
            else:
                o_ref[rows, :] = jnp.where(lane < HD, m_ref[...], mixed).astype(bf16)
                rz_ref[rows, :] = jnp.where(lane < HD, rz_ref[rows, :], rz)

        scores(0)
        for t in range(len(units)):
            if t + 1 < len(units):
                scores(t + 1)
            weights(t)
            mix(t)

    by_blocks(n, qb, nq, emit, lambda rows: dead_block(rows, (o_ref, rz_ref)))


def dead_block(rows, refs):
    for ref in refs:
        ref[rows, :] = jnp.zeros((rows.stop - rows.start, ref.shape[1]), ref.dtype)


def by_blocks(n, qb, nq, emit, dead):
    @pl.when(n > (nq - 1) * qb)
    def _():
        emit(list(range(nq)))

    @pl.when(n <= (nq - 1) * qb)
    def _():
        for i in range(nq):

            @pl.when(n > i * qb)
            def _():
                emit([i])

            @pl.when(n <= i * qb)
            def _():
                dead(slice(i * qb, (i + 1) * qb))


def attention_forward(lens, qkv, first, groups, before=(), deps=(), qb=256):
    s = qkv.shape[0]
    nq = s // qb
    hp = H // 2

    def columns(off):
        return pl.BlockSpec((s, 128), lambda g: (0, first + g + off))

    kept_shape = [sds((H, qb, (i + 1) * qb), bf16) for i in range(nq)]
    kept_spec = [pl.BlockSpec((2, qb, (i + 1) * qb), lambda g: (first + g, 0, 0)) for i in range(nq)]
    return pl.pallas_call(
        functools.partial(fwd_kernel, qb=qb, nq=nq, rc=32),
        grid=(groups,),
        in_specs=[smem(), columns(0), columns(hp), columns(2 * hp)] + [pl.BlockSpec(memory_space=pl.ANY)] * len(before),
        out_specs=[columns(0)] * 2 + kept_spec * 2,
        out_shape=[sds((s, H * HD), bf16), sds((s, H * HD), f32)] + kept_shape * 2,
        input_output_aliases={4 + k: k for k in range(len(before))},
        scratch_shapes=[
            pltpu.VMEM((2, qb, s), f32),
            pltpu.VMEM((2, qb, 128), f32),
            pltpu.VMEM((qb, 128), f32),
        ],
        compiler_params=params(60),
        cost_estimate=cost(7.5 * groups),
    )(tie(lens, *deps), qkv, qkv, qkv, *before)


def bwd_kernel(len_ref, q_ref, k_ref, v_ref, o_ref, rz_ref, d_ref, *rest, qb, nq, rc):
    p_refs, a_refs = rest[:nq], rest[nq : 2 * nq]
    out, dk_ref, dv_ref, dp_ref, ds_ref, low_ref, total_ref, low_t, q_t, dq_ref = rest[-10:]
    n = len_ref[0]
    scale = HD ** (-0.5)
    lane = lax.broadcasted_iota(jnp.int32, (1, 128), 1)
    dk_ref[...] = jnp.zeros_like(dk_ref)
    dv_ref[...] = jnp.zeros_like(dv_ref)

    def emit(blocks):
        units = [(i, h) for i in blocks for h in range(2)]

        def weight_grads(t):
            i, h = units[t]
            nk = (i + 1) * qb
            mine = (lane < HD) if h == 0 else (lane >= HD)
            if h == 0:
                rows = slice(i * qb, (i + 1) * qb)
                grad = d_ref[rows, :] * rz_ref[rows, :]
                low = grad.astype(bf16)
                along = grad * o_ref[rows, :].astype(f32)
                low_ref[i % 2] = low
                low_t[i % 2] = low.T
                q_t[i % 2] = q_ref[rows, :].T
                for k in range(2):
                    half = jnp.where((lane < HD) if k == 0 else (lane >= HD), along, 0.0)
                    total_ref[i % 2, k] = jnp.broadcast_to(jnp.sum(half, axis=1, keepdims=True), (qb, 128))
            low = low_ref[i % 2]
            dp_ref[t % 2, :, :nk] = dot(jnp.where(mine, low, jnp.zeros_like(low)), v_ref[:nk, :], NT)

        def score_grads(t):
            i, h = units[t]
            for r0 in range(0, qb, rc):
                rr = slice(r0, r0 + rc)
                total = jnp.concatenate([total_ref[i % 2, h, rr, :]] * (qb // 128), axis=1)
                for j in range(i + 1):
                    cols = slice(j * qb, (j + 1) * qb)
                    first = a_refs[i][h, rr, cols].astype(f32) * dp_ref[t % 2, rr, cols]
                    ds_ref[t % 2, rr, cols] = (first - p_refs[i][h, rr, cols].astype(f32) * total).astype(bf16)

        def grads(t):
            i, h = units[t]
            nk = (i + 1) * qb
            part = slice(h * HD, (h + 1) * HD)
            ds = ds_ref[t % 2, :, :nk]
            dq = dot(ds, k_ref[:nk, :], NN)
            if h == 0:
                dq_ref[...] = dq
            else:
                out[0, i * qb : nk, :] = (jnp.where(lane < HD, dq_ref[...], dq) * scale).astype(bf16)
            dv_ref[part, :nk] += dot(low_t[i % 2, part, :], p_refs[i][h], NN)
            dk_ref[part, :nk] += dot(q_t[i % 2, part, :], ds, NN)

        weight_grads(0)
        for t in range(len(units)):
            if t + 1 < len(units):
                weight_grads(t + 1)
            score_grads(t)
            grads(t)

    by_blocks(n, qb, nq, emit, lambda rows: dead_block(rows, (out.at[0],)))
    out[1] = (dk_ref[...] * scale).T.astype(bf16)
    out[2] = dv_ref[...].T.astype(bf16)


def attention_backward(lens, qkv, o, rz, dol, kept, deps=(), qb=256, first=0, groups=H // 2):
    s = qkv.shape[0]
    nq = s // qb
    hp = H // 2

    def columns(off):
        return pl.BlockSpec((s, 128), lambda g: (0, first + g + off))

    kept_spec = [pl.BlockSpec((2, qb, (i + 1) * qb), lambda g: (first + g, 0, 0)) for i in range(nq)]
    return pl.pallas_call(
        functools.partial(bwd_kernel, qb=qb, nq=nq, rc=64),
        grid=(groups,),
        in_specs=[smem(), columns(0), columns(hp), columns(2 * hp)] + [columns(0)] * 3 + kept_spec * 2,
        out_specs=pl.BlockSpec((3, s, 128), lambda g: (0, 0, g)),
        out_shape=sds((3, s, 128 * groups), bf16),
        scratch_shapes=[pltpu.VMEM((128, s), f32)] * 2
        + [
            pltpu.VMEM((2, qb, s), f32),
            pltpu.VMEM((2, qb, s), bf16),
            pltpu.VMEM((2, qb, 128), bf16),
            pltpu.VMEM((2, 2, qb, 128), f32),
            pltpu.VMEM((2, 128, qb), bf16),
            pltpu.VMEM((2, 128, qb), bf16),
            pltpu.VMEM((qb, 128), f32),
        ],
        compiler_params=params(40),
        cost_estimate=cost(26),
    )(tie(lens, *deps), qkv, qkv, qkv, o, rz, dol, *kept)


def ffn_kernel(len_ref, idx_ref, x_ref, o_ref, ct_ref, *rest, rb, n, nu, pieces, cut):
    parts, rest = rest[:pieces], rest[pieces:]
    bo_ref, g2_ref, b2_ref, bu_ref, bd_ref = rest[:5]
    (y_ref, g_ref, du_ref, c_ref, dyl_ref, drl_ref, dr_ref, dol_ref) = rest[5:13]
    sbd, sbu, sg2, sb2, sbo, w_ref, wd, sems = rest[13:]
    i = pl.program_id(0)
    d = x_ref.shape[1]
    each = d // n
    chips, rows, wide = w_ref.shape

    def weight(at):
        return w_ref[:, :, at : at + d].reshape(d, d)

    core = idx_ref[3]

    def copies(k):
        if pieces == 1:
            return [pltpu.make_async_copy(parts[0], w_ref, sems.at[0])]
        who, later, half = core if k < 4 else 1 - core, (k // 2) % 2, wide // 2
        lane = pl.multiple_of(who * half + later * cut, 128)
        size = half - cut if later else cut
        return [
            pltpu.make_async_copy(
                parts[k].at[at], w_ref.at[gathered_chip(idx_ref, k, at), :, pl.ds(lane, size)], sems.at[k * 8 + at]
            )
            for at in range(8)
        ]

    def wait(which):
        for k in which:
            for copy in copies(k):
                copy.wait()

    order = (0, 1, 4, 5, 2, 3, 6, 7) if pieces > 1 else (0,)

    @pl.when(i == 0)
    def _():
        for k in order:
            for copy in copies(k):
                copy.start()
        for s in (sbd, sbu, sg2, sb2, sbo):
            s[...] = jnp.zeros_like(s)
        wait(order[:4])

    live = (lax.broadcasted_iota(jnp.int32, (rb, 1), 0) + i * rb) < len_ref[0]
    r = x_ref[...].astype(f32) + dot(o_ref[...], weight(0), NN) + bo_ref[...]
    n2, k2 = norm_stats(r)
    g2 = g2_ref[...]
    c = (n2 * g2 + b2_ref[...]).astype(bf16)
    c_ref[...] = c
    dyl = jnp.where(live, ct_ref[...], jnp.zeros((), bf16))
    dyl_ref[...] = dyl
    y = r + bd_ref[...]
    dc = jnp.zeros_like(r)

    @pl.when(i == 0)
    def _():
        wait(order[4:])
        for dev in range(n):
            for j in range(nu):
                at = (dev * nu + j) * each
                row = dev * each
                lane = (1 + nu + j) * d
                wd[at : at + each, :] = w_ref[row // rows, row % rows : row % rows + each, lane : lane + d]

    k0 = math.sqrt(2 / math.pi)
    for j in range(nu):
        cols = slice(j * d, (j + 1) * d)
        wu = weight((1 + j) * d)
        wdj = wd[cols, :]
        u = dot(c, wu, NN) + bu_ref[:, cols]
        t = dot(dyl, wdj, NT)
        u2 = u * u
        hp = 0.5 + 0.5 * jnp.tanh(u * (k0 + (k0 * 0.044715) * u2))
        g = (u * hp).astype(bf16)
        slope = hp + u * (2.0 * hp * (1.0 - hp)) * (k0 + (3 * k0 * 0.044715) * u2)
        du = (t * slope).astype(bf16)
        g_ref[:, cols] = g
        du_ref[:, cols] = du
        y = y + dot(g, wdj, NN)
        dc = dc + dot(du, wu, NT)
        sbu[:, cols] += jnp.sum(du.astype(f32), axis=0, keepdims=True)
    y_ref[...] = jnp.where(live, y, 0.0).astype(bf16)
    q2 = dc * g2
    inner = q2 - jnp.mean(q2, axis=1, keepdims=True) - n2 * jnp.mean(q2 * n2, axis=1, keepdims=True)
    dr = dyl.astype(f32) + k2 * inner
    dr_ref[...] = dr
    drl = dr.astype(bf16)
    drl_ref[...] = drl
    dol_ref[...] = dot(drl, weight(0), NT)
    sbd[...] += jnp.sum(dyl.astype(f32), axis=0, keepdims=True)
    sg2[...] += jnp.sum(dc * n2, axis=0, keepdims=True)
    sb2[...] += jnp.sum(dc, axis=0, keepdims=True)
    sbo[...] += jnp.sum(drl.astype(f32), axis=0, keepdims=True)


def ffn_call(lens, idx, x, o, ct, parts, bo, g2, b2, bu, bd, n, cut, rb=256):
    s, d = x.shape
    ff = bu.shape[1]
    nu = ff // d
    wide = d + 2 * ff

    def row(w):
        return pl.BlockSpec((rb, w), lambda i: (i, 0))

    def acc(w):
        return pl.BlockSpec((1, w), lambda i: (0, 0))

    return pl.pallas_call(
        functools.partial(ffn_kernel, rb=rb, n=n, nu=nu, pieces=len(parts), cut=cut),
        grid=(s // rb,),
        in_specs=[smem(), smem(), row(d), row(d), row(d)]
        + [pl.BlockSpec(memory_space=pltpu.HBM)] * len(parts)
        + [whole((1, d)), whole((1, d)), whole((1, d)), whole((1, ff)), whole((1, d))],
        out_specs=[row(d), row(ff), row(ff), row(d), row(d), row(d), row(d), row(d)]
        + [acc(d), acc(ff), acc(d), acc(d), acc(d)],
        out_shape=[
            sds((s, d), bf16),
            sds((s, ff), bf16),
            sds((s, ff), bf16),
            sds((s, d), bf16),
            sds((s, d), bf16),
            sds((s, d), bf16),
            sds((s, d), f32),
            sds((s, d), f32),
            sds((1, d), f32),
            sds((1, ff), f32),
            sds((1, d), f32),
            sds((1, d), f32),
            sds((1, d), f32),
        ],
        scratch_shapes=[
            pltpu.VMEM((d // 48, 48, wide), bf16),
            pltpu.VMEM((ff, d), bf16),
            pltpu.SemaphoreType.DMA((64,)),
        ],
        compiler_params=params(60),
        cost_estimate=cost(37),
    )(lens, idx, x, o, ct, *parts, bo, g2, b2, bu, bd)


def wgrad_kernel(a_ref, b_ref, o_ref):
    b = b_ref[0] if len(b_ref.shape) == 3 else b_ref[...]
    o_ref[...] = dot(a_ref[...], b, TN).astype(o_ref.dtype)


def wgrad(a, b, ta, tb):
    s, m = a.shape
    if b.ndim == 3:
        n = b.shape[0] * b.shape[2]
        b_spec = pl.BlockSpec((1, s, b.shape[2]), lambda i, j: (j, 0, 0))
        tb = b.shape[2]
    else:
        n = b.shape[1]
        b_spec = pl.BlockSpec((s, tb), lambda i, j: (0, j))
    return pl.pallas_call(
        wgrad_kernel,
        grid=(m // ta, n // tb),
        in_specs=[pl.BlockSpec((s, ta), lambda i, j: (0, i)), b_spec],
        out_specs=pl.BlockSpec((ta, tb), lambda i, j: (i, j)),
        out_shape=sds((m, n), bf16),
        compiler_params=params(40),
        cost_estimate=cost(9),
    )(a, b)


def by_core(idx_ref, grad, keep, send, each):
    pairs = grad.reshape(grad.shape[0] // (2 * each), 2, each, grad.shape[1])
    first = idx_ref[3] == 0
    keep[...] = jnp.where(first, pairs[:, 0], pairs[:, 1]).astype(bf16)
    send[...] = jnp.where(first, pairs[:, 1], pairs[:, 0]).astype(bf16)


def down_kernel(idx_ref, g_ref, b_ref, keep, send, *, each, nu):
    grad = dot(g_ref[...], b_ref[...], TN)
    d = grad.shape[1]
    chips = grad.shape[0] // (2 * each * nu)
    parts = grad.reshape(chips, 2, nu, each, d)
    first = idx_ref[3] == 0
    for j in range(nu):
        cols = slice(j * d, (j + 1) * d)
        keep[:, :, cols] = jnp.where(first, parts[:, 0, j], parts[:, 1, j]).astype(bf16)
        send[:, :, cols] = jnp.where(first, parts[:, 1, j], parts[:, 0, j]).astype(bf16)


def down_grad(idx, g, dyl, n):
    s, ff = g.shape
    d = dyl.shape[1]
    each, nu = d // n, ff // d
    chips = n // 2 // nu
    spec = pl.BlockSpec((chips, each, ff), lambda i: (i, 0, 0))
    return pl.pallas_call(
        functools.partial(down_kernel, each=each, nu=nu),
        grid=(nu,),
        in_specs=[smem(), pl.BlockSpec((s, d), lambda i: (0, i)), whole((s, d))],
        out_specs=[spec, spec],
        out_shape=[sds((n // 2, each, ff), bf16)] * 2,
        compiler_params=params(24),
        cost_estimate=cost(9),
    )(idx, g, dyl)


def up_kernel(idx_ref, c_ref, du_ref, keep, send, *, each):
    by_core(idx_ref, dot(c_ref[...], du_ref[...], TN), keep, send, each)


def up_grad(idx, c, du, n):
    s, d = c.shape
    ff = du.shape[1]
    each = d // n
    spec = pl.BlockSpec((n // 2, each, d), lambda j: (0, 0, j))
    return pl.pallas_call(
        functools.partial(up_kernel, each=each),
        grid=(ff // d,),
        in_specs=[smem(), whole((s, d)), pl.BlockSpec((s, d), lambda j: (0, j))],
        out_specs=[spec, spec],
        out_shape=[sds((n // 2, each, ff), bf16)] * 2,
        compiler_params=params(24),
        cost_estimate=cost(9),
    )(idx, c, du)


def attention_grads_kernel(idx_ref, a_ref, dqkv_ref, o_ref, drl_ref, *rest, each):
    keep_a, send_a, keep_b, send_b = rest[-4:]
    j = pl.program_id(0)

    @pl.when(j < 2)
    def _():
        by_core(idx_ref, dot(a_ref[...], dqkv_ref[0], TN), keep_a, send_a, each)

    @pl.when(j == 2)
    def _():
        by_core(idx_ref, dot(a_ref[...], dqkv_ref[0], TN), keep_b, send_b, each)

    @pl.when(j == 3)
    def _():
        by_core(idx_ref, dot(o_ref[...], drl_ref[...], TN), keep_b, send_b, each)


def attention_grads(idx, a, dqkv, o, drl, n, deps=()):
    s, d = a.shape
    each = d // n
    spec_a = pl.BlockSpec((n // 2, each, d), lambda j: (0, 0, jnp.minimum(j, 1)))
    spec_b = pl.BlockSpec((n // 2, each, d), lambda j: (0, 0, jnp.maximum(j - 2, 0)))
    return pl.pallas_call(
        functools.partial(attention_grads_kernel, each=each),
        grid=(4,),
        in_specs=[
            smem(),
            whole((s, d)),
            pl.BlockSpec((1, s, d), lambda j: (jnp.minimum(j, 2), 0, 0)),
            whole((s, d)),
            whole((s, d)),
        ]
       ,
        out_specs=[spec_a, spec_a, spec_b, spec_b],
        out_shape=[sds((n // 2, each, 2 * d), bf16)] * 4,
        compiler_params=params(40),
        cost_estimate=cost(40),
    )(tie(idx, *deps), a, dqkv, o, drl)


def first_kernel(x_ref, dr_ref, dq_ref, w_ref, g_ref, sbo, sg2, sb2, sbd, sbu, *rest):
    gi_ref, out = rest[-2:]
    i = pl.program_id(0)
    d = x_ref.shape[1]
    quarter = w_ref.shape[3]

    @pl.when(i == 0)
    def _():
        out[:, : 5 * d] = jnp.zeros((1, 5 * d), f32)
        for k, ref in enumerate((sbo, sg2, sb2, sbd)):
            out[:, (5 + k) * d : (6 + k) * d] = ref[...]
        out[:, 9 * d :] = sbu[...]

    normal, inverse = norm_stats(x_ref[...].astype(f32))
    da = jnp.zeros(normal.shape, f32)
    for k in range(4):
        w = w_ref[k].reshape(d, quarter)
        at = k * quarter
        while at < min((k + 1) * quarter, 3 * d):
            j = at // d
            end = min((k + 1) * quarter, (j + 1) * d)
            part = dq_ref[j, :, at - j * d : end - j * d]
            da = da + dot(part, w[:, at - k * quarter : end - k * quarter], NT)
            out[:, 2 * d + at : 2 * d + end] += jnp.sum(part.astype(f32), axis=0, keepdims=True)
            at = end
    q1 = da * g_ref[...]
    inner = (
        q1 - jnp.mean(q1, axis=1, keepdims=True) - normal * jnp.mean(q1 * normal, axis=1, keepdims=True)
    )
    gi_ref[...] = dr_ref[...] + inverse * inner
    out[:, :d] += jnp.sum(da * normal, axis=0, keepdims=True)
    out[:, d : 2 * d] += jnp.sum(da, axis=0, keepdims=True)


def first_backward(x, dr, dqkv, w, gain, sums, deps=(), rb=256):
    s, d = x.shape

    def row(w):
        return pl.BlockSpec((rb, w), lambda i: (i, 0))

    wide = 9 * d + sums[-1].shape[1]
    return pl.pallas_call(
        first_kernel,
        grid=(s // rb,),
        in_specs=[row(d), row(d), pl.BlockSpec((3, rb, d), lambda i: (0, i, 0)), whole(w.shape), whole((1, d))]
        + [whole(t.shape) for t in sums]
       ,
        out_specs=[row(d), pl.BlockSpec((1, wide), lambda i: (0, 0))],
        out_shape=[sds((s, d), f32), sds((1, wide), f32)],
        compiler_params=params(40),
        cost_estimate=cost(10),
    )(x, dr, dqkv, w, tie(gain, *deps), *sums)


def scatter_sum(buf, n, order):
    lin = lax.axis_index(AXES)
    bits = n.bit_length() - 1
    rest = buf.shape[1:]
    buf = buf.reshape((2,) * bits + rest)
    left = list(range(bits - 1, -1, -1))
    for step, b in enumerate(order):
        axis = left.index(b)
        left.pop(axis)
        bit = (lin >> b) & 1
        send = lax.dynamic_index_in_dim(buf, 1 - bit, axis, keepdims=False)
        keep = lax.dynamic_index_in_dim(buf, bit, axis, keepdims=False)
        got = lax.ppermute(send, AXES, [(i, i ^ (1 << b)) for i in range(n)])
        buf = keep.astype(f32) + got.astype(f32)
        if step < bits - 1:
            buf = buf.astype(send.dtype)
    return buf


def permute(x, mask, n=32):
    return lax.ppermute(x, AXES, [(i, i ^ mask) for i in range(n)])


CORE, XBIT, YBIT = 1, 8, 16


def join(block, got):
    return jnp.concatenate([block[None], got[None]])


def gather_cores(mine, theirs, core):
    got = permute(theirs, CORE)
    return jnp.where(core == 0, jnp.concatenate([mine, got]), jnp.concatenate([got, mine]))


def gather_first(block, cut):
    a, b = block[..., :cut], block[..., cut:]
    return a, permute(a, XBIT), b, permute(b, YBIT)


def gather_second(a, b):
    parts = (a, permute(a, YBIT), b, permute(b, XBIT))
    return [t.reshape((8,) + t.shape[-2:]) for t in parts]


def fold_kernel(idx_ref, *refs, plan, joined):
    ins, outs = refs[: 2 * len(plan)], refs[-2 if joined else -2 * len(plan) :]
    lane = 0
    for k, (dim, which) in enumerate(plan):
        kept, got = ins[2 * k], ins[2 * k + 1]
        lead, wide = kept.shape[:-2], kept.shape[-1]
        for side in range(2):
            out = outs[side if joined else 2 * k + side]
            at = idx_ref[which] if side == 0 else 1 - idx_ref[which]
            for t in itertools.product(*[range(m) for m in lead[:dim] + lead[dim + 1 :]]):
                source = t[:dim] + (at,) + t[dim:]
                value = (kept[source].astype(f32) + got[source].astype(f32)).astype(bf16)
                if joined:
                    out[t + (slice(None), slice(lane, lane + wide))] = value
                else:
                    out[t] = value
        lane += wide


def fold(idx, pairs, plan, us, deps=(), joined=False):
    stepped = pairs[0][0].ndim > 3 and not joined
    args, in_specs, out_specs, out_shape, total = [], [], [], [], 0
    for (kept, got), (dim, _) in zip(pairs, plan):
        lead, (each, wide) = kept.shape[:-2], kept.shape[-2:]
        left = lead[:dim] + lead[dim + 1 :]
        total += wide
        args += [kept, got]

        def spec(shape):
            if not stepped:
                return pl.BlockSpec()
            m = len(shape)
            return pl.BlockSpec(shape[:-3] + (1,) + shape[-2:], lambda i: (0,) * (m - 3) + (i, 0, 0))

        in_specs += [spec(kept.shape)] * 2
        out_specs += [spec(left + (each, wide))] * 2
        out_shape += [sds(left + (each, wide), bf16)] * 2
    if joined:
        out_specs, out_shape = [pl.BlockSpec()] * 2, [sds(left + (each, total), bf16)] * 2
    grid = {"grid": (pairs[0][0].shape[-3],)} if stepped else {}
    return pl.pallas_call(
        functools.partial(fold_kernel, plan=plan, joined=joined),
        in_specs=[smem()] + in_specs,
        out_specs=out_specs,
        out_shape=out_shape,
        compiler_params=params(24),
        cost_estimate=cost(us),
        **grid,
    )(tie(idx, *deps), *args)


def last_kernel(kept, got, *refs, cuts):
    outs = refs[-len(cuts) :]
    total = kept[...].astype(f32) + got[...].astype(f32)
    each = total.shape[0]
    at = 0
    for out, (rows, wide) in zip(outs, cuts):
        for j in range(rows):
            out[j * each : (j + 1) * each, :] = total[:, at : at + wide]
            at += wide


def fold_last(kept, got, cuts, deps=()):
    each = kept.shape[0]
    return pl.pallas_call(
        functools.partial(last_kernel, cuts=cuts),
        in_specs=[pl.BlockSpec()] * 2,
        out_specs=[pl.BlockSpec()] * len(cuts),
        out_shape=[sds((rows * each, wide), f32) for rows, wide in cuts],
        compiler_params=params(24),
        cost_estimate=cost(1),
    )(tie(kept, *deps), got)


def body(
    n,
    dp,
    layer_input,
    lengths,
    ln1_gain,
    ln1_bias,
    w_qkv,
    b_qkv,
    w_out,
    b_out,
    ln2_gain,
    ln2_bias,
    w_up,
    b_up,
    w_down,
    b_down,
    cotangent,
):
    s, d = layer_input.shape[1:]
    x = layer_input.reshape(s, d)
    ct = cotangent.reshape(s, d)
    e, ff = w_qkv.shape[1], w_up.shape[1]
    each = d // n
    nu = ff // d
    fast = n == 32 and dp == 4
    lin = lax.axis_index(AXES)
    idx = jnp.stack([(lin >> 3) & 1, (lin >> 4) & 1, (lin >> 1) & 3, lin & 1, (lin >> 1) & 1, (lin >> 2) & 1]).astype(jnp.int32)
    vectors = (ln1_gain, ln1_bias, b_out, ln2_gain, ln2_bias, b_down, b_qkv, b_up)
    layout = vector_layout(each, d, e, ff)
    mine, theirs = prepare(w_qkv, vectors, layout)
    mine_rest, theirs_rest = prepare_rest(tie(w_out, mine), w_up, w_down)
    cut_q, cut_r = (e + 256) // 4, 128 * (-(-(d + 2 * ff) // 512))
    if fast:
        core = lin & 1
        q = gather_cores(mine, theirs, core)
        r = gather_cores(mine_rest, theirs_rest, core)
        q = join(q, permute(q, 4))
        q = tie(q, r)
        q = join(q, permute(q, 2))
        r = tie(r, q)
        a0, a1, b0, b1 = gather_first(q, cut_q)
        got_r = permute(r, 4)
        qa, qb = join(a0, a1), join(b0, b1)
        parts = gather_second(qa, qb)
        r = join(r, tie(got_r, qa, qb))
        parts[1], parts[3] = tie(parts[1], r), tie(parts[3], r)
        parts += [permute(t, CORE) for t in parts]
        ra, rb = r[..., :cut_r], r[..., cut_r:]
        ra, rb = join(ra, permute(ra, 2)), join(rb, permute(rb, 2))
        got_ra, got_rb = permute(ra, XBIT), permute(rb, YBIT)
        x_in = tie(x, ra, rb)
    else:
        def gathered(own, other):
            both = jnp.where((lin & 1) == 0, jnp.concatenate([own, other], 1), jnp.concatenate([other, own], 1))
            return lax.all_gather(both, AXES, axis=0, tiled=True)

        x_in = x
        parts = [gathered(mine, theirs)]
        rest = [gathered(mine_rest, theirs_rest).reshape(d // 48, 48, d + 2 * ff)]
    a, qkv, wq, g1, b1, bo, g2, b2, bd, bq, bu = qkv_call(idx, x_in, parts, n, layout, e)
    if fast:
        ra, rb = join(ra, tie(got_ra, qkv)), join(rb, tie(got_rb, qkv))
        ra, ga, rb, gb = gather_second(ra, rb)
        o, rz, *kept = attention_forward(lengths, qkv, 0, H // 2, deps=(ra, rb))
        other_ra, other_rb = permute(ra, CORE), permute(rb, CORE)
        ga, gb = tie(ga, o, other_ra, other_rb), tie(gb, o, other_ra, other_rb)
        rest = [ra, ga, rb, gb, other_ra, permute(ga, CORE), other_rb, permute(gb, CORE)]
    else:
        o, rz, *kept = attention_forward(lengths, qkv, 0, H // 2)
    (y, g, du, c, dyl, drl, dr, dol, sbd, sbu, sg2, sb2, sbo) = ffn_call(
        lengths, idx, x, o, ct, rest, bo, g2, b2, bu, bd, n, cut_r
    )
    sums = (sbo, sg2, sb2, sbd, sbu)
    if fast:
        core_x, core_y, deep_0, deep_1 = 0, 1, 4, 5

        def chips(t):
            return t.reshape((2, 2, 4) + t.shape[1:])

        def deep(t):
            return t.reshape((2, 2) + t.shape[1:])

        keep_d, send_d = down_grad(idx, g, dyl, n)
        got_d = permute(send_d, CORE)
        keep_u, send_u = up_grad(idx, c, du, n)
        got_u = permute(send_u, CORE)
        kd, sd = fold(idx, [(chips(keep_d), chips(got_d))], [(1, core_x)], 2.5, deps=(keep_u,))
        rd = permute(sd, XBIT)
        ku, su = fold(idx, [(chips(keep_u), chips(got_u))], [(0, core_y)], 2.5, deps=(kd,))
        ru = permute(su, YBIT)
        dqkv = attention_backward(lengths, qkv, o, rz, dol, kept, deps=(ku,))
        kd, sd, ku, su = fold(idx, [(kd, rd), (ku, ru)], [(0, core_y), (0, core_x)], 2.5, deps=(dqkv,))
        rd, ru = permute(sd, YBIT), permute(su, XBIT)
        ka, sa, kb, sb = attention_grads(idx, a, dqkv, o, drl, n, deps=(kd,))
        ga, gb = permute(sa, CORE), permute(sb, CORE)
        pairs = [(deep(kd), deep(rd)), (deep(ku), deep(ru))]
        kw, sw = fold(idx, pairs, [(1, deep_0)] * 2, 30, deps=(ka,), joined=True)
        rw = permute(sw, 2)
        pairs = [(chips(ka), chips(ga)), (chips(kb), chips(gb))]
        ka, sa, kb, sb = fold(idx, pairs, [(1, core_x), (0, core_y)], 2.5, deps=(kw,))
        ra, rb = permute(sa, XBIT), permute(sb, YBIT)
        grad_input, total = first_backward(x, dr, dqkv, wq, g1, sums, deps=(ka,))
        got = permute(total, CORE)
        kw, sw = fold(idx, [(kw, rw)], [(0, deep_1)], 1, deps=(total,))
        rw = permute(sw, 4)
        ka, sa, kb, sb = fold(idx, [(ka, ra), (kb, rb)], [(0, core_y), (0, core_x)], 1, deps=(kw,))
        ra, rb = permute(sa, YBIT), permute(sb, XBIT)
        total = total + tie(got, ka)
        got = [permute(total, mask) for mask in (XBIT, YBIT, XBIT | YBIT)]
        grad_down, grad_up = fold_last(kw, rw, [(nu, d), (1, ff)], deps=(ra, rb))
        got = lax.optimization_barrier((*got, grad_up))
        total = total + got[0] + got[1] + got[2]
        pairs = [(deep(ka), deep(ra)), (deep(kb), deep(rb))]
        kq, sq = fold(idx, pairs, [(1, deep_0)] * 2, 1, deps=(grad_up, total), joined=True)
        rq = permute(sq, 2)
        got = [permute(total, mask) for mask in (2, 4, 6)]
        kq, sq = fold(idx, [(kq, rq)], [(0, deep_1)], 1)
        rq = permute(sq, 4)
        got = lax.optimization_barrier((*got, kq))
        total = total + got[0] + got[1] + got[2]
        grad_qkv, grad_out = fold_last(kq, rq, [(1, e), (1, d)])
    else:
        order = list(range(n.bit_length() - 1))
        grad_down = scatter_sum(wgrad(g, dyl, d, d).reshape(n, ff // n, d), n, order)
        grad_up = scatter_sum(wgrad(c, du, d, d).reshape(n, each, ff), n, order)
        grad_out = scatter_sum(wgrad(o, drl, d, d).reshape(n, each, d), n, order)
        dqkv = attention_backward(lengths, qkv, o, rz, dol, kept)
        grad_qkv = scatter_sum(wgrad(a, dqkv, d, d).reshape(n, each, e), n, order)
        grad_input, total = first_backward(x, dr, dqkv, wq, g1, sums)
        total = lax.psum(total, AXES)
    shares, at = [], 0
    for size in (each, each, 3 * each, each, each, each, each, nu * each):
        shares.append(lax.dynamic_slice_in_dim(total[0], at + lin * size, size))
        at += n * size
    gs1, gb1, gbq, gbo, gs2, gb2, gbd, gbu = shares
    return (
        y.reshape(layer_input.shape),
        grad_input.reshape(layer_input.shape),
        gs1,
        gb1,
        grad_qkv,
        gbq,
        grad_out,
        gbo,
        gs2,
        gb2,
        grad_up,
        gbu,
        grad_down,
        gbd,
    )


def solution(mesh):
    split = P(AXES)
    wide = P(AXES, None)
    cube = P(AXES, None, None)
    in_specs = (
        cube, split, split, split, wide, split, wide, split, split, split, wide, split, wide, split, cube,
    )
    out_specs = (
        cube, cube, split, split, wide, split, wide, split, split, split, wide, split, wide, split,
    )
    n = mesh.shape["dp"] * mesh.shape["fsdp"]
    return jax.shard_map(
        functools.partial(body, n, mesh.shape["dp"]),
        mesh=mesh,
        in_specs=in_specs,
        out_specs=out_specs,
        check_vma=False,
    )
```

```python
import functools
import itertools
import math

import jax
import jax.numpy as jnp
from jax import lax
from jax.experimental import pallas as pl
from jax.experimental.pallas import tpu as pltpu
from jax.sharding import PartitionSpec as P

H = 12
HD = 64
AXES = ("dp", "fsdp")
NORM_EPS = 1e-05
LOG2E = math.log2(math.e)
NT = (((1,), (1,)), ((), ()))
NN = (((1,), (0,)), ((), ()))
TN = (((0,), (0,)), ((), ()))
bf16 = jnp.bfloat16
f32 = jnp.float32
MIB = 2**20


def dot(a, b, dims):
    return lax.dot_general(a, b, dims, preferred_element_type=f32)


def whole(shape):
    return pl.BlockSpec(shape, lambda *i: (0,) * len(shape), pipeline_mode=pl.Buffered(1))


def smem():
    return pl.BlockSpec(memory_space=pltpu.SMEM)


def tie(value, *others):
    return lax.optimization_barrier((value, *others))[0]


def params(mib):
    return pltpu.CompilerParams(vmem_limit_bytes=mib * MIB)


def sds(shape, dtype):
    return jax.ShapeDtypeStruct(shape, dtype)


def cost(us):
    return pl.CostEstimate(flops=int(us * 1e9), bytes_accessed=0, transcendentals=0)


def norm_stats(values):
    mean = jnp.mean(values, axis=1, keepdims=True)
    centred = values - mean
    inverse = lax.rsqrt(jnp.mean(centred * centred, axis=1, keepdims=True) + NORM_EPS)
    return centred * inverse, inverse


def vector_layout(each, d, e, ff):
    return [(1, each * k, each) for k in range(6)] + [(0, 0, each * (e // d)), (0, 128, each * (ff // d))]


def by_half(ref, core, own, other):
    half = own.shape[1]
    own[...] = ref[:, pl.ds(pl.multiple_of(core * half, 128), half)]
    other[...] = ref[:, pl.ds(pl.multiple_of((1 - core) * half, 128), half)]


def fetch(pairs, sems):
    copies = [pltpu.make_async_copy(ref, to, sems.at[k]) for k, (ref, to) in enumerate(pairs)]
    for copy in copies:
        copy.start()
    return copies


def prepare_kernel(*refs, layout):
    ins, (own, other), (both, low, sems), small = refs[:9], refs[9:11], refs[11:14], refs[14:]
    e = ins[0].shape[1]
    copies = fetch(list(zip(ins, (both.at[:, :e], *small))), sems)
    low[...] = jnp.zeros_like(low)
    for copy in copies:
        copy.wait()
    for k, (row, lane, size) in enumerate(layout):
        low[row : row + 1, lane : lane + size] = small[k][...].astype(f32)
    both[:, e:] = low[...].astype(bf16)
    by_half(both, lax.axis_index("fsdp") & 1, own, other)


def prepare(wq, vectors, layout):
    each, e = wq.shape
    return pl.pallas_call(
        functools.partial(prepare_kernel, layout=layout),
        in_specs=[pl.BlockSpec(memory_space=pltpu.HBM)] * 9,
        out_shape=[sds((each, (e + 256) // 2), bf16)] * 2,
        scratch_shapes=[
            pltpu.VMEM((each, e + 256), bf16),
            pltpu.VMEM((each, 256), f32),
            pltpu.SemaphoreType.DMA((9,)),
        ]
        + [pltpu.VMEM((1, v.shape[0]), bf16) for v in vectors],
        compiler_params=params(60),
        cost_estimate=cost(2),
    )(wq, *[v.reshape(1, -1) for v in vectors])


def prepare_rest_kernel(wo, wu, wd, own, other, rest, down, sems, *, nu):
    each, d = wo.shape
    ff = wu.shape[1]
    copies = fetch([(wo, rest.at[:, :d]), (wu, rest.at[:, d : d + ff]), (wd, down)], sems)
    for copy in copies:
        copy.wait()
    for j in range(nu):
        rest[:, d + ff + j * d : d + ff + (j + 1) * d] = down[j * each : (j + 1) * each, :]
    by_half(rest, lax.axis_index("fsdp") & 1, own, other)


def prepare_rest(wo, wu, wd):
    each, d = wo.shape
    ff = wu.shape[1]
    wide = d + 2 * ff
    return pl.pallas_call(
        functools.partial(prepare_rest_kernel, nu=ff // d),
        in_specs=[pl.BlockSpec(memory_space=pltpu.HBM)] * 3,
        out_shape=[sds((each, wide // 2), bf16)] * 2,
        scratch_shapes=[
            pltpu.VMEM((each, wide), bf16),
            pltpu.VMEM(wd.shape, bf16),
            pltpu.SemaphoreType.DMA((3,)),
        ],
        compiler_params=params(60),
        cost_estimate=cost(2),
    )(wo, wu, wd)


def gathered_chip(idx_ref, k, at):
    x, y, z = (idx_ref[i] for i in range(3))
    first, deep = at // 4, z ^ ((at // 2) % 2 + 2 * (at % 2))
    second = k % 2
    if (k // 2) % 2 == 0:
        return ((y ^ second) * 2 + (x ^ first)) * 4 + deep
    return ((y ^ first) * 2 + (x ^ second)) * 4 + deep


def qkv_kernel(idx_ref, x_ref, *rest, n, each, layout, pieces):
    parts, (a_ref, o_ref, w_ref), vecs, low = rest[:pieces], rest[pieces : pieces + 3], rest[pieces + 3 : -1], rest[-1]
    quarter = w_ref.shape[3]
    e = o_ref.shape[1]

    @pl.when(pl.program_id(0) == 0)
    def _():
        if pieces == 1:
            for k in range(4):
                w_ref[k] = parts[0][:, k * quarter : (k + 1) * quarter].reshape(w_ref.shape[1:])
        else:
            core = idx_ref[3]
            for k, part in enumerate(parts):
                quarter_at = 2 * (core if k < 4 else 1 - core) + (k // 2) % 2
                for at in range(8):
                    w_ref[quarter_at, gathered_chip(idx_ref, k, at)] = part[at]
        low[...] = w_ref[3, :, :, quarter - 256 :].astype(f32)
        for dev in range(n):
            for out, (row, lane, size) in zip(vecs, layout):
                at = dev * each + row
                out[:, dev * size : (dev + 1) * size] = low[at // 48, at % 48 : at % 48 + 1, lane : lane + size]

    normal, _ = norm_stats(x_ref[...].astype(f32))
    a = (normal * vecs[0][...] + vecs[1][...]).astype(bf16)
    a_ref[...] = a
    for k in range(4):
        cols = slice(k * quarter, min((k + 1) * quarter, e))
        wide = cols.stop - cols.start
        w = w_ref[k].reshape(a.shape[1], quarter)
        o_ref[:, cols] = (dot(a, w[:, :wide], NN) + vecs[6][:, cols]).astype(bf16)


def qkv_call(idx, x, parts, n, layout, e, rb=512):
    s, d = x.shape
    each = d // n
    quarter = (e + 256) // 4
    sizes = [n * size for _, _, size in layout]
    return pl.pallas_call(
        functools.partial(qkv_kernel, n=n, each=each, layout=layout, pieces=len(parts)),
        grid=(s // rb,),
        in_specs=[smem(), pl.BlockSpec((rb, d), lambda i: (i, 0))] + [whole(p.shape) for p in parts],
        out_specs=[
            pl.BlockSpec((rb, d), lambda i: (i, 0)),
            pl.BlockSpec((rb, e), lambda i: (i, 0)),
            whole((4, d // 48, 48, quarter)),
        ]
        + [whole((1, size)) for size in sizes],
        out_shape=[sds((s, d), bf16), sds((s, e), bf16), sds((4, d // 48, 48, quarter), bf16)]
        + [sds((1, size), f32) for size in sizes],
        scratch_shapes=[pltpu.VMEM((d // 48, 48, 256), f32)],
        compiler_params=params(60),
        cost_estimate=cost(9),
    )(idx, x, *parts)


def fwd_kernel(len_ref, q_ref, k_ref, v_ref, *refs, qb, nq, rc):
    s_ref, z_ref, m_ref = refs[-3:]
    o_ref, rz_ref, *kept = refs[-5 - 2 * nq : -3]
    p_refs, a_refs = kept[:nq], kept[nq:]
    n = len_ref[0]
    lane = lax.broadcasted_iota(jnp.int32, (1, 128), 1)

    def emit(blocks):
        units = [(i, h) for i in blocks for h in range(2)]

        def scores(t):
            i, h = units[t]
            q = q_ref[i * qb : (i + 1) * qb, :] * jnp.asarray(HD**-0.5, bf16)
            mine = (lane < HD) if h == 0 else (lane >= HD)
            nk = (i + 1) * qb
            s_ref[t % 2, :, :nk] = dot(jnp.where(mine, q, jnp.zeros_like(q)), k_ref[:nk, :], NT)

        def weights(t):
            i, h = units[t]
            for r0 in range(0, qb, rc):
                rr = slice(r0, r0 + rc)
                row = lax.broadcasted_iota(jnp.int32, (rc, qb), 0) + r0
                col = lax.broadcasted_iota(jnp.int32, (rc, qb), 1)
                mask = (col <= row) & (col < n - i * qb)
                top = jnp.where(mask, jnp.abs(s_ref[t % 2, rr, i * qb : (i + 1) * qb]), 0.0)
                for j in range(i):
                    top = jnp.maximum(top, jnp.abs(s_ref[t % 2, rr, j * qb : (j + 1) * qb]))
                top = jnp.max(top, axis=1, keepdims=True)
                top = jnp.sqrt(top * top + 1.0)
                total = jnp.zeros((rc, qb), f32)
                for j in range(i + 1):
                    cols = slice(j * qb, (j + 1) * qb)
                    s = s_ref[t % 2, rr, cols]
                    square = s * s + 1.0
                    inv = lax.rsqrt(square)
                    e = jnp.exp(square * inv - top)
                    if j == i:
                        e = jnp.where(mask, e, 0.0)
                    total = total + e
                    p_refs[i][h, rr, cols] = (s * inv * e).astype(bf16)
                    a_refs[i][h, rr, cols] = ((1.0 - inv * inv * (1.0 - inv)) * e).astype(bf16)
                rz = 1.0 / jnp.sum(total, axis=1, keepdims=True)
                z_ref[t % 2, rr, :] = jnp.broadcast_to(rz, (rc, 128))

        def mix(t):
            i, h = units[t]
            rows = slice(i * qb, (i + 1) * qb)
            rz = z_ref[t % 2]
            mixed = dot(p_refs[i][h], v_ref[: (i + 1) * qb, :], NN) * rz
            if h == 0:
                m_ref[...] = mixed
                rz_ref[rows, :] = rz
            else:
                o_ref[rows, :] = jnp.where(lane < HD, m_ref[...], mixed).astype(bf16)
                rz_ref[rows, :] = jnp.where(lane < HD, rz_ref[rows, :], rz)

        scores(0)
        for t in range(len(units)):
            if t + 1 < len(units):
                scores(t + 1)
            weights(t)
            mix(t)

    by_blocks(n, qb, nq, emit, lambda rows: dead_block(rows, (o_ref, rz_ref)))


def dead_block(rows, refs):
    for ref in refs:
        ref[rows, :] = jnp.zeros((rows.stop - rows.start, ref.shape[1]), ref.dtype)


def by_blocks(n, qb, nq, emit, dead):
    @pl.when(n > (nq - 1) * qb)
    def _():
        emit(list(range(nq)))

    @pl.when(n <= (nq - 1) * qb)
    def _():
        for i in range(nq):

            @pl.when(n > i * qb)
            def _():
                emit([i])

            @pl.when(n <= i * qb)
            def _():
                dead(slice(i * qb, (i + 1) * qb))


def attention_forward(lens, qkv, first, groups, before=(), deps=(), qb=256):
    s = qkv.shape[0]
    nq = s // qb
    hp = H // 2

    def columns(off):
        return pl.BlockSpec((s, 128), lambda g: (0, first + g + off))

    kept_shape = [sds((H, qb, (i + 1) * qb), bf16) for i in range(nq)]
    kept_spec = [pl.BlockSpec((2, qb, (i + 1) * qb), lambda g: (first + g, 0, 0)) for i in range(nq)]
    return pl.pallas_call(
        functools.partial(fwd_kernel, qb=qb, nq=nq, rc=32),
        grid=(groups,),
        in_specs=[smem(), columns(0), columns(hp), columns(2 * hp)] + [pl.BlockSpec(memory_space=pl.ANY)] * len(before),
        out_specs=[columns(0)] * 2 + kept_spec * 2,
        out_shape=[sds((s, H * HD), bf16), sds((s, H * HD), f32)] + kept_shape * 2,
        input_output_aliases={4 + k: k for k in range(len(before))},
        scratch_shapes=[
            pltpu.VMEM((2, qb, s), f32),
            pltpu.VMEM((2, qb, 128), f32),
            pltpu.VMEM((qb, 128), f32),
        ],
        compiler_params=params(60),
        cost_estimate=cost(7.5 * groups),
    )(tie(lens, *deps), qkv, qkv, qkv, *before)


def bwd_kernel(len_ref, q_ref, k_ref, v_ref, o_ref, rz_ref, d_ref, *rest, qb, nq, rc):
    p_refs, a_refs = rest[:nq], rest[nq : 2 * nq]
    out, dk_ref, dv_ref, dp_ref, ds_ref, low_ref, total_ref, low_t, q_t, dq_ref = rest[-10:]
    n = len_ref[0]
    scale = HD ** (-0.5)
    lane = lax.broadcasted_iota(jnp.int32, (1, 128), 1)
    dk_ref[...] = jnp.zeros_like(dk_ref)
    dv_ref[...] = jnp.zeros_like(dv_ref)

    def emit(blocks):
        units = [(i, h) for i in blocks for h in range(2)]

        def weight_grads(t):
            i, h = units[t]
            nk = (i + 1) * qb
            mine = (lane < HD) if h == 0 else (lane >= HD)
            if h == 0:
                rows = slice(i * qb, (i + 1) * qb)
                grad = d_ref[rows, :] * rz_ref[rows, :]
                low = grad.astype(bf16)
                along = grad * o_ref[rows, :].astype(f32)
                low_ref[i % 2] = low
                low_t[i % 2] = low.T
                q_t[i % 2] = q_ref[rows, :].T
                for k in range(2):
                    half = jnp.where((lane < HD) if k == 0 else (lane >= HD), along, 0.0)
                    total_ref[i % 2, k] = jnp.broadcast_to(jnp.sum(half, axis=1, keepdims=True), (qb, 128))
            low = low_ref[i % 2]
            dp_ref[t % 2, :, :nk] = dot(jnp.where(mine, low, jnp.zeros_like(low)), v_ref[:nk, :], NT)

        def score_grads(t):
            i, h = units[t]
            for r0 in range(0, qb, rc):
                rr = slice(r0, r0 + rc)
                total = jnp.concatenate([total_ref[i % 2, h, rr, :]] * (qb // 128), axis=1)
                for j in range(i + 1):
                    cols = slice(j * qb, (j + 1) * qb)
                    first = a_refs[i][h, rr, cols].astype(f32) * dp_ref[t % 2, rr, cols]
                    ds_ref[t % 2, rr, cols] = (first - p_refs[i][h, rr, cols].astype(f32) * total).astype(bf16)

        def grads(t):
            i, h = units[t]
            nk = (i + 1) * qb
            part = slice(h * HD, (h + 1) * HD)
            ds = ds_ref[t % 2, :, :nk]
            dq = dot(ds, k_ref[:nk, :], NN)
            if h == 0:
                dq_ref[...] = dq
            else:
                out[0, i * qb : nk, :] = (jnp.where(lane < HD, dq_ref[...], dq) * scale).astype(bf16)
            dv_ref[part, :nk] += dot(low_t[i % 2, part, :], p_refs[i][h], NN)
            dk_ref[part, :nk] += dot(q_t[i % 2, part, :], ds, NN)

        weight_grads(0)
        for t in range(len(units)):
            if t + 1 < len(units):
                weight_grads(t + 1)
            score_grads(t)
            grads(t)

    by_blocks(n, qb, nq, emit, lambda rows: dead_block(rows, (out.at[0],)))
    out[1] = (dk_ref[...] * scale).T.astype(bf16)
    out[2] = dv_ref[...].T.astype(bf16)


def attention_backward(lens, qkv, o, rz, dol, kept, deps=(), qb=256, first=0, groups=H // 2):
    s = qkv.shape[0]
    nq = s // qb
    hp = H // 2

    def columns(off):
        return pl.BlockSpec((s, 128), lambda g: (0, first + g + off))

    kept_spec = [pl.BlockSpec((2, qb, (i + 1) * qb), lambda g: (first + g, 0, 0)) for i in range(nq)]
    return pl.pallas_call(
        functools.partial(bwd_kernel, qb=qb, nq=nq, rc=64),
        grid=(groups,),
        in_specs=[smem(), columns(0), columns(hp), columns(2 * hp)] + [columns(0)] * 3 + kept_spec * 2,
        out_specs=pl.BlockSpec((3, s, 128), lambda g: (0, 0, g)),
        out_shape=sds((3, s, 128 * groups), bf16),
        scratch_shapes=[pltpu.VMEM((128, s), f32)] * 2
        + [
            pltpu.VMEM((2, qb, s), f32),
            pltpu.VMEM((2, qb, s), bf16),
            pltpu.VMEM((2, qb, 128), bf16),
            pltpu.VMEM((2, 2, qb, 128), f32),
            pltpu.VMEM((2, 128, qb), bf16),
            pltpu.VMEM((2, 128, qb), bf16),
            pltpu.VMEM((qb, 128), f32),
        ],
        compiler_params=params(40),
        cost_estimate=cost(26),
    )(tie(lens, *deps), qkv, qkv, qkv, o, rz, dol, *kept)


def ffn_kernel(len_ref, idx_ref, x_ref, o_ref, ct_ref, *rest, rb, n, nu, pieces, cut):
    parts, rest = rest[:pieces], rest[pieces:]
    bo_ref, g2_ref, b2_ref, bu_ref, bd_ref = rest[:5]
    (y_ref, g_ref, du_ref, c_ref, dyl_ref, drl_ref, dr_ref, dol_ref) = rest[5:13]
    sbd, sbu, sg2, sb2, sbo, w_ref, wd, sems = rest[13:]
    i = pl.program_id(0)
    d = x_ref.shape[1]
    each = d // n
    chips, rows, wide = w_ref.shape

    def weight(at):
        return w_ref[:, :, at : at + d].reshape(d, d)

    core = idx_ref[3]

    def copies(k):
        if pieces == 1:
            return [pltpu.make_async_copy(parts[0], w_ref, sems.at[0])]
        who, later, half = core if k < 4 else 1 - core, (k // 2) % 2, wide // 2
        lane = pl.multiple_of(who * half + later * cut, 128)
        size = half - cut if later else cut
        return [
            pltpu.make_async_copy(
                parts[k].at[at], w_ref.at[gathered_chip(idx_ref, k, at), :, pl.ds(lane, size)], sems.at[k * 8 + at]
            )
            for at in range(8)
        ]

    def wait(which):
        for k in which:
            for copy in copies(k):
                copy.wait()

    order = (0, 1, 4, 5, 2, 3, 6, 7) if pieces > 1 else (0,)

    @pl.when(i == 0)
    def _():
        for k in order:
            for copy in copies(k):
                copy.start()
        for s in (sbd, sbu, sg2, sb2, sbo):
            s[...] = jnp.zeros_like(s)
        wait(order[:4])

    live = (lax.broadcasted_iota(jnp.int32, (rb, 1), 0) + i * rb) < len_ref[0]
    r = x_ref[...].astype(f32) + dot(o_ref[...], weight(0), NN) + bo_ref[...]
    n2, k2 = norm_stats(r)
    g2 = g2_ref[...]
    c = (n2 * g2 + b2_ref[...]).astype(bf16)
    c_ref[...] = c
    dyl = jnp.where(live, ct_ref[...], jnp.zeros((), bf16))
    dyl_ref[...] = dyl
    y = r + bd_ref[...]
    dc = jnp.zeros_like(r)

    @pl.when(i == 0)
    def _():
        wait(order[4:])
        for dev in range(n):
            for j in range(nu):
                at = (dev * nu + j) * each
                row = dev * each
                lane = (1 + nu + j) * d
                wd[at : at + each, :] = w_ref[row // rows, row % rows : row % rows + each, lane : lane + d]

    k0 = math.sqrt(2 / math.pi)
    for j in range(nu):
        cols = slice(j * d, (j + 1) * d)
        wu = weight((1 + j) * d)
        wdj = wd[cols, :]
        u = dot(c, wu, NN) + bu_ref[:, cols]
        t = dot(dyl, wdj, NT)
        u2 = u * u
        hp = 0.5 + 0.5 * jnp.tanh(u * (k0 + (k0 * 0.044715) * u2))
        g = (u * hp).astype(bf16)
        slope = hp + u * (2.0 * hp * (1.0 - hp)) * (k0 + (3 * k0 * 0.044715) * u2)
        du = (t * slope).astype(bf16)
        g_ref[:, cols] = g
        du_ref[:, cols] = du
        y = y + dot(g, wdj, NN)
        dc = dc + dot(du, wu, NT)
        sbu[:, cols] += jnp.sum(du.astype(f32), axis=0, keepdims=True)
    y_ref[...] = jnp.where(live, y, 0.0).astype(bf16)
    q2 = dc * g2
    inner = q2 - jnp.mean(q2, axis=1, keepdims=True) - n2 * jnp.mean(q2 * n2, axis=1, keepdims=True)
    dr = dyl.astype(f32) + k2 * inner
    dr_ref[...] = dr
    drl = dr.astype(bf16)
    drl_ref[...] = drl
    dol_ref[...] = dot(drl, weight(0), NT)
    sbd[...] += jnp.sum(dyl.astype(f32), axis=0, keepdims=True)
    sg2[...] += jnp.sum(dc * n2, axis=0, keepdims=True)
    sb2[...] += jnp.sum(dc, axis=0, keepdims=True)
    sbo[...] += jnp.sum(drl.astype(f32), axis=0, keepdims=True)


def ffn_call(lens, idx, x, o, ct, parts, bo, g2, b2, bu, bd, n, cut, rb=256):
    s, d = x.shape
    ff = bu.shape[1]
    nu = ff // d
    wide = d + 2 * ff

    def row(w):
        return pl.BlockSpec((rb, w), lambda i: (i, 0))

    def acc(w):
        return pl.BlockSpec((1, w), lambda i: (0, 0))

    return pl.pallas_call(
        functools.partial(ffn_kernel, rb=rb, n=n, nu=nu, pieces=len(parts), cut=cut),
        grid=(s // rb,),
        in_specs=[smem(), smem(), row(d), row(d), row(d)]
        + [pl.BlockSpec(memory_space=pltpu.HBM)] * len(parts)
        + [whole((1, d)), whole((1, d)), whole((1, d)), whole((1, ff)), whole((1, d))],
        out_specs=[row(d), row(ff), row(ff), row(d), row(d), row(d), row(d), row(d)]
        + [acc(d), acc(ff), acc(d), acc(d), acc(d)],
        out_shape=[
            sds((s, d), bf16),
            sds((s, ff), bf16),
            sds((s, ff), bf16),
            sds((s, d), bf16),
            sds((s, d), bf16),
            sds((s, d), bf16),
            sds((s, d), f32),
            sds((s, d), f32),
            sds((1, d), f32),
            sds((1, ff), f32),
            sds((1, d), f32),
            sds((1, d), f32),
            sds((1, d), f32),
        ],
        scratch_shapes=[
            pltpu.VMEM((d // 48, 48, wide), bf16),
            pltpu.VMEM((ff, d), bf16),
            pltpu.SemaphoreType.DMA((64,)),
        ],
        compiler_params=params(60),
        cost_estimate=cost(37),
    )(lens, idx, x, o, ct, *parts, bo, g2, b2, bu, bd)


def wgrad_kernel(a_ref, b_ref, o_ref):
    b = b_ref[0] if len(b_ref.shape) == 3 else b_ref[...]
    o_ref[...] = dot(a_ref[...], b, TN).astype(o_ref.dtype)


def wgrad(a, b, ta, tb):
    s, m = a.shape
    if b.ndim == 3:
        n = b.shape[0] * b.shape[2]
        b_spec = pl.BlockSpec((1, s, b.shape[2]), lambda i, j: (j, 0, 0))
        tb = b.shape[2]
    else:
        n = b.shape[1]
        b_spec = pl.BlockSpec((s, tb), lambda i, j: (0, j))
    return pl.pallas_call(
        wgrad_kernel,
        grid=(m // ta, n // tb),
        in_specs=[pl.BlockSpec((s, ta), lambda i, j: (0, i)), b_spec],
        out_specs=pl.BlockSpec((ta, tb), lambda i, j: (i, j)),
        out_shape=sds((m, n), bf16),
        compiler_params=params(40),
        cost_estimate=cost(9),
    )(a, b)


def by_core(idx_ref, grad, keep, send, each):
    pairs = grad.reshape(grad.shape[0] // (2 * each), 2, each, grad.shape[1])
    first = idx_ref[3] == 0
    keep[...] = jnp.where(first, pairs[:, 0], pairs[:, 1]).astype(bf16)
    send[...] = jnp.where(first, pairs[:, 1], pairs[:, 0]).astype(bf16)


def down_kernel(idx_ref, g_ref, b_ref, keep, send, *, each, nu):
    grad = dot(g_ref[...], b_ref[...], TN)
    d = grad.shape[1]
    chips = grad.shape[0] // (2 * each * nu)
    parts = grad.reshape(chips, 2, nu, each, d)
    first = idx_ref[3] == 0
    for j in range(nu):
        cols = slice(j * d, (j + 1) * d)
        keep[:, :, cols] = jnp.where(first, parts[:, 0, j], parts[:, 1, j]).astype(bf16)
        send[:, :, cols] = jnp.where(first, parts[:, 1, j], parts[:, 0, j]).astype(bf16)


def down_grad(idx, g, dyl, n):
    s, ff = g.shape
    d = dyl.shape[1]
    each, nu = d // n, ff // d
    chips = n // 2 // nu
    spec = pl.BlockSpec((chips, each, ff), lambda i: (i, 0, 0))
    return pl.pallas_call(
        functools.partial(down_kernel, each=each, nu=nu),
        grid=(nu,),
        in_specs=[smem(), pl.BlockSpec((s, d), lambda i: (0, i)), whole((s, d))],
        out_specs=[spec, spec],
        out_shape=[sds((n // 2, each, ff), bf16)] * 2,
        compiler_params=params(24),
        cost_estimate=cost(9),
    )(idx, g, dyl)


def up_kernel(idx_ref, c_ref, du_ref, keep, send, *, each):
    by_core(idx_ref, dot(c_ref[...], du_ref[...], TN), keep, send, each)


def up_grad(idx, c, du, n):
    s, d = c.shape
    ff = du.shape[1]
    each = d // n
    spec = pl.BlockSpec((n // 2, each, d), lambda j: (0, 0, j))
    return pl.pallas_call(
        functools.partial(up_kernel, each=each),
        grid=(ff // d,),
        in_specs=[smem(), whole((s, d)), pl.BlockSpec((s, d), lambda j: (0, j))],
        out_specs=[spec, spec],
        out_shape=[sds((n // 2, each, ff), bf16)] * 2,
        compiler_params=params(24),
        cost_estimate=cost(9),
    )(idx, c, du)


def attention_grads_kernel(idx_ref, a_ref, dqkv_ref, o_ref, drl_ref, *rest, each):
    keep_a, send_a, keep_b, send_b = rest[-4:]
    j = pl.program_id(0)

    @pl.when(j < 2)
    def _():
        by_core(idx_ref, dot(a_ref[...], dqkv_ref[0], TN), keep_a, send_a, each)

    @pl.when(j == 2)
    def _():
        by_core(idx_ref, dot(a_ref[...], dqkv_ref[0], TN), keep_b, send_b, each)

    @pl.when(j == 3)
    def _():
        by_core(idx_ref, dot(o_ref[...], drl_ref[...], TN), keep_b, send_b, each)


def attention_grads(idx, a, dqkv, o, drl, n, deps=()):
    s, d = a.shape
    each = d // n
    spec_a = pl.BlockSpec((n // 2, each, d), lambda j: (0, 0, jnp.minimum(j, 1)))
    spec_b = pl.BlockSpec((n // 2, each, d), lambda j: (0, 0, jnp.maximum(j - 2, 0)))
    return pl.pallas_call(
        functools.partial(attention_grads_kernel, each=each),
        grid=(4,),
        in_specs=[
            smem(),
            whole((s, d)),
            pl.BlockSpec((1, s, d), lambda j: (jnp.minimum(j, 2), 0, 0)),
            whole((s, d)),
            whole((s, d)),
        ]
       ,
        out_specs=[spec_a, spec_a, spec_b, spec_b],
        out_shape=[sds((n // 2, each, 2 * d), bf16)] * 4,
        compiler_params=params(40),
        cost_estimate=cost(40),
    )(tie(idx, *deps), a, dqkv, o, drl)


def first_kernel(x_ref, dr_ref, dq_ref, w_ref, g_ref, sbo, sg2, sb2, sbd, sbu, *rest):
    gi_ref, out = rest[-2:]
    i = pl.program_id(0)
    d = x_ref.shape[1]
    quarter = w_ref.shape[3]

    @pl.when(i == 0)
    def _():
        out[:, : 5 * d] = jnp.zeros((1, 5 * d), f32)
        for k, ref in enumerate((sbo, sg2, sb2, sbd)):
            out[:, (5 + k) * d : (6 + k) * d] = ref[...]
        out[:, 9 * d :] = sbu[...]

    normal, inverse = norm_stats(x_ref[...].astype(f32))
    da = jnp.zeros(normal.shape, f32)
    for k in range(4):
        w = w_ref[k].reshape(d, quarter)
        at = k * quarter
        while at < min((k + 1) * quarter, 3 * d):
            j = at // d
            end = min((k + 1) * quarter, (j + 1) * d)
            part = dq_ref[j, :, at - j * d : end - j * d]
            da = da + dot(part, w[:, at - k * quarter : end - k * quarter], NT)
            out[:, 2 * d + at : 2 * d + end] += jnp.sum(part.astype(f32), axis=0, keepdims=True)
            at = end
    q1 = da * g_ref[...]
    inner = (
        q1 - jnp.mean(q1, axis=1, keepdims=True) - normal * jnp.mean(q1 * normal, axis=1, keepdims=True)
    )
    gi_ref[...] = dr_ref[...] + inverse * inner
    out[:, :d] += jnp.sum(da * normal, axis=0, keepdims=True)
    out[:, d : 2 * d] += jnp.sum(da, axis=0, keepdims=True)


def first_backward(x, dr, dqkv, w, gain, sums, deps=(), rb=256):
    s, d = x.shape

    def row(w):
        return pl.BlockSpec((rb, w), lambda i: (i, 0))

    wide = 9 * d + sums[-1].shape[1]
    return pl.pallas_call(
        first_kernel,
        grid=(s // rb,),
        in_specs=[row(d), row(d), pl.BlockSpec((3, rb, d), lambda i: (0, i, 0)), whole(w.shape), whole((1, d))]
        + [whole(t.shape) for t in sums]
       ,
        out_specs=[row(d), pl.BlockSpec((1, wide), lambda i: (0, 0))],
        out_shape=[sds((s, d), f32), sds((1, wide), f32)],
        compiler_params=params(40),
        cost_estimate=cost(10),
    )(x, dr, dqkv, w, tie(gain, *deps), *sums)


def scatter_sum(buf, n, order):
    lin = lax.axis_index(AXES)
    bits = n.bit_length() - 1
    rest = buf.shape[1:]
    buf = buf.reshape((2,) * bits + rest)
    left = list(range(bits - 1, -1, -1))
    for step, b in enumerate(order):
        axis = left.index(b)
        left.pop(axis)
        bit = (lin >> b) & 1
        send = lax.dynamic_index_in_dim(buf, 1 - bit, axis, keepdims=False)
        keep = lax.dynamic_index_in_dim(buf, bit, axis, keepdims=False)
        got = lax.ppermute(send, AXES, [(i, i ^ (1 << b)) for i in range(n)])
        buf = keep.astype(f32) + got.astype(f32)
        if step < bits - 1:
            buf = buf.astype(send.dtype)
    return buf


def permute(x, mask, n=32):
    return lax.ppermute(x, AXES, [(i, i ^ mask) for i in range(n)])


CORE, XBIT, YBIT = 1, 8, 16


def join(block, got):
    return jnp.concatenate([block[None], got[None]])


def gather_cores(mine, theirs, core):
    got = permute(theirs, CORE)
    return jnp.where(core == 0, jnp.concatenate([mine, got]), jnp.concatenate([got, mine]))


def gather_first(block, cut):
    a, b = block[..., :cut], block[..., cut:]
    return a, permute(a, XBIT), b, permute(b, YBIT)


def gather_second(a, b):
    parts = (a, permute(a, YBIT), b, permute(b, XBIT))
    return [t.reshape((8,) + t.shape[-2:]) for t in parts]


def fold_kernel(idx_ref, *refs, plan, joined):
    ins, outs = refs[: 2 * len(plan)], refs[-2 if joined else -2 * len(plan) :]
    lane = 0
    for k, (dim, which) in enumerate(plan):
        kept, got = ins[2 * k], ins[2 * k + 1]
        lead, wide = kept.shape[:-2], kept.shape[-1]
        for side in range(2):
            out = outs[side if joined else 2 * k + side]
            at = idx_ref[which] if side == 0 else 1 - idx_ref[which]
            for t in itertools.product(*[range(m) for m in lead[:dim] + lead[dim + 1 :]]):
                source = t[:dim] + (at,) + t[dim:]
                value = (kept[source].astype(f32) + got[source].astype(f32)).astype(bf16)
                if joined:
                    out[t + (slice(None), slice(lane, lane + wide))] = value
                else:
                    out[t] = value
        lane += wide


def fold(idx, pairs, plan, us, deps=(), joined=False):
    args, in_specs, out_specs, out_shape, total = [], [], [], [], 0
    for (kept, got), (dim, _) in zip(pairs, plan):
        lead, (each, wide) = kept.shape[:-2], kept.shape[-2:]
        left = lead[:dim] + lead[dim + 1 :]
        total += wide
        args += [kept, got]
        in_specs += [pl.BlockSpec()] * 2
        out_specs += [pl.BlockSpec()] * 2
        out_shape += [sds(left + (each, wide), bf16)] * 2
    if joined:
        out_specs, out_shape = [pl.BlockSpec()] * 2, [sds(left + (each, total), bf16)] * 2
    return pl.pallas_call(
        functools.partial(fold_kernel, plan=plan, joined=joined),
        in_specs=[smem()] + in_specs,
        out_specs=out_specs,
        out_shape=out_shape,
        compiler_params=params(24),
        cost_estimate=cost(us),
    )(tie(idx, *deps), *args)


def last_kernel(kept, got, *refs, cuts):
    outs = refs[-len(cuts) :]
    total = kept[...].astype(f32) + got[...].astype(f32)
    each = total.shape[0]
    at = 0
    for out, (rows, wide) in zip(outs, cuts):
        for j in range(rows):
            out[j * each : (j + 1) * each, :] = total[:, at : at + wide]
            at += wide


def fold_last(kept, got, cuts, deps=()):
    each = kept.shape[0]
    return pl.pallas_call(
        functools.partial(last_kernel, cuts=cuts),
        in_specs=[pl.BlockSpec()] * 2,
        out_specs=[pl.BlockSpec()] * len(cuts),
        out_shape=[sds((rows * each, wide), f32) for rows, wide in cuts],
        compiler_params=params(24),
        cost_estimate=cost(1),
    )(tie(kept, *deps), got)


def body(
    n,
    dp,
    layer_input,
    lengths,
    ln1_gain,
    ln1_bias,
    w_qkv,
    b_qkv,
    w_out,
    b_out,
    ln2_gain,
    ln2_bias,
    w_up,
    b_up,
    w_down,
    b_down,
    cotangent,
):
    s, d = layer_input.shape[1:]
    x = layer_input.reshape(s, d)
    ct = cotangent.reshape(s, d)
    e, ff = w_qkv.shape[1], w_up.shape[1]
    each = d // n
    nu = ff // d
    fast = n == 32 and dp == 4
    lin = lax.axis_index(AXES)
    idx = jnp.stack([(lin >> 3) & 1, (lin >> 4) & 1, (lin >> 1) & 3, lin & 1, (lin >> 1) & 1, (lin >> 2) & 1]).astype(jnp.int32)
    vectors = (ln1_gain, ln1_bias, b_out, ln2_gain, ln2_bias, b_down, b_qkv, b_up)
    layout = vector_layout(each, d, e, ff)
    mine, theirs = prepare(w_qkv, vectors, layout)
    mine_rest, theirs_rest = prepare_rest(tie(w_out, mine), w_up, w_down)
    cut_q, cut_r = (e + 256) // 4, 128 * (-(-(d + 2 * ff) // 512))
    if fast:
        core = lin & 1
        q = gather_cores(mine, theirs, core)
        r = gather_cores(mine_rest, theirs_rest, core)
        q = join(q, permute(q, 4))
        q = tie(q, r)
        q = join(q, permute(q, 2))
        r = tie(r, q)
        a0, a1, b0, b1 = gather_first(q, cut_q)
        got_r = permute(r, 4)
        qa, qb = join(a0, a1), join(b0, b1)
        parts = gather_second(qa, qb)
        r = join(r, tie(got_r, qa, qb))
        parts[1], parts[3] = tie(parts[1], r), tie(parts[3], r)
        parts += [permute(t, CORE) for t in parts]
        ra, rb = r[..., :cut_r], r[..., cut_r:]
        ra, rb = join(ra, permute(ra, 2)), join(rb, permute(rb, 2))
        got_ra, got_rb = permute(ra, XBIT), permute(rb, YBIT)
        x_in = tie(x, ra, rb)
    else:
        def gathered(own, other):
            both = jnp.where((lin & 1) == 0, jnp.concatenate([own, other], 1), jnp.concatenate([other, own], 1))
            return lax.all_gather(both, AXES, axis=0, tiled=True)

        x_in = x
        parts = [gathered(mine, theirs)]
        rest = [gathered(mine_rest, theirs_rest).reshape(d // 48, 48, d + 2 * ff)]
    a, qkv, wq, g1, b1, bo, g2, b2, bd, bq, bu = qkv_call(idx, x_in, parts, n, layout, e)
    if fast:
        ra, rb = join(ra, tie(got_ra, qkv)), join(rb, tie(got_rb, qkv))
        ra, ga, rb, gb = gather_second(ra, rb)
        o, rz, *kept = attention_forward(lengths, qkv, 0, H // 2, deps=(ra, rb))
        other_ra, other_rb = permute(ra, CORE), permute(rb, CORE)
        ga, gb = tie(ga, o, other_ra, other_rb), tie(gb, o, other_ra, other_rb)
        rest = [ra, ga, rb, gb, other_ra, permute(ga, CORE), other_rb, permute(gb, CORE)]
    else:
        o, rz, *kept = attention_forward(lengths, qkv, 0, H // 2)
    (y, g, du, c, dyl, drl, dr, dol, sbd, sbu, sg2, sb2, sbo) = ffn_call(
        lengths, idx, x, o, ct, rest, bo, g2, b2, bu, bd, n, cut_r
    )
    sums = (sbo, sg2, sb2, sbd, sbu)
    if fast:
        core_x, core_y, deep_0, deep_1 = 0, 1, 4, 5

        def chips(t):
            return t.reshape((2, 2, 4) + t.shape[1:])

        def deep(t):
            return t.reshape((2, 2) + t.shape[1:])

        keep_d, send_d = down_grad(idx, g, dyl, n)
        got_d = permute(send_d, CORE)
        keep_u, send_u = up_grad(idx, c, du, n)
        got_u = permute(send_u, CORE)
        kd, sd = fold(idx, [(chips(keep_d), chips(got_d))], [(1, core_x)], 2.5, deps=(keep_u,))
        rd = permute(sd, XBIT)
        ku, su = fold(idx, [(chips(keep_u), chips(got_u))], [(0, core_y)], 2.5, deps=(kd,))
        ru = permute(su, YBIT)
        dqkv = attention_backward(lengths, qkv, o, rz, dol, kept, deps=(ku,))
        kd, sd, ku, su = fold(idx, [(kd, rd), (ku, ru)], [(0, core_y), (0, core_x)], 2.5, deps=(dqkv,))
        rd, ru = permute(sd, YBIT), permute(su, XBIT)
        ka, sa, kb, sb = attention_grads(idx, a, dqkv, o, drl, n, deps=(kd,))
        ga, gb = permute(sa, CORE), permute(sb, CORE)
        pairs = [(deep(kd), deep(rd)), (deep(ku), deep(ru))]
        kw, sw = fold(idx, pairs, [(1, deep_0)] * 2, 30, deps=(ka,), joined=True)
        rw = permute(sw, 2)
        pairs = [(chips(ka), chips(ga)), (chips(kb), chips(gb))]
        ka, sa, kb, sb = fold(idx, pairs, [(1, core_x), (0, core_y)], 2.5, deps=(kw,))
        ra, rb = permute(sa, XBIT), permute(sb, YBIT)
        grad_input, total = first_backward(x, dr, dqkv, wq, g1, sums, deps=(ka,))
        got = permute(total, CORE)
        kw, sw = fold(idx, [(kw, rw)], [(0, deep_1)], 1, deps=(total,))
        rw = permute(sw, 4)
        ka, sa, kb, sb = fold(idx, [(ka, ra), (kb, rb)], [(0, core_y), (0, core_x)], 1, deps=(kw,))
        ra, rb = permute(sa, YBIT), permute(sb, XBIT)
        total = total + tie(got, ka)
        got = [permute(total, mask) for mask in (XBIT, YBIT, XBIT | YBIT)]
        grad_down, grad_up = fold_last(kw, rw, [(nu, d), (1, ff)], deps=(ra, rb))
        got = lax.optimization_barrier((*got, grad_up))
        total = total + got[0] + got[1] + got[2]
        pairs = [(deep(ka), deep(ra)), (deep(kb), deep(rb))]
        kq, sq = fold(idx, pairs, [(1, deep_0)] * 2, 1, deps=(grad_up, total), joined=True)
        rq = permute(sq, 2)
        got = [permute(total, mask) for mask in (2, 4, 6)]
        kq, sq = fold(idx, [(kq, rq)], [(0, deep_1)], 1)
        rq = permute(sq, 4)
        got = lax.optimization_barrier((*got, kq))
        total = total + got[0] + got[1] + got[2]
        grad_qkv, grad_out = fold_last(kq, rq, [(1, e), (1, d)])
    else:
        order = list(range(n.bit_length() - 1))
        grad_down = scatter_sum(wgrad(g, dyl, d, d).reshape(n, ff // n, d), n, order)
        grad_up = scatter_sum(wgrad(c, du, d, d).reshape(n, each, ff), n, order)
        grad_out = scatter_sum(wgrad(o, drl, d, d).reshape(n, each, d), n, order)
        dqkv = attention_backward(lengths, qkv, o, rz, dol, kept)
        grad_qkv = scatter_sum(wgrad(a, dqkv, d, d).reshape(n, each, e), n, order)
        grad_input, total = first_backward(x, dr, dqkv, wq, g1, sums)
        total = lax.psum(total, AXES)
    shares, at = [], 0
    for size in (each, each, 3 * each, each, each, each, each, nu * each):
        shares.append(lax.dynamic_slice_in_dim(total[0], at + lin * size, size))
        at += n * size
    gs1, gb1, gbq, gbo, gs2, gb2, gbd, gbu = shares
    return (
        y.reshape(layer_input.shape),
        grad_input.reshape(layer_input.shape),
        gs1,
        gb1,
        grad_qkv,
        gbq,
        grad_out,
        gbo,
        gs2,
        gb2,
        grad_up,
        gbu,
        grad_down,
        gbd,
    )


def solution(mesh):
    split = P(AXES)
    wide = P(AXES, None)
    cube = P(AXES, None, None)
    in_specs = (
        cube, split, split, split, wide, split, wide, split, split, split, wide, split, wide, split, cube,
    )
    out_specs = (
        cube, cube, split, split, wide, split, wide, split, split, split, wide, split, wide, split,
    )
    n = mesh.shape["dp"] * mesh.shape["fsdp"]
    return jax.shard_map(
        functools.partial(body, n, mesh.shape["dp"]),
        mesh=mesh,
        in_specs=in_specs,
        out_specs=out_specs,
        check_vma=False,
    )
```
